512 devices in a mesh: clip: 16 (over x_hi, y), tm: 32 (over z, x_lo, core).
Axes of the slice: x: 4 (x_hi: 2, x_lo: 2; x = x_hi * 2 + x_lo), y: 8, z: 8, core: 2. Of those that a mesh axis runs over, the one named last changes fastest.
Arguments:
- video: bfloat16 [16, 64, 288, 384], P('clip', 'tm'), may hold values from -6 to 6
- conv_w: bfloat16 [3, 384, 384], P(None, 'tm'), may hold values from -0.1875 to 0.1875
- qkv_w: bfloat16 [384, 1152], P('tm'), as said below
- out_w: bfloat16 [384, 384], P('tm'), may hold values from -0.3125 to 0.3125
- gain: bfloat16 [384], P('tm'), may hold values from 0.5 to 3.5
- cotangent: bfloat16 [16, 64, 288, 384], P('clip', 'tm'), may hold values from -6 to 6
Outputs:
- grad_video: bfloat16 [16, 64, 288, 384], P('clip', 'tm')
- grad_conv: float32 [3, 384, 384], P(None, 'tm')
- grad_qkv: float32 [384, 1152], P('tm')
- grad_out: float32 [384, 384], P('tm')
- grad_gain: float32 [384], P('tm')
The draws below stay inside these ranges and needn't reach their ends.
Inputs may be any that keep to these rules, and one draw needn't show every extreme that they name: `qkv_w`: projection weights with entries of order 384^-0.5.
All inputs are finite; a program needn't handle non-finite values.
Results may differ from the reference program's by a relative error of at most 0.035.
Values may be sent and summed in bfloat16 or wider, within the bound.
A program may use at most 64 MiB of HBM per device.

```python
import math
import jax
import jax.numpy as jnp
from jax import lax

C = 384
HW = 288
FRAMES = 64
CLIPS = 16


def draw_gain(key, part):
    key = jax.random.fold_in(key, 11)
    logs = jax.random.uniform(key, (C,), jnp.float32, math.log(0.5), math.log(2.0))
    return jnp.exp(logs).astype(jnp.bfloat16)


def draw_qkv_w(key, part):
    key = jax.random.fold_in(key, 12)
    base = jax.random.normal(key, (C, 3 * C), jnp.float32) / math.sqrt(C)
    return base.astype(jnp.bfloat16)


def block_scale(rng, dims, shards, smallest, high):
    factor_of = 1.0
    for dim, parts in shards:
        steps = jax.random.uniform(jax.random.fold_in(jax.random.fold_in(rng, 6), dim), (parts,), jnp.float32, smallest / len(shards), high / len(shards))
        factor_of = factor_of * jnp.repeat(jnp.exp(steps), dims[dim] // parts).reshape((-1,) + (1,) * (len(dims) - 1 - dim))
    return factor_of


def noise(rng, shape, deviation, most, cuts=(), kind=jnp.bfloat16):
    result = jax.random.normal(rng, shape, jnp.float32) * deviation
    if len(cuts) > 0:
        result = block_scale(rng, shape, cuts, -0.22, 0.18) * result
    return jnp.clip(result, min=-most, max=most).astype(kind)


def setup_inputs(seed: int = 0) -> dict:
    key_list = jax.random.split(jax.random.key(seed), 7)
    return {
        "video": noise(key_list[0], (CLIPS, FRAMES, HW, C), 1.0, 6.0, ((0, 16), (1, 32))),
        "conv_w": noise(key_list[1], (3, C, C), (3 * C) ** -0.5, 0.1875, ((1, 32),)),
        "qkv_w": draw_qkv_w(jax.random.fold_in(key_list[6], 71), 0),
        "out_w": noise(key_list[3], (C, C), C ** -0.5, 0.3125, ((0, 32),)),
        "gain": draw_gain(jax.random.fold_in(key_list[6], 71), 0),
        "cotangent": noise(key_list[5], (CLIPS, FRAMES, HW, C), 1.0, 6.0, ((0, 16), (1, 32))),
    }


epsilon = 1e-06

def project(values, matrix):
    flat = values.reshape(-1, values.shape[-1])
    product = jnp.dot(flat, matrix, preferred_element_type=jnp.float32)
    return product.reshape(values.shape[:-1] + (matrix.shape[-1],))

def shifted(frames, steps):
    pad = jnp.zeros((steps,) + frames.shape[1:], frames.dtype)
    return jnp.concatenate([pad, frames[:frames.shape[0] - steps]], 0)

def advanced(frames, steps):
    pad = jnp.zeros((steps,) + frames.shape[1:], frames.dtype)
    return jnp.concatenate([frames[steps:], pad], 0)

def normalize(hidden, gain):
    wide = hidden.astype(jnp.float32)
    inverse = lax.rsqrt(lax.optimization_barrier(jnp.mean(wide * wide, axis=-1, keepdims=True)) + epsilon)
    return ((wide * inverse * gain.astype(jnp.float32)).astype(jnp.bfloat16), inverse)

def normalize_back(hidden, inverse, gain, grad_norm, cotangent):
    wide = hidden.astype(jnp.float32)
    incoming = grad_norm.astype(jnp.float32)
    scaled = incoming * gain.astype(jnp.float32)
    inner = lax.optimization_barrier(jnp.mean(scaled * wide, axis=-1, keepdims=True))
    grad_hidden = cotangent.astype(jnp.float32) + inverse * scaled - wide * inverse ** 3 * inner
    return (grad_hidden.astype(jnp.bfloat16), incoming * wide * inverse)

def attend(query, keys, values):
    width = query.shape[-1]
    factor = 1.0 / math.sqrt(width)
    scores = jnp.einsum('tpc,upc->ptu', query.astype(jnp.float32), keys.astype(jnp.float32)) * factor
    length = query.shape[0]
    causal = jnp.arange(length)[:, None] >= jnp.arange(length)[None, :]
    scores = jnp.where(causal[None], scores, -1e+30)
    top = lax.optimization_barrier(jnp.max(scores, axis=-1, keepdims=True))
    raised = jnp.exp(scores - top)
    probs = raised / lax.optimization_barrier(jnp.sum(raised, axis=-1, keepdims=True))
    rounded = probs.astype(jnp.bfloat16)
    attended = jnp.einsum('ptu,upc->tpc', rounded.astype(jnp.float32), values.astype(jnp.float32))
    return (attended.astype(jnp.bfloat16), probs, rounded)

def attend_back(query, keys, values, probs, rounded, grad_att):
    width = query.shape[-1]
    factor = 1.0 / math.sqrt(width)
    incoming = grad_att.astype(jnp.float32)
    dprob = jnp.einsum('tpc,upc->ptu', incoming, values.astype(jnp.float32))
    dvalue = jnp.einsum('ptu,tpc->upc', rounded.astype(jnp.float32), incoming)
    dscore = probs * (dprob - lax.optimization_barrier(jnp.sum(dprob * probs, axis=-1, keepdims=True)))
    dquery = jnp.einsum('ptu,upc->tpc', dscore, keys.astype(jnp.float32), precision=lax.Precision.HIGHEST) * factor
    dkey = jnp.einsum('ptu,tpc->upc', dscore, query.astype(jnp.float32), precision=lax.Precision.HIGHEST) * factor
    return jnp.concatenate([dquery.astype(jnp.bfloat16), dkey.astype(jnp.bfloat16), dvalue.astype(jnp.bfloat16)], -1)

def plain_sum(left, right):
    flat_left = left.reshape(-1, left.shape[-1]).astype(jnp.float32)
    flat_right = right.reshape(-1, right.shape[-1]).astype(jnp.float32)
    return jnp.einsum('rc,rd->cd', flat_left, flat_right, precision=lax.Precision.HIGHEST)

def reference(video, conv_w, qkv_w, out_w, gain, cotangent):

    def one_clip(carry, pair):
        frames, grad_output = pair
        first = shifted(frames, 1)
        second = shifted(frames, 2)
        mixed = project(frames, conv_w[0]) + project(first, conv_w[1]) + project(second, conv_w[2])
        hidden = (frames.astype(jnp.float32) + mixed).astype(jnp.bfloat16)
        normed, inverse = normalize(hidden, gain)
        packed = project(normed, qkv_w).astype(jnp.bfloat16)
        query = packed[..., :C]
        keys = packed[..., C:2 * C]
        values = packed[..., 2 * C:]
        attended, probs, rounded = attend(query, keys, values)
        grad_att = project(grad_output, out_w.T).astype(jnp.bfloat16)
        grad_packed = attend_back(query, keys, values, probs, rounded, grad_att)
        grad_norm = project(grad_packed, qkv_w.T).astype(jnp.bfloat16)
        grad_hidden, gain_terms = normalize_back(hidden, inverse, gain, grad_norm, grad_output)
        grad_frames = grad_hidden.astype(jnp.float32) + project(grad_hidden, conv_w[0].T)
        grad_frames = grad_frames + project(advanced(grad_hidden, 1), conv_w[1].T)
        grad_frames = grad_frames + project(advanced(grad_hidden, 2), conv_w[2].T)
        conv_sum = jnp.stack([plain_sum(frames, grad_hidden), plain_sum(first, grad_hidden), plain_sum(second, grad_hidden)], 0)
        gain_sum = lax.optimization_barrier(jnp.sum(gain_terms.reshape(-1, gain_terms.shape[-1]), axis=0))
        new_carry = (carry[0] + conv_sum, carry[1] + plain_sum(normed, grad_packed), carry[2] + plain_sum(attended, grad_output), carry[3] + gain_sum)
        return (new_carry, grad_frames.astype(jnp.bfloat16))
    start = (jnp.zeros((3, C, C), jnp.float32), jnp.zeros((C, 3 * C), jnp.float32), jnp.zeros((C, C), jnp.float32), jnp.zeros((C,), jnp.float32))
    totals, grad_video = lax.scan(one_clip, start, (video, cotangent))
    factor = 1.0 / math.sqrt(CLIPS * FRAMES * HW)
    return (grad_video, totals[0] * factor, totals[1] * factor, totals[2] * factor, totals[3] * factor)
```

```python
import functools
import math

import jax
import jax.numpy as jnp
from jax import lax
from jax.experimental import pallas as pl
from jax.experimental.pallas import tpu as pltpu
from jax.sharding import PartitionSpec as P

epsilon = 1e-06
F32 = jnp.float32
BF16 = jnp.bfloat16

C = 384
FRAMES = 64
SPOTS = 9
ROWS = SPOTS * FRAMES
PARTS = ((0, 5), (5, 4))
BLOCKS = (((0, 192), (192, 128)), ((0, 128), (128, 128)))
MATS = 7
WIDE = MATS * C


def mm(a, b):
    return lax.dot_general(a, b, (((1,), (0,)), ((), ())), preferred_element_type=F32)


def mm_nt(a, b):
    return lax.dot_general(a, b, (((1,), (1,)), ((), ())), preferred_element_type=F32)


def mm_tn(a, b):
    return lax.dot_general(a, b, (((0,), (0,)), ((), ())), preferred_element_type=F32)


def iotas(rows, columns):
    shape = (rows, columns)
    return lax.broadcasted_iota(jnp.int32, shape, 0), lax.broadcasted_iota(jnp.int32, shape, 1)


def delay_matrix(size, steps):
    row, col = iotas(size, size)
    return jnp.where((row - col == steps) & ((row & (FRAMES - 1)) >= steps), 1.0, 0.0).astype(BF16)


def forward(blocks, w, gain, x, s1, s2, hidden, inverse, normed, packed):
    for steps, ref in ((1, s1), (2, s2)):
        for first, size in blocks:
            rows = pl.ds(first, size)
            ref[rows, :] = mm(delay_matrix(size, steps), x[rows, :]).astype(BF16)
    mixed = mm(x[...], w[:, 0:C]) + mm(s1[...], w[:, C : 2 * C]) + mm(s2[...], w[:, 2 * C : 3 * C])
    hidden[...] = (x[...].astype(F32) + mixed).astype(BF16)
    wide = hidden[...].astype(F32)
    inverse[...] = lax.rsqrt(jnp.mean(wide * wide, axis=-1, keepdims=True) + epsilon)
    normed[...] = (wide * inverse[...] * gain[...]).astype(BF16)
    packed[...] = mm(normed[...], w[:, 3 * C : 6 * C]).astype(BF16)


def seen(size):
    row, col = iotas(size, size)
    return ((row >> 6) == (col >> 6)) & (col <= row)


def attention(blocks, w, cot, packed, attended, grad_att, grad_packed):
    factor = 1.0 / math.sqrt(C)
    grad_att[...] = mm_nt(cot[...], w[:, 6 * C : 7 * C]).astype(BF16)
    for first, size in blocks:
        part = pl.ds(first, size)
        query, keys, values = (packed[part, i * C : (i + 1) * C] for i in range(3))
        scores = jnp.where(seen(size), mm_nt(query, keys) * factor, -1e30)
        raised = jnp.exp(scores - jnp.max(scores, axis=-1, keepdims=True))
        probs = raised / jnp.sum(raised, axis=-1, keepdims=True)
        rounded = probs.astype(BF16)
        attended[part, :] = mm(rounded, values).astype(BF16)
        incoming = grad_att[part, :]
        dprob = mm_nt(incoming, values)
        dscore = probs * (dprob - jnp.sum(dprob * probs, axis=-1, keepdims=True))
        dscore = (dscore * factor).astype(BF16)
        grad_packed[part, 0:C] = mm(dscore, keys).astype(BF16)
        grad_packed[part, C : 2 * C] = mm_tn(dscore, query).astype(BF16)
        grad_packed[part, 2 * C : 3 * C] = mm_tn(rounded, incoming).astype(BF16)


def normalize_back(w, gain, cot, hidden, inverse, grad_packed, grad_hidden):
    grad_norm = mm_nt(grad_packed[...], w[:, 3 * C : 6 * C]).astype(BF16).astype(F32)
    wide = hidden[...].astype(F32)
    inv = inverse[...]
    scaled = grad_norm * gain[...]
    inner = jnp.mean(scaled * wide, axis=-1, keepdims=True)
    back = cot[...].astype(F32) + inv * scaled - wide * (inv * inv * inv * inner)
    grad_hidden[...] = back.astype(BF16)
    return jnp.sum(grad_norm * wide * inv, axis=0, keepdims=True)


def conv_back(blocks, w, grad_hidden, a1, a2, gv):
    for steps, ref in ((1, a1), (2, a2)):
        for first, size in blocks:
            rows = pl.ds(first, size)
            ref[rows, :] = mm_tn(delay_matrix(size, steps), grad_hidden[rows, :]).astype(BF16)
    grad = grad_hidden[...].astype(F32) + mm_nt(grad_hidden[...], w[:, 0:C])
    grad = grad + mm_nt(a1[...], w[:, C : 2 * C]) + mm_nt(a2[...], w[:, 2 * C : 3 * C])
    gv[...] = grad.astype(BF16)


WAYS = 32
PIECE = 112
CUTS = ((0, 64), (64, 48))
BACK = 64
SHARE = 12
QUAD = 4 * SHARE
HALF = C // 2
MESH = pl.DeviceIdType.MESH
FAR_FIRST = (4, 3, 5, 2, 6, 1, 7)


def ninth(n):
    return (n * 57) >> 9


def fifth(n):
    return (n * 205) >> 10


def twelfth(n):
    return (n * 1366) >> 14


def picks(target, rows, columns):
    row, col = iotas(rows, columns)
    return jnp.where(col == target(row), 1.0, 0.0).astype(BF16)


class Place:
    def __init__(self):
        self.clip, self.tm = lax.axis_index("clip"), lax.axis_index("tm")
        self.y, self.z = lax.rem(self.clip, 8), lax.div(self.tm, 4)
        self.low = lax.rem(lax.div(self.tm, 2), 2)
        self.x = lax.div(self.clip, 8) * 2 + self.low
        self.core = lax.rem(self.tm, 2)
        self.rail = self.low * 2 + self.core

    def at(self, dx=0, dy=0, dz=0, other=False):
        x, y, z = lax.rem(self.x + dx, 4), lax.rem(self.y + dy, 8), lax.rem(self.z + dz, 8)
        core = 1 - self.core if other else self.core
        return (lax.div(x, 2) * 8 + y, z * 4 + lax.rem(x, 2) * 2 + core)

    def peer(self, k):
        return (self.clip, lax.rem(self.tm + k, WAYS))


def greet(me, outer):
    barrier = pltpu.get_barrier_semaphore()

    def tell(device):
        pl.semaphore_signal(barrier, inc=1, device_id=device, device_id_type=MESH)

    def step(k, carry):
        tell(me.peer(k))
        return carry

    lax.fori_loop(1, WAYS, step, 0)
    for k in range(1, 8):
        tell(me.at(dy=k))
    for device in outer:
        tell(device)
    return lambda: pl.semaphore_wait(barrier, WAYS - 1 + 7 + len(outer))


def remote(src, dst, sems, index, device):
    return pltpu.make_async_remote_copy(
        src_ref=src, dst_ref=dst, send_sem=sems[0].at[index], recv_sem=sems[1].at[index],
        device_id=device, device_id_type=MESH,
    )


def settle(ref, sem):
    pltpu.make_async_copy(ref, ref, sem).wait()


def each_peer(act, first=0, last=WAYS - 1):
    def step(i, carry):
        act(lax.rem(i + 12, WAYS - 1) + 1)
        return carry

    lax.fori_loop(first, last, step, 0)


class Exchange:
    def __init__(self, me, src, dst, cuts, sems, hops, hop_sems):
        self.__dict__.update(locals())

    def send(self, part, k):
        me, rows = self.me, pl.ds(*self.cuts[part])
        device = me.peer(k)
        target = device[1]
        opposite = lax.rem(me.z + 4, 8) == lax.div(target, 4)
        over = opposite & (lax.rem(target, 2) != me.core)
        piece = self.src.at[target, rows]

        @pl.when(over)
        def _():
            slot = self.hops.at[part, lax.rem(lax.div(target, 2), 2), pl.ds(0, self.cuts[part][1])]
            pltpu.make_async_remote_copy(
                src_ref=piece, dst_ref=slot, send_sem=self.sems[0].at[part],
                recv_sem=self.hop_sems[1].at[part], device_id=me.at(dz=6), device_id_type=MESH,
            ).start()

        @pl.when(jnp.logical_not(over))
        def _():
            remote(piece, self.dst.at[me.tm, rows], self.sems, part, device).start()

    def forward(self, part):
        me, size = self.me, self.cuts[part][1]
        self.settle_hops(part, self.hop_sems[1])
        source, target = me.at(dz=2)[1], me.at(dz=6, other=True)
        for low in range(2):
            device = (target[0], lax.div(target[1], 4) * 4 + low * 2 + 1 - me.core)
            pltpu.make_async_remote_copy(
                src_ref=self.hops.at[part, low, pl.ds(0, size)],
                dst_ref=self.dst.at[source, pl.ds(*self.cuts[part])],
                send_sem=self.hop_sems[0].at[part], recv_sem=self.sems[1].at[part],
                device_id=device, device_id_type=MESH,
            ).start()

    def settle_hops(self, part, sems):
        settle(self.hops.at[part, :, pl.ds(0, self.cuts[part][1])], sems.at[part])

    def arrive(self, part):
        settle(self.dst.at[pl.ds(0, WAYS - 1), pl.ds(*self.cuts[part])], self.sems[1].at[part])

    def drain(self):
        for part in range(2):
            settle(self.src.at[pl.ds(0, WAYS - 1), pl.ds(*self.cuts[part])], self.sems[0].at[part])
            self.settle_hops(part, self.hop_sems[0])


def pack_in(d, video, cot, out):
    base = lax.min(lax.div(d * SPOTS, 16) * 16, 256)
    base = pl.multiple_of(base, 16)
    pieces = [
        ref[0, f, pl.ds(base, 32), c * 128 : (c + 1) * 128]
        for ref in (video, cot) for c in range(3) for f in range(2)
    ]
    shift = d * SPOTS - base

    def column(r):
        block = jnp.where(r < 64, fifth(r), (r - 64) >> 2)
        spot = jnp.where(r < 64, r - fifth(r) * 5, 5 + (r & 3))
        return block * 32 + spot + shift

    pick = picks(column, PIECE, 384)
    out[d] = mm(pick, jnp.concatenate(pieces, 0)).astype(BF16)


def pack_weights(tm, conv, qkv, out_w, gain, shard):
    row, col = iotas(SHARE, C)
    own = col == tm * SHARE + row
    line = mm(gain[...], jnp.where(own, 1.0, 0.0).astype(BF16))
    diagonal = jnp.where(own, line, 0.0).astype(BF16)
    mats = [conv[0], conv[1], conv[2], qkv[:, 0:C], qkv[:, C : 2 * C], qkv[:, 2 * C : 3 * C], out_w[...], diagonal]
    for h in range(2):
        total = 0.0
        for j in range(4):
            total = total + mm(picks(lambda r: r - j * SHARE, QUAD, SHARE), mats[4 * h + j])
        shard[h] = total.astype(BF16)


def unpack_in(part, landed, x, cot):
    (start, rows), spots = CUTS[part], PARTS[part][1]
    for a, ref in ((0, x), (1, cot)):
        for c in range(3):
            first = (a * 3 + c) * 2 * spots
            base = min(first // 16 * 16, rows - 32)

            def column(r):
                return ((r & 15) >> 1) * 32 + (r & 1) * spots + (r >> 4) + (first - base)

            pick = picks(column, spots * 16, 256)
            for g in range(4):
                source = landed[8 * g : 8 * g + 8, start + base : start + base + 32, :]
                got = mm(pick, source.reshape(256, 128)).astype(BF16)
                for p in range(spots):
                    row = p * FRAMES + 16 * g
                    ref[row : row + 16, c * 128 : (c + 1) * 128] = got[16 * p : 16 * p + 16]


def unpack_weights(weights, w, gain):
    for m in range(MATS + 1):
        h, j = m // 4, m % 4
        base, size = ((0, 16), (0, 32), (16, 32), (32, 16))[j]

        def column(r):
            block = twelfth(r)
            return ((block & 3) * 8 + (block >> 2)) * size + (r - block * SHARE) + j * SHARE - base

        source = weights[h, :, :, base : base + size, :].reshape(WAYS * size, C)
        got = mm(picks(column, C, WAYS * size), source)
        if m < MATS:
            w[:, m * C : (m + 1) * C] = got.astype(BF16)
        else:
            gain[...] = jnp.sum(got, axis=0, keepdims=True)


def pack_out(part, gv, out):
    spots = PARTS[part][1]

    def column(r):
        inner = r & 31
        block = fifth(inner) if spots == 5 else inner >> 2
        spot = inner - block * spots
        return (block >> 1) * (16 * spots) + spot * 16 + (r >> 5) * 2 + (block & 1)

    pick = picks(column, 256, 48 * spots)
    for g in range(4):
        pieces = [
            gv[p * FRAMES + 16 * g : p * FRAMES + 16 * g + 16, c * 128 : (c + 1) * 128]
            for c in range(3) for p in range(spots)
        ]
        got = mm(pick, jnp.concatenate(pieces, 0)).astype(BF16)
        out[8 * g : 8 * g + 8, 32 * part : 32 * part + 32, :] = got.reshape(8, 32, 128)


def unpack_out(landed, grad_video):
    for f in range(2):
        for c in range(3):

            def column(r):
                spot = r - ninth(r) * SPOTS
                inner = jnp.where(spot < 5, c * 10 + f * 5 + spot, 32 + c * 8 + f * 4 + spot - 5)
                return ninth(r) * BACK + inner

            pick = picks(column, 144, 16 * BACK)
            for h in range(2):
                source = landed[16 * h : 16 * h + 16].reshape(16 * BACK, 128)
                got = mm(pick, source).astype(BF16)
                grad_video[0, f, 144 * h : 144 * h + 144, c * 128 : (c + 1) * 128] = got


def gather_weights(me, shard, weights, z_sems, y_sems, x_sems, c_sems):
    half = lax.rem(me.y, 2)
    begun = []

    def go(copy):
        copy.start()
        begun.append(copy)
        return copy

    def block(dz, *rows):
        return weights.at[half, me.rail, lax.rem(me.z + dz, 8), *rows]

    def over_z():
        for k in (2, 6, 1, 7):
            go(remote(shard.at[half], block(0), z_sems, k, me.at(dz=k)))
        weights[half, me.rail, me.z] = shard[half]

    def onward():
        for copy in begun[:2]:
            copy.wait_recv()
        top, low = pl.ds(0, 32), pl.ds(32, 16)
        go(remote(block(6, top), block(6, top), z_sems, 4, me.at(dz=2)))
        go(remote(block(2, low), block(2, low), z_sems, 0, me.at(dz=6)))
        go(remote(block(6), block(6), z_sems, 3, me.at(dz=1)))
        go(remote(block(2), block(2), z_sems, 5, me.at(dz=7)))

    def rest(between):
        for copy in begun[2:]:
            copy.wait_recv()
        beyond = (1 - me.low) * 2 + me.core
        part = lambda h, rail, i: weights.at[h, rail, pl.ds(4 * i, 4)]
        ys, xs, cs = [], [], []
        for i, step in ((0, 1), (1, 7)):
            mine = part(half, me.rail, i)
            ys.append(go(remote(mine, mine, y_sems, i, me.at(dy=step))))
        for i, step in ((0, 1), (1, 3)):
            mine = part(half, me.rail, i)
            xs.append(go(remote(mine, mine, x_sems, i, me.at(dx=step))))
            cs.append(go(remote(mine, mine, c_sems, i, me.at(other=True))))
        between()
        for i, step in ((0, 1), (1, 3)):
            ys[i].wait_recv()
            mine = part(1 - half, me.rail, i)
            xs.append(go(remote(mine, mine, x_sems, 2 + i, me.at(dx=step))))
            cs.append(go(remote(mine, mine, c_sems, 2 + i, me.at(other=True))))
        for n in range(4):
            xs[n].wait_recv()
            mine = part(half if n < 2 else 1 - half, beyond, n % 2)
            cs.append(go(remote(mine, mine, c_sems, 4 + n, me.at(other=True))))
        for copy in cs:
            copy.wait_recv()

    def drain():
        for copy in begun:
            copy.wait_send()

    return over_z, onward, rest, drain


class Sums:
    def __init__(self, me, sums, core_in, held, mid, x_in, z_in, y_in, y_out, totals, sems):
        self.__dict__.update(locals())
        self.round = lax.rem(me.x + me.core, 2)
        self.mine = lax.div(me.x, 2)

    def to_core(self, r, i):
        slot = lax.rem(self.me.core + 1 + r, 2) + 2 * i
        return remote(
            self.sums.at[r, slot], self.core_in.at[r, i], self.sems["c"], 2 * r + i,
            self.me.at(other=True),
        )

    def to_mid(self, r, i):
        part = self.held.at[r, 1 - self.mine, pl.ds(i * HALF, HALF)]
        return remote(part, self.mid.at[i], self.sems["m"], 2 * r + i, self.me.at(dx=3 if i else 1))

    def to_owner(self, r, i):
        step = 3 if i else 1
        which = lax.div(lax.rem(self.me.x + step, 4), 2)
        copy = remote(
            self.held.at[r, which], self.x_in.at[i], self.sems["x"], 2 * r + i, self.me.at(dx=step)
        )
        return which, copy

    def over_z(self, k):
        first = pl.multiple_of(lax.rem(self.me.z + k, 8) * QUAD, QUAD)
        part = self.held.at[self.round, self.mine, pl.ds(first, QUAD)]
        return remote(part, self.z_in.at[k], self.sems["z"], 0, self.me.at(dz=k))

    def over_y(self, k):
        mine = self.y_in.at[self.me.y]
        return remote(mine, mine, self.sems["y"], 0, self.me.at(dy=k))

    def over_row(self, k):
        dx, other = ((2, False), (2, True), (1, False), (3, False), (1, True), (3, True), (0, True))[k]
        own = self.round * 4 + self.me.x
        return remote(
            self.y_out, self.totals.at[own], self.sems["f"], 0, self.me.at(dx=dx, other=other)
        )

    def when_owner(self, r, act):
        pl.when(self.round == r)(act)

    def core_send(self, r):
        for i in range(2):
            self.to_core(r, i).start()

    def core_add(self, r):
        for i in range(2):
            self.to_core(r, i).wait_recv()
            slot = lax.rem(self.me.core + r, 2) + 2 * i
            both = self.sums[r, slot].astype(F32) + self.core_in[r, i].astype(F32)
            self.held[r, i] = both.astype(BF16)

        def act():
            for i in range(2):
                self.to_mid(r, i).start()

        self.when_owner(r, act)

    def relay(self, r):
        def act():
            for i in range(2):
                self.to_mid(r, i).wait_recv()
                which, copy = self.to_owner(r, i)
                rows = pl.ds(i * HALF, HALF)
                both = self.held[r, which, rows, :].astype(F32) + self.mid[i].astype(F32)
                self.held[r, which, rows, :] = both.astype(BF16)
                copy.start()

        self.when_owner(1 - r, act)

    def own_x(self, r):
        def act():
            total = self.held[r, self.mine].astype(F32)
            for i in range(2):
                self.to_owner(r, i)[1].wait_recv()
                total = total + self.x_in[i].astype(F32)
            self.held[r, self.mine] = total.astype(BF16)
            for k in FAR_FIRST:
                self.over_z(k).start()

        self.when_owner(r, act)

    def own_z(self):
        here = pl.ds(pl.multiple_of(self.me.z * QUAD, QUAD), QUAD)
        total = self.held[self.round, self.mine, here, :].astype(F32)
        settle(self.z_in.at[pl.ds(1, 7)], self.sems["z"][1].at[0])
        for k in range(1, 8):
            total = total + self.z_in[k].astype(F32)
        self.y_in[self.me.y] = total.astype(BF16)
        for k in FAR_FIRST:
            self.over_y(k).start()

    def own_y(self):
        settle(self.y_in.at[pl.ds(1, 7)], self.sems["y"][1].at[0])
        total = self.y_in[0].astype(F32)
        for k in range(1, 8):
            total = total + self.y_in[k].astype(F32)
        self.y_out[...] = total.astype(BF16)
        for k in range(7):
            self.over_row(k).start()
        self.totals[self.round * 4 + self.me.x] = self.y_out[...]

    def drain(self):
        for sem in (*self.sems["f"], self.sems["z"][0], self.sems["y"][0]):
            settle(self.z_in.at[pl.ds(1, 7)], sem.at[0])
        for r in range(2):
            for i in range(2):
                self.to_core(r, i).wait_send()

            def owner(r=r):
                for i in range(2):
                    self.to_mid(r, i).wait_send()

            def other(r=r):
                for i in range(2):
                    self.to_owner(r, i)[1].wait_send()

            self.when_owner(r, owner)
            self.when_owner(1 - r, other)


def main_kernel(
    video_in, cot_in, conv_in, qkv_in, out_in, gain_in, grad_video, totals,
    video, cotangent, conv, qkv, out_w, parcels, shard, landed, weights,
    w, gain, parcels_out, landed_out, hops_in, hops_out, acc, gain_acc,
    x, cot, s1, s2, hidden, inverse, normed, packed, attended, grad_att, grad_packed,
    grad_hidden, a1, a2, gv,
    sums, core_in, held, mid, x_in, z_in, y_in, y_out,
    l_s, i_s, i_r, o_s, o_r, h_s, h_r, g_s, g_r, wz_s, wz_r, wy_s, wy_r, wx_s, wx_r, wc_s, wc_r,
    sc_s, sc_r, sm_s, sm_r, sx_s, sx_r, sz_s, sz_r, sy_s, sy_r, sf_s, sf_r,
):
    me = Place()
    pairs = (
        (conv_in, conv), (qkv_in, qkv), (out_in, out_w), (video_in, video), (cot_in, cotangent)
    )
    reads = [pltpu.make_async_copy(src, dst, l_s.at[n]) for n, (src, dst) in enumerate(pairs)]
    for copy in reads:
        copy.start()
    outer = jnp.where(me.low == 0, 3, 1)
    met = greet(me, [me.at(dx=dx, other=o) for dx in (2, outer) for o in (False, True)])
    for copy in reads[:3]:
        copy.wait()
    pack_weights(me.tm, conv, qkv, out_w, gain_in, shard)
    for copy in reads[3:]:
        copy.wait()
    met()

    over_z, onward, rest, drain = gather_weights(
        me, shard, weights, (wz_s, wz_r), (wy_s, wy_r), (wx_s, wx_r), (wc_s, wc_r)
    )
    over_z()

    coming = Exchange(me, parcels, landed, CUTS, (i_s, i_r), hops_in, (h_s, h_r))
    going = Exchange(
        me, parcels_out, landed_out, ((0, 32), (32, 32)), (o_s, o_r), hops_out, (g_s, g_r)
    )

    def pack_and_send(k):
        pack_in(me.peer(k)[1], video, cotangent, parcels)
        coming.send(0, k)

    each_peer(pack_and_send, 0, 10)
    onward()
    each_peer(pack_and_send, 10)
    coming.forward(0)
    pack_in(me.tm, video, cotangent, landed)
    rest(lambda: each_peer(lambda k: coming.send(1, k)))
    coming.forward(1)
    unpack_weights(weights, w, gain)

    total = Sums(
        me, sums, core_in, held, mid, x_in, z_in, y_in, y_out, totals,
        dict(
            c=(sc_s, sc_r), m=(sm_s, sm_r), x=(sx_s, sx_r), z=(sz_s, sz_r), y=(sy_s, sy_r),
            f=(sf_s, sf_r),
        ),
    )
    tall = (
        x, cot, s1, s2, hidden, inverse, normed, packed, attended, grad_att, grad_packed,
        grad_hidden, a1, a2, gv,
    )
    for part, (first, spots) in enumerate(PARTS):
        rows = pl.ds(first * FRAMES, spots * FRAMES)
        (
            px, pcot, ps1, ps2, phidden, pinverse, pnormed, ppacked, pattended, pgrad_att,
            pgrad_packed, pgrad_hidden, pa1, pa2, pgv,
        ) = (ref.at[rows] for ref in tall)
        blocks = BLOCKS[part]
        coming.arrive(part)
        unpack_in(part, landed, px, pcot)
        if part == 1:
            going.forward(0)
        forward(blocks, w, gain, px, ps1, ps2, phidden, pinverse, pnormed, ppacked)
        attention(blocks, w, pcot, ppacked, pattended, pgrad_att, pgrad_packed)

        def add(n, left, right):
            product = mm_tn(left, right)
            if part == 0:
                acc[n] = product
            else:
                sums[n // 4, n % 4] = (acc[n] + product).astype(BF16)

        def early_sums():
            add(0, pattended[...], pcot[...])
            for i in range(3):
                add(1 + i, pnormed[...], pgrad_packed[:, i * C : (i + 1) * C])

        def late_sums():
            for tap, ref in enumerate((px, ps1, ps2)):
                add(4 + tap, ref[...], pgrad_hidden[...])

        def send_back():
            pack_out(part, pgv, parcels_out)
            landed_out[me.tm, 32 * part : 32 * part + 32, :] = (
                parcels_out[me.tm, 32 * part : 32 * part + 32, :]
            )

        def norm_back():
            return normalize_back(w, gain, pcot, phidden, pinverse, pgrad_packed, pgrad_hidden)

        if part == 0:
            gain_acc[...] = norm_back()
            conv_back(blocks, w, pgrad_hidden, pa1, pa2, pgv)
            send_back()
            each_peer(lambda k: going.send(0, k))
            early_sums()
            late_sums()
        else:
            early_sums()
            total.core_send(0)
            gain_sum = gain_acc[...] + norm_back()
            row, col = iotas(C, C)
            sums[1, 3] = jnp.where(row == col, gain_sum, 0.0).astype(BF16)
            late_sums()
            total.core_send(1)
            total.core_add(0)
            conv_back(blocks, w, pgrad_hidden, pa1, pa2, pgv)
            total.relay(0)
            total.core_add(1)
            send_back()
            total.own_x(0)
            each_peer(lambda k: going.send(1, k))
    total.relay(1)
    total.own_x(1)
    going.forward(1)
    total.own_z()
    for part in range(2):
        going.arrive(part)
    unpack_out(landed_out, grad_video)
    total.own_y()
    total.drain()
    drain()
    coming.drain()
    going.drain()


def call(kernel, outs, scratch, places, out_places, collective=None):
    extra = {} if collective is None else dict(collective_id=collective, has_side_effects=True)
    return pl.pallas_call(
        kernel,
        out_shape=[jax.ShapeDtypeStruct(*o) for o in outs],
        in_specs=[pl.BlockSpec(memory_space=place) for place in places],
        out_specs=[pl.BlockSpec(memory_space=place) for place in out_places],
        scratch_shapes=scratch,
        compiler_params=pltpu.CompilerParams(vmem_limit_bytes=56 * 1024 * 1024, **extra),
    )


def main(*args):
    def held(*shape, kind=BF16):
        return pltpu.VMEM(shape, kind)

    tall = held(ROWS, C)
    scratch = [
        held(1, 2, 288, C), held(1, 2, 288, C), held(3, SHARE, C), held(SHARE, 3 * C), held(SHARE, C),
        held(WAYS, PIECE, 128), held(2, QUAD, C), held(WAYS, PIECE, 128), held(2, 4, 8, QUAD, C),
        held(C, WIDE), held(1, C, kind=F32), held(WAYS, BACK, 128), held(WAYS, BACK, 128),
        held(2, 2, 64, 128), held(2, 2, 32, 128), held(MATS, C, C, kind=F32),
        held(1, C, kind=F32),
        tall, tall, tall, tall, tall, held(ROWS, 1, kind=F32), tall, held(ROWS, 3 * C), tall, tall,
        held(ROWS, 3 * C), tall, tall, tall, tall,
        held(2, 4, C, C), held(2, 2, C, C), held(2, 2, C, C), held(2, HALF, C), held(2, C, C),
        held(8, QUAD, C), held(8, QUAD, C), held(QUAD, C),
    ]
    counts = [5] + [2] * 8 + [8, 8, 2, 2, 4, 4, 8, 8] + [4] * 6 + [1] * 6
    scratch += [pltpu.SemaphoreType.DMA((n,)) for n in counts]
    outs = [(args[0].shape, BF16), ((8, QUAD, C), BF16)]
    places = [pl.ANY] * 5 + [pltpu.VMEM]
    return call(main_kernel, outs, scratch, places, [pltpu.VMEM] * 2, 1)(*args)


def finish_kernel(factor, grad_in, totals, grad_video, conv, qkv, out_w, gain, sem):
    copy = pltpu.make_async_copy(grad_in, grad_video, sem)
    copy.start()
    tm = lax.axis_index("tm")
    pick = picks(lambda r: r + lax.rem(tm, 4) * SHARE, 16, QUAD)
    got = [mm(pick, totals[m]) for m in range(8)]
    for i in range(3):
        conv[i] = got[4 + i][0:SHARE] * factor
        qkv[:, i * C : (i + 1) * C] = got[1 + i][0:SHARE] * factor
    out_w[...] = got[0][0:SHARE] * factor
    row, col = iotas(C, SHARE)
    line = mm(got[7].astype(BF16), jnp.where(row == tm * SHARE + col, 1.0, 0.0).astype(BF16))
    row, col = iotas(16, SHARE)
    gain[...] = jnp.sum(jnp.where(row == col, line, 0.0), axis=0, keepdims=True) * factor
    copy.wait()


def body(video, conv_w, qkv_w, out_w, gain, cotangent):
    grad_video, totals = main(video, cotangent, conv_w, qkv_w, out_w, gain.reshape(1, SHARE))
    factor = 1.0 / math.sqrt(
        lax.axis_size("clip") * lax.axis_size("tm") * video.shape[1] * video.shape[2]
    )
    outs = [
        (video.shape, BF16), (conv_w.shape, F32), (qkv_w.shape, F32), (out_w.shape, F32),
        ((1, SHARE), F32),
    ]
    got = call(
        functools.partial(finish_kernel, factor), outs, [pltpu.SemaphoreType.DMA],
        [pltpu.VMEM] * 2, [pl.ANY] + [pltpu.VMEM] * 4,
    )(grad_video, totals)
    return (*got[:4], got[4].reshape(SHARE))


def solution(mesh):
    in_specs = (
        P("clip", "tm", None, None),
        P(None, "tm", None),
        P("tm", None),
        P("tm", None),
        P("tm"),
        P("clip", "tm", None, None),
    )
    out_specs = (
        P("clip", "tm", None, None),
        P(None, "tm", None),
        P("tm", None),
        P("tm", None),
        P("tm"),
    )
    return jax.shard_map(body, mesh=mesh, in_specs=in_specs, out_specs=out_specs, check_vma=False)
```

```python
import functools
import math

import jax
import jax.numpy as jnp
from jax import lax
from jax.experimental import pallas as pl
from jax.experimental.pallas import tpu as pltpu
from jax.sharding import PartitionSpec as P

epsilon = 1e-06
F32 = jnp.float32
BF16 = jnp.bfloat16

C = 384
FRAMES = 64
SPOTS = 9
ROWS = SPOTS * FRAMES
PARTS = ((0, 5), (5, 4))
BLOCKS = (((0, 192), (192, 128)), ((0, 128), (128, 128)))
MATS = 7
WIDE = MATS * C


def mm(a, b):
    return lax.dot_general(a, b, (((1,), (0,)), ((), ())), preferred_element_type=F32)


def mm_nt(a, b):
    return lax.dot_general(a, b, (((1,), (1,)), ((), ())), preferred_element_type=F32)


def mm_tn(a, b):
    return lax.dot_general(a, b, (((0,), (0,)), ((), ())), preferred_element_type=F32)


def iotas(rows, columns):
    shape = (rows, columns)
    return lax.broadcasted_iota(jnp.int32, shape, 0), lax.broadcasted_iota(jnp.int32, shape, 1)


def delay_matrix(size, steps):
    row, col = iotas(size, size)
    return jnp.where((row - col == steps) & ((row & (FRAMES - 1)) >= steps), 1.0, 0.0).astype(BF16)


def forward(blocks, w, gain, x, s1, s2, hidden, inverse, normed, packed):
    for steps, ref in ((1, s1), (2, s2)):
        for first, size in blocks:
            rows = pl.ds(first, size)
            ref[rows, :] = mm(delay_matrix(size, steps), x[rows, :]).astype(BF16)
    mixed = mm(x[...], w[:, 0:C]) + mm(s1[...], w[:, C : 2 * C]) + mm(s2[...], w[:, 2 * C : 3 * C])
    hidden[...] = (x[...].astype(F32) + mixed).astype(BF16)
    wide = hidden[...].astype(F32)
    inverse[...] = lax.rsqrt(jnp.mean(wide * wide, axis=-1, keepdims=True) + epsilon)
    normed[...] = (wide * inverse[...] * gain[...]).astype(BF16)
    packed[...] = mm(normed[...], w[:, 3 * C : 6 * C]).astype(BF16)


def seen(size):
    row, col = iotas(size, size)
    return ((row >> 6) == (col >> 6)) & (col <= row)


def attention(blocks, w, cot, packed, attended, grad_att, grad_packed):
    factor = 1.0 / math.sqrt(C)
    grad_att[...] = mm_nt(cot[...], w[:, 6 * C : 7 * C]).astype(BF16)
    for first, size in blocks:
        part = pl.ds(first, size)
        query, keys, values = (packed[part, i * C : (i + 1) * C] for i in range(3))
        scores = jnp.where(seen(size), mm_nt(query, keys) * factor, -1e30)
        raised = jnp.exp(scores - jnp.max(scores, axis=-1, keepdims=True))
        probs = raised / jnp.sum(raised, axis=-1, keepdims=True)
        rounded = probs.astype(BF16)
        attended[part, :] = mm(rounded, values).astype(BF16)
        incoming = grad_att[part, :]
        dprob = mm_nt(incoming, values)
        dscore = probs * (dprob - jnp.sum(dprob * probs, axis=-1, keepdims=True))
        dscore = (dscore * factor).astype(BF16)
        grad_packed[part, 0:C] = mm(dscore, keys).astype(BF16)
        grad_packed[part, C : 2 * C] = mm_tn(dscore, query).astype(BF16)
        grad_packed[part, 2 * C : 3 * C] = mm_tn(rounded, incoming).astype(BF16)


def normalize_back(w, gain, cot, hidden, inverse, grad_packed, grad_hidden):
    grad_norm = mm_nt(grad_packed[...], w[:, 3 * C : 6 * C]).astype(BF16).astype(F32)
    wide = hidden[...].astype(F32)
    inv = inverse[...]
    scaled = grad_norm * gain[...]
    inner = jnp.mean(scaled * wide, axis=-1, keepdims=True)
    back = cot[...].astype(F32) + inv * scaled - wide * (inv * inv * inv * inner)
    grad_hidden[...] = back.astype(BF16)
    return jnp.sum(grad_norm * wide * inv, axis=0, keepdims=True)


def conv_back(blocks, w, grad_hidden, a1, a2, gv):
    for steps, ref in ((1, a1), (2, a2)):
        for first, size in blocks:
            rows = pl.ds(first, size)
            ref[rows, :] = mm_tn(delay_matrix(size, steps), grad_hidden[rows, :]).astype(BF16)
    grad = grad_hidden[...].astype(F32) + mm_nt(grad_hidden[...], w[:, 0:C])
    grad = grad + mm_nt(a1[...], w[:, C : 2 * C]) + mm_nt(a2[...], w[:, 2 * C : 3 * C])
    gv[...] = grad.astype(BF16)


WAYS = 32
PIECE = 112
CUTS = ((0, 64), (64, 48))
BACK = 64
SHARE = 12
QUAD = 4 * SHARE
HALF = C // 2
MESH = pl.DeviceIdType.MESH
FAR_FIRST = (4, 3, 5, 2, 6, 1, 7)


def ninth(n):
    return (n * 57) >> 9


def fifth(n):
    return (n * 205) >> 10


def twelfth(n):
    return (n * 1366) >> 14


def picks(target, rows, columns):
    width = min(columns, 128)
    row, col = iotas(rows, width)
    lane = target(row) - col
    parts = [
        jnp.where(lane == first, 1.0, 0.0).astype(BF16)
        for first in range(0, columns // width * width, width)
    ]
    rest = columns - columns // width * width
    if rest:
        last = lane[:, 0:rest] == columns - rest
        parts.append(jnp.where(last, 1.0, 0.0).astype(BF16))
    return parts[0] if len(parts) == 1 else jnp.concatenate(parts, 1)


def wrap(n, size):
    return jnp.where(n >= size, n - size, n)


def upper(x):
    return jnp.where(x >= 2, 1, 0)


class Place:
    def __init__(self):
        self.clip, self.tm = lax.axis_index("clip"), lax.axis_index("tm")
        self.y, self.z = lax.rem(self.clip, 8), lax.div(self.tm, 4)
        self.low = lax.rem(lax.div(self.tm, 2), 2)
        self.x = lax.div(self.clip, 8) * 2 + self.low
        self.core = lax.rem(self.tm, 2)
        self.rail = self.low * 2 + self.core

    def at(self, dx=0, dy=0, dz=0, other=False):
        x, y, z = wrap(self.x + dx, 4), wrap(self.y + dy, 8), wrap(self.z + dz, 8)
        core = 1 - self.core if other else self.core
        return (upper(x) * 8 + y, z * 4 + (x - upper(x) * 2) * 2 + core)

    def peer(self, k):
        return (self.clip, wrap(self.tm + k, WAYS))


def greet(me, outer):
    barrier = pltpu.get_barrier_semaphore()

    def tell(device):
        pl.semaphore_signal(barrier, inc=1, device_id=device, device_id_type=MESH)

    def step(k, carry):
        tell(me.peer(k))
        return carry

    lax.fori_loop(1, WAYS, step, 0)
    for k in range(1, 8):
        tell(me.at(dy=k))
    for device in outer:
        tell(device)
    return lambda: pl.semaphore_wait(barrier, WAYS - 1 + 7 + len(outer))


def remote(src, dst, sems, index, device):
    return pltpu.make_async_remote_copy(
        src_ref=src, dst_ref=dst, send_sem=sems[0].at[index], recv_sem=sems[1].at[index],
        device_id=device, device_id_type=MESH,
    )


def settle(ref, sem):
    pltpu.make_async_copy(ref, ref, sem).wait()


def each_peer(act):
    def step(k, carry):
        act(k)
        return carry

    lax.fori_loop(13, WAYS, step, 0)
    lax.fori_loop(1, 13, step, 0)


def pack_in(d, video, cot, out):
    base = lax.min(lax.div(d * SPOTS, 16) * 16, 256)
    base = pl.multiple_of(base, 16)
    pieces = [
        ref[0, f, pl.ds(base, 32), c * 128 : (c + 1) * 128]
        for ref in (video, cot) for c in range(3) for f in range(2)
    ]
    shift = d * SPOTS - base

    def column(r):
        block = jnp.where(r < 64, fifth(r), (r - 64) >> 2)
        spot = jnp.where(r < 64, r - fifth(r) * 5, 5 + (r & 3))
        return block * 32 + spot + shift

    pick = picks(column, PIECE, 384)
    out[d] = mm(pick, jnp.concatenate(pieces, 0)).astype(BF16)


def pack_weights(tm, conv, qkv, out_w, gain, shard):
    row, col = iotas(SHARE, C)
    own = col == tm * SHARE + row
    line = mm(gain[...], jnp.where(own, 1.0, 0.0).astype(BF16))
    diagonal = jnp.where(own, line, 0.0).astype(BF16)
    mats = [conv[0], conv[1], conv[2], qkv[:, 0:C], qkv[:, C : 2 * C], qkv[:, 2 * C : 3 * C], out_w[...], diagonal]
    for h in range(2):
        total = 0.0
        for j in range(4):
            total = total + mm(picks(lambda r: r - j * SHARE, QUAD, SHARE), mats[4 * h + j])
        shard[h] = total.astype(BF16)


def unpack_in(part, landed, x, cot):
    (start, rows), spots = CUTS[part], PARTS[part][1]
    for a, ref in ((0, x), (1, cot)):
        for c in range(3):
            first = (a * 3 + c) * 2 * spots
            base = min(first // 16 * 16, rows - 32)

            def column(r):
                return ((r & 15) >> 1) * 32 + (r & 1) * spots + (r >> 4) + (first - base)

            pick = picks(column, spots * 16, 256)
            for g in range(4):
                source = landed[8 * g : 8 * g + 8, start + base : start + base + 32, :]
                got = mm(pick, source.reshape(256, 128)).astype(BF16)
                for p in range(spots):
                    row = p * FRAMES + 16 * g
                    ref[row : row + 16, c * 128 : (c + 1) * 128] = got[16 * p : 16 * p + 16]


def unpack_weights(weights, w, gain):
    for j in range(4):
        base, size = ((0, 16), (0, 32), (16, 32), (32, 16))[j]

        def column(r):
            block = twelfth(r)
            return ((block & 3) * 8 + (block >> 2)) * size + (r - block * SHARE) + j * SHARE - base

        pick = picks(column, C, WAYS * size)
        for h in range(2):
            m = 4 * h + j
            source = weights[h, :, :, base : base + size, :].reshape(WAYS * size, C)
            got = mm(pick, source)
            if m < MATS:
                w[:, m * C : (m + 1) * C] = got.astype(BF16)
            else:
                gain[...] = jnp.sum(got, axis=0, keepdims=True)


def pack_out(part, gv, out):
    spots = PARTS[part][1]

    def column(r):
        inner = r & 31
        block = fifth(inner) if spots == 5 else inner >> 2
        spot = inner - block * spots
        return (block >> 1) * (16 * spots) + spot * 16 + (r >> 5) * 2 + (block & 1)

    pick = picks(column, 256, 48 * spots)
    for g in range(4):
        pieces = [
            gv[p * FRAMES + 16 * g : p * FRAMES + 16 * g + 16, c * 128 : (c + 1) * 128]
            for c in range(3) for p in range(spots)
        ]
        got = mm(pick, jnp.concatenate(pieces, 0)).astype(BF16)
        out[8 * g : 8 * g + 8, 32 * part : 32 * part + 32, :] = got.reshape(8, 32, 128)


def unpack_out(landed, grad_video):
    for f in range(2):
        for c in range(3):

            def column(r):
                spot = r - ninth(r) * SPOTS
                inner = jnp.where(spot < 5, c * 10 + f * 5 + spot, 32 + c * 8 + f * 4 + spot - 5)
                return ninth(r) * BACK + inner

            pick = picks(column, 144, 16 * BACK)
            for h in range(2):
                source = landed[16 * h : 16 * h + 16].reshape(16 * BACK, 128)
                got = mm(pick, source).astype(BF16)
                grad_video[0, f, 144 * h : 144 * h + 144, c * 128 : (c + 1) * 128] = got


def gather_weights(me, shard, weights, z_sems, y_sems, x_sems, c_sems):
    half = lax.rem(me.y, 2)
    begun = []

    def go(copy):
        copy.start()
        begun.append(copy)
        return copy

    def block(dz, *rows):
        return weights.at[half, me.rail, wrap(me.z + dz, 8), *rows]

    def over_z():
        for k in (2, 6, 1, 7):
            go(remote(shard.at[half], block(0), z_sems, k, me.at(dz=k)))
        weights[half, me.rail, me.z] = shard[half]

    def onward():
        for copy in begun[:2]:
            copy.wait_recv()
        top, low = pl.ds(0, 32), pl.ds(32, 16)
        go(remote(block(6, top), block(6, top), z_sems, 4, me.at(dz=2)))
        go(remote(block(2, low), block(2, low), z_sems, 0, me.at(dz=6)))
        go(remote(block(6), block(6), z_sems, 3, me.at(dz=1)))
        go(remote(block(2), block(2), z_sems, 5, me.at(dz=7)))

    def rest(between):
        for copy in begun[2:]:
            copy.wait_recv()
        beyond = (1 - me.low) * 2 + me.core
        part = lambda h, rail, i: weights.at[h, rail, pl.ds(4 * i, 4)]
        ys, xs, cs = [], [], []
        for i, step in ((0, 1), (1, 7)):
            mine = part(half, me.rail, i)
            ys.append(go(remote(mine, mine, y_sems, i, me.at(dy=step))))
        for i, step in ((0, 1), (1, 3)):
            mine = part(half, me.rail, i)
            xs.append(go(remote(mine, mine, x_sems, i, me.at(dx=step))))
            cs.append(go(remote(mine, mine, c_sems, i, me.at(other=True))))
        between()
        for i, step in ((0, 1), (1, 3)):
            ys[i].wait_recv()
            mine = part(1 - half, me.rail, i)
            xs.append(go(remote(mine, mine, x_sems, 2 + i, me.at(dx=step))))
            cs.append(go(remote(mine, mine, c_sems, 2 + i, me.at(other=True))))
        for n in range(4):
            xs[n].wait_recv()
            mine = part(half if n < 2 else 1 - half, beyond, n % 2)
            cs.append(go(remote(mine, mine, c_sems, 4 + n, me.at(other=True))))
        for copy in cs:
            copy.wait_recv()

    def drain():
        for copy in begun:
            copy.wait_send()

    return over_z, onward, rest, drain


class Sums:
    def __init__(self, me, sums, core_in, held, mid, x_in, z_in, y_in, y_out, totals, sems):
        self.__dict__.update(locals())
        self.round = lax.rem(me.x + me.core, 2)
        self.mine = lax.div(me.x, 2)

    def to_core(self, r, i):
        slot = (self.me.core if r else 1 - self.me.core) + 2 * i
        return remote(
            self.sums.at[r, slot], self.core_in.at[r, i], self.sems["c"], 2 * r + i,
            self.me.at(other=True),
        )

    def to_mid(self, r, i):
        part = self.held.at[r, 1 - self.mine, pl.ds(i * HALF, HALF)]
        return remote(part, self.mid.at[i], self.sems["m"], 2 * r + i, self.me.at(dx=3 if i else 1))

    def to_owner(self, r, i):
        step = 3 if i else 1
        which = upper(wrap(self.me.x + step, 4))
        copy = remote(
            self.held.at[r, which], self.x_in.at[i], self.sems["x"], 2 * r + i, self.me.at(dx=step)
        )
        return which, copy

    def over_z(self, k):
        first = pl.multiple_of(wrap(self.me.z + k, 8) * QUAD, QUAD)
        part = self.held.at[self.round, self.mine, pl.ds(first, QUAD)]
        return remote(part, self.z_in.at[k], self.sems["z"], 0, self.me.at(dz=k))

    def over_y(self, k):
        mine = self.y_in.at[self.me.y]
        return remote(mine, mine, self.sems["y"], 0, self.me.at(dy=k))

    def over_row(self, k):
        dx, other = ((2, False), (2, True), (1, False), (3, False), (1, True), (3, True), (0, True))[k]
        own = self.round * 4 + self.me.x
        return remote(
            self.y_out, self.totals.at[own], self.sems["f"], 0, self.me.at(dx=dx, other=other)
        )

    def when_owner(self, r, act):
        pl.when(self.round == r)(act)

    def core_send(self, r):
        for i in range(2):
            self.to_core(r, i).start()

    def core_add(self, r):
        for i in range(2):
            self.to_core(r, i).wait_recv()
            slot = (1 - self.me.core if r else self.me.core) + 2 * i
            both = self.sums[r, slot].astype(F32) + self.core_in[r, i].astype(F32)
            self.held[r, i] = both.astype(BF16)

        def act():
            for i in range(2):
                self.to_mid(r, i).start()

        self.when_owner(r, act)

    def relay(self, r):
        def act():
            for i in range(2):
                self.to_mid(r, i).wait_recv()
                which, copy = self.to_owner(r, i)
                rows = pl.ds(i * HALF, HALF)
                both = self.held[r, which, rows, :].astype(F32) + self.mid[i].astype(F32)
                self.held[r, which, rows, :] = both.astype(BF16)
                copy.start()

        self.when_owner(1 - r, act)

    def own_x(self, r):
        def act():
            total = self.held[r, self.mine].astype(F32)
            for i in range(2):
                self.to_owner(r, i)[1].wait_recv()
                total = total + self.x_in[i].astype(F32)
            self.held[r, self.mine] = total.astype(BF16)
            for k in FAR_FIRST:
                self.over_z(k).start()

        self.when_owner(r, act)

    def own_z(self):
        here = pl.ds(pl.multiple_of(self.me.z * QUAD, QUAD), QUAD)
        total = self.held[self.round, self.mine, here, :].astype(F32)
        settle(self.z_in.at[pl.ds(1, 7)], self.sems["z"][1].at[0])
        for k in range(1, 8):
            total = total + self.z_in[k].astype(F32)
        self.y_in[self.me.y] = total.astype(BF16)
        for k in FAR_FIRST:
            self.over_y(k).start()

    def own_y(self):
        settle(self.y_in.at[pl.ds(1, 7)], self.sems["y"][1].at[0])
        total = self.y_in[0].astype(F32)
        for k in range(1, 8):
            total = total + self.y_in[k].astype(F32)
        self.y_out[...] = total.astype(BF16)
        for k in range(7):
            self.over_row(k).start()
        self.totals[self.round * 4 + self.me.x] = self.y_out[...]

    def drain(self):
        for sem in (*self.sems["f"], self.sems["z"][0], self.sems["y"][0]):
            settle(self.z_in.at[pl.ds(1, 7)], sem.at[0])
        for r in range(2):
            for i in range(2):
                self.to_core(r, i).wait_send()

            def owner(r=r):
                for i in range(2):
                    self.to_mid(r, i).wait_send()

            def other(r=r):
                for i in range(2):
                    self.to_owner(r, i)[1].wait_send()

            self.when_owner(r, owner)
            self.when_owner(1 - r, other)


def main_kernel(
    video_in, cot_in, conv_in, qkv_in, out_in, gain_in, grad_video, totals,
    video, cotangent, conv, qkv, out_w, parcels, shard, landed, weights,
    w, gain, parcels_out, landed_out, acc, gain_acc,
    x, cot, s1, s2, hidden, inverse, normed, packed, attended, grad_att, grad_packed,
    grad_hidden, a1, a2, gv,
    sums, core_in, held, mid, x_in, z_in, y_in, y_out,
    l_s, i_s, i_r, o_s, o_r, wz_s, wz_r, wy_s, wy_r, wx_s, wx_r, wc_s, wc_r,
    sc_s, sc_r, sm_s, sm_r, sx_s, sx_r, sz_s, sz_r, sy_s, sy_r, sf_s, sf_r,
):
    me = Place()
    pairs = (
        (conv_in, conv), (qkv_in, qkv), (out_in, out_w), (video_in, video), (cot_in, cotangent)
    )
    reads = [pltpu.make_async_copy(src, dst, l_s.at[n]) for n, (src, dst) in enumerate(pairs)]
    for copy in reads:
        copy.start()
    outer = jnp.where(me.low == 0, 3, 1)
    met = greet(me, [me.at(dx=dx, other=o) for dx in (2, outer) for o in (False, True)])
    for copy in reads[:3]:
        copy.wait()
    pack_weights(me.tm, conv, qkv, out_w, gain_in, shard)
    for copy in reads[3:]:
        copy.wait()
    met()

    over_z, onward, rest, drain = gather_weights(
        me, shard, weights, (wz_s, wz_r), (wy_s, wy_r), (wx_s, wx_r), (wc_s, wc_r)
    )
    over_z()

    def coming(part, k):
        device, rows = me.peer(k), pl.ds(*CUTS[part])
        return remote(
            parcels.at[device[1], rows], landed.at[me.tm, rows], (i_s, i_r), part, device
        )

    def going(part, k):
        device, rows = me.peer(k), pl.ds(32 * part, 32)
        return remote(
            parcels_out.at[device[1], rows], landed_out.at[me.tm, rows], (o_s, o_r), part, device
        )

    def arrive(part, sems):
        settle(landed.at[pl.ds(0, WAYS - 1), pl.ds(*CUTS[part])], sems.at[part])

    def returned(part, sems):
        settle(landed_out.at[pl.ds(0, WAYS - 1), pl.ds(32 * part, 32)], sems.at[part])

    def two(i, carry):
        pack_in(me.peer(2 * i)[1], video, cotangent, parcels)
        pack_in(me.peer(2 * i + 1)[1], video, cotangent, parcels)
        coming(0, 2 * i).start()
        coming(0, 2 * i + 1).start()
        return carry

    lax.fori_loop(7, 16, two, 0)
    onward()
    lax.fori_loop(1, 7, two, 0)
    pack_in(me.peer(1)[1], video, cotangent, parcels)
    coming(0, 1).start()
    pack_in(me.tm, video, cotangent, landed)
    rest(lambda: each_peer(lambda k: coming(1, k).start()))
    unpack_weights(weights, w, gain)

    total = Sums(
        me, sums, core_in, held, mid, x_in, z_in, y_in, y_out, totals,
        dict(
            c=(sc_s, sc_r), m=(sm_s, sm_r), x=(sx_s, sx_r), z=(sz_s, sz_r), y=(sy_s, sy_r),
            f=(sf_s, sf_r),
        ),
    )
    tall = (
        x, cot, s1, s2, hidden, inverse, normed, packed, attended, grad_att, grad_packed,
        grad_hidden, a1, a2, gv,
    )
    for part, (first, spots) in enumerate(PARTS):
        rows = pl.ds(first * FRAMES, spots * FRAMES)
        (
            px, pcot, ps1, ps2, phidden, pinverse, pnormed, ppacked, pattended, pgrad_att,
            pgrad_packed, pgrad_hidden, pa1, pa2, pgv,
        ) = (ref.at[rows] for ref in tall)
        blocks = BLOCKS[part]
        arrive(part, i_r)
        unpack_in(part, landed, px, pcot)
        forward(blocks, w, gain, px, ps1, ps2, phidden, pinverse, pnormed, ppacked)
        attention(blocks, w, pcot, ppacked, pattended, pgrad_att, pgrad_packed)

        def add(n, product):
            if part == 0:
                acc[n] = product
            else:
                sums[n // 4, n % 4] = (acc[n] + product).astype(BF16)

        def early_sums():
            add(0, mm_tn(pattended[...], pcot[...]))
            product = mm_tn(pnormed[...], pgrad_packed[...])
            for i in range(3):
                add(1 + i, product[:, i * C : (i + 1) * C])

        def late_sums():
            for tap, ref in enumerate((px, ps1, ps2)):
                add(4 + tap, mm_tn(ref[...], pgrad_hidden[...]))

        def send_back():
            pack_out(part, pgv, parcels_out)
            landed_out[me.tm, 32 * part : 32 * part + 32, :] = (
                parcels_out[me.tm, 32 * part : 32 * part + 32, :]
            )

        def norm_back():
            return normalize_back(w, gain, pcot, phidden, pinverse, pgrad_packed, pgrad_hidden)

        if part == 0:
            gain_acc[...] = norm_back()
            conv_back(blocks, w, pgrad_hidden, pa1, pa2, pgv)
            send_back()
            each_peer(lambda k: going(0, k).start())
            early_sums()
            late_sums()
        else:
            early_sums()
            total.core_send(0)
            gain_sum = gain_acc[...] + norm_back()
            row, col = iotas(C, C)
            sums[1, 3] = jnp.where(row == col, gain_sum, 0.0).astype(BF16)
            late_sums()
            total.core_send(1)
            total.core_add(0)
            conv_back(blocks, w, pgrad_hidden, pa1, pa2, pgv)
            total.relay(0)
            total.core_add(1)
            send_back()
            total.own_x(0)
            each_peer(lambda k: going(1, k).start())
    total.relay(1)
    total.own_x(1)
    total.own_z()
    for part in range(2):
        returned(part, o_r)
    unpack_out(landed_out, grad_video)
    total.own_y()
    total.drain()
    drain()
    for part in range(2):
        arrive(part, i_s)
        returned(part, o_s)


def call(kernel, outs, scratch, places, out_places, mib, collective=None):
    extra = {} if collective is None else dict(collective_id=collective, has_side_effects=True)
    return pl.pallas_call(
        kernel,
        out_shape=[jax.ShapeDtypeStruct(*o) for o in outs],
        in_specs=[pl.BlockSpec(memory_space=place) for place in places],
        out_specs=[pl.BlockSpec(memory_space=place) for place in out_places],
        scratch_shapes=scratch,
        compiler_params=pltpu.CompilerParams(vmem_limit_bytes=mib * 1024 * 1024, **extra),
    )


def main(*args):
    def held(*shape, kind=BF16):
        return pltpu.VMEM(shape, kind)

    tall = held(ROWS, C)
    scratch = [
        held(1, 2, 288, C), held(1, 2, 288, C), held(3, SHARE, C), held(SHARE, 3 * C), held(SHARE, C),
        held(WAYS, PIECE, 128), held(2, QUAD, C), held(WAYS, PIECE, 128), held(2, 4, 8, QUAD, C),
        held(C, WIDE), held(1, C, kind=F32), held(WAYS, BACK, 128), held(WAYS, BACK, 128), held(MATS, C, C, kind=F32),
        held(1, C, kind=F32),
        tall, tall, tall, tall, tall, held(ROWS, 1, kind=F32), tall, held(ROWS, 3 * C), tall, tall,
        held(ROWS, 3 * C), tall, tall, tall, tall,
        held(2, 4, C, C), held(2, 2, C, C), held(2, 2, C, C), held(2, HALF, C), held(2, C, C),
        held(8, QUAD, C), held(8, QUAD, C), held(QUAD, C),
    ]
    counts = [5] + [2] * 4 + [8, 8, 2, 2, 4, 4, 8, 8] + [4] * 6 + [1] * 6
    scratch += [pltpu.SemaphoreType.DMA((n,)) for n in counts]
    outs = [(args[0].shape, BF16), ((8, QUAD, C), BF16)]
    places = [pl.ANY] * 5 + [pltpu.VMEM]
    return call(main_kernel, outs, scratch, places, [pltpu.VMEM] * 2, 56, 1)(*args)


def finish_kernel(factor, grad_in, totals, grad_video, conv, qkv, out_w, gain):
    grad_video[...] = grad_in[...]
    tm = lax.axis_index("tm")
    pick = picks(lambda r: r + lax.rem(tm, 4) * SHARE, 16, QUAD)
    got = [mm(pick, totals[m]) for m in range(8)]
    for i in range(3):
        conv[i] = got[4 + i][0:SHARE] * factor
        qkv[:, i * C : (i + 1) * C] = got[1 + i][0:SHARE] * factor
    out_w[...] = got[0][0:SHARE] * factor
    row, col = iotas(C, SHARE)
    line = mm(got[7].astype(BF16), jnp.where(row == tm * SHARE + col, 1.0, 0.0).astype(BF16))
    row, col = iotas(16, SHARE)
    gain[...] = jnp.sum(jnp.where(row == col, line, 0.0), axis=0, keepdims=True) * factor


def body(video, conv_w, qkv_w, out_w, gain, cotangent):
    grad_video, totals = main(video, cotangent, conv_w, qkv_w, out_w, gain.reshape(1, SHARE))
    factor = 1.0 / math.sqrt(
        lax.axis_size("clip") * lax.axis_size("tm") * video.shape[1] * video.shape[2]
    )
    outs = [
        (video.shape, BF16), (conv_w.shape, F32), (qkv_w.shape, F32), (out_w.shape, F32),
        ((1, SHARE), F32),
    ]
    got = call(
        functools.partial(finish_kernel, factor), outs, [], [pltpu.VMEM] * 2, [pltpu.VMEM] * 5, 8
    )(grad_video, totals)
    return (*got[:4], got[4].reshape(SHARE))


def solution(mesh):
    in_specs = (
        P("clip", "tm", None, None),
        P(None, "tm", None),
        P("tm", None),
        P("tm", None),
        P("tm"),
        P("clip", "tm", None, None),
    )
    out_specs = (
        P("clip", "tm", None, None),
        P(None, "tm", None),
        P("tm", None),
        P("tm", None),
        P("tm"),
    )
    return jax.shard_map(body, mesh=mesh, in_specs=in_specs, out_specs=out_specs, check_vma=False)
```

```python
import functools
import math

import jax
import jax.numpy as jnp
from jax import lax
from jax.experimental import pallas as pl
from jax.experimental.pallas import tpu as pltpu
from jax.sharding import PartitionSpec as P

epsilon = 1e-06
F32 = jnp.float32
BF16 = jnp.bfloat16

C = 384
FRAMES = 64
SPOTS = 9
ROWS = SPOTS * FRAMES
PARTS = ((0, 5), (5, 4))
BLOCKS = (((0, 192), (192, 128)), ((0, 128), (128, 128)))
MATS = 7
WIDE = MATS * C


def mm(a, b):
    return lax.dot_general(a, b, (((1,), (0,)), ((), ())), preferred_element_type=F32)


def mm_nt(a, b):
    return lax.dot_general(a, b, (((1,), (1,)), ((), ())), preferred_element_type=F32)


def mm_tn(a, b):
    return lax.dot_general(a, b, (((0,), (0,)), ((), ())), preferred_element_type=F32)


def iotas(rows, columns):
    shape = (rows, columns)
    return lax.broadcasted_iota(jnp.int32, shape, 0), lax.broadcasted_iota(jnp.int32, shape, 1)


def delay_matrix(size, steps):
    row, col = iotas(size, size)
    return jnp.where((row - col == steps) & ((row & (FRAMES - 1)) >= steps), 1.0, 0.0).astype(BF16)


def forward(blocks, w, gain, x, s1, s2, hidden, inverse, normed, packed):
    for steps, ref in ((1, s1), (2, s2)):
        for first, size in blocks:
            rows = pl.ds(first, size)
            ref[rows, :] = mm(delay_matrix(size, steps), x[rows, :]).astype(BF16)
    mixed = mm(x[...], w[:, 0:C]) + mm(s1[...], w[:, C : 2 * C]) + mm(s2[...], w[:, 2 * C : 3 * C])
    hidden[...] = (x[...].astype(F32) + mixed).astype(BF16)
    wide = hidden[...].astype(F32)
    inverse[...] = lax.rsqrt(jnp.mean(wide * wide, axis=-1, keepdims=True) + epsilon)
    normed[...] = (wide * inverse[...] * gain[...]).astype(BF16)
    packed[...] = mm(normed[...], w[:, 3 * C : 6 * C]).astype(BF16)


def seen(size):
    row, col = iotas(size, size)
    return ((row >> 6) == (col >> 6)) & (col <= row)


def attention(blocks, w, cot, packed, attended, grad_att, grad_packed):
    factor = 1.0 / math.sqrt(C)
    grad_att[...] = mm_nt(cot[...], w[:, 6 * C : 7 * C]).astype(BF16)
    for first, size in blocks:
        part = pl.ds(first, size)
        query, keys, values = (packed[part, i * C : (i + 1) * C] for i in range(3))
        scores = jnp.where(seen(size), mm_nt(query, keys) * factor, -1e30)
        raised = jnp.exp(scores - jnp.max(scores, axis=-1, keepdims=True))
        probs = raised / jnp.sum(raised, axis=-1, keepdims=True)
        rounded = probs.astype(BF16)
        attended[part, :] = mm(rounded, values).astype(BF16)
        incoming = grad_att[part, :]
        dprob = mm_nt(incoming, values)
        dscore = probs * (dprob - jnp.sum(dprob * probs, axis=-1, keepdims=True))
        dscore = (dscore * factor).astype(BF16)
        grad_packed[part, 0:C] = mm(dscore, keys).astype(BF16)
        grad_packed[part, C : 2 * C] = mm_tn(dscore, query).astype(BF16)
        grad_packed[part, 2 * C : 3 * C] = mm_tn(rounded, incoming).astype(BF16)


def normalize_back(w, gain, cot, hidden, inverse, grad_packed, grad_hidden):
    grad_norm = mm_nt(grad_packed[...], w[:, 3 * C : 6 * C]).astype(BF16).astype(F32)
    wide = hidden[...].astype(F32)
    inv = inverse[...]
    scaled = grad_norm * gain[...]
    inner = jnp.mean(scaled * wide, axis=-1, keepdims=True)
    back = cot[...].astype(F32) + inv * scaled - wide * (inv * inv * inv * inner)
    grad_hidden[...] = back.astype(BF16)
    return jnp.sum(grad_norm * wide * inv, axis=0, keepdims=True)


def conv_back(blocks, w, grad_hidden, a1, a2, gv):
    for steps, ref in ((1, a1), (2, a2)):
        for first, size in blocks:
            rows = pl.ds(first, size)
            ref[rows, :] = mm_tn(delay_matrix(size, steps), grad_hidden[rows, :]).astype(BF16)
    grad = grad_hidden[...].astype(F32) + mm_nt(grad_hidden[...], w[:, 0:C])
    grad = grad + mm_nt(a1[...], w[:, C : 2 * C]) + mm_nt(a2[...], w[:, 2 * C : 3 * C])
    gv[...] = grad.astype(BF16)


WAYS = 32
PIECE = 112
CUTS = ((0, 64), (64, 48))
BACK = 64
SHARE = 12
QUAD = 4 * SHARE
HALF = C // 2
MESH = pl.DeviceIdType.MESH
FAR_FIRST = (4, 3, 5, 2, 6, 1, 7)


def ninth(n):
    return (n * 57) >> 9


def fifth(n):
    return (n * 205) >> 10


def twelfth(n):
    return (n * 1366) >> 14


def picks(target, rows, columns):
    width = min(columns, 128)
    row, col = iotas(rows, width)
    lane = target(row) - col
    parts = [
        jnp.where(lane == first, 1.0, 0.0).astype(BF16)
        for first in range(0, columns // width * width, width)
    ]
    rest = columns - columns // width * width
    if rest:
        last = lane[:, 0:rest] == columns - rest
        parts.append(jnp.where(last, 1.0, 0.0).astype(BF16))
    return parts[0] if len(parts) == 1 else jnp.concatenate(parts, 1)


def wrap(n, size):
    return jnp.where(n >= size, n - size, n)


def upper(x):
    return jnp.where(x >= 2, 1, 0)


class Place:
    def __init__(self):
        self.clip, self.tm = lax.axis_index("clip"), lax.axis_index("tm")
        self.y, self.z = lax.rem(self.clip, 8), lax.div(self.tm, 4)
        self.low = lax.rem(lax.div(self.tm, 2), 2)
        self.x = lax.div(self.clip, 8) * 2 + self.low
        self.core = lax.rem(self.tm, 2)
        self.rail = self.low * 2 + self.core

    def at(self, dx=0, dy=0, dz=0, other=False):
        x, y, z = wrap(self.x + dx, 4), wrap(self.y + dy, 8), wrap(self.z + dz, 8)
        core = 1 - self.core if other else self.core
        return (upper(x) * 8 + y, z * 4 + (x - upper(x) * 2) * 2 + core)

    def peer(self, k):
        return (self.clip, wrap(self.tm + k, WAYS))


def greet(me, outer):
    barrier = pltpu.get_barrier_semaphore()

    def tell(device):
        pl.semaphore_signal(barrier, inc=1, device_id=device, device_id_type=MESH)

    def step(k, carry):
        tell(me.peer(k))
        return carry

    lax.fori_loop(1, WAYS, step, 0)
    for k in range(1, 8):
        tell(me.at(dy=k))
    for device in outer:
        tell(device)
    return lambda: pl.semaphore_wait(barrier, WAYS - 1 + 7 + len(outer))


def remote(src, dst, sems, index, device):
    return pltpu.make_async_remote_copy(
        src_ref=src, dst_ref=dst, send_sem=sems[0].at[index], recv_sem=sems[1].at[index],
        device_id=device, device_id_type=MESH,
    )


def settle(ref, sem):
    pltpu.make_async_copy(ref, ref, sem).wait()


def each_peer(act):
    def step(i, carry):
        act(16 - i)
        act(16 + i)
        return carry

    act(16)
    lax.fori_loop(1, 16, step, 0)


def pack_in(d, video, cot, out):
    base = lax.min(lax.div(d * SPOTS, 16) * 16, 256)
    base = pl.multiple_of(base, 16)
    pieces = [
        ref[0, f, pl.ds(base, 32), c * 128 : (c + 1) * 128]
        for ref in (video, cot) for c in range(3) for f in range(2)
    ]
    shift = d * SPOTS - base

    def column(r):
        block = jnp.where(r < 64, fifth(r), (r - 64) >> 2)
        spot = jnp.where(r < 64, r - fifth(r) * 5, 5 + (r & 3))
        return block * 32 + spot + shift

    pick = picks(column, PIECE, 384)
    out[d] = mm(pick, jnp.concatenate(pieces, 0)).astype(BF16)


def pack_weights(tm, conv, qkv, out_w, gain, shard):
    row, col = iotas(SHARE, C)
    own = col == tm * SHARE + row
    line = mm(gain[...], jnp.where(own, 1.0, 0.0).astype(BF16))
    diagonal = jnp.where(own, line, 0.0).astype(BF16)
    mats = [conv[0], conv[1], conv[2], qkv[:, 0:C], qkv[:, C : 2 * C], qkv[:, 2 * C : 3 * C], out_w[...], diagonal]
    for h in range(2):
        total = 0.0
        for j in range(4):
            total = total + mm(picks(lambda r: r - j * SHARE, QUAD, SHARE), mats[4 * h + j])
        shard[h] = total.astype(BF16)


def unpack_in(part, landed, x, cot):
    (start, rows), spots = CUTS[part], PARTS[part][1]
    for a, ref in ((0, x), (1, cot)):
        for c in range(3):
            first = (a * 3 + c) * 2 * spots
            base = min(first // 16 * 16, rows - 32)

            def column(r):
                return ((r & 15) >> 1) * 32 + (r & 1) * spots + (r >> 4) + (first - base)

            pick = picks(column, spots * 16, 256)
            for g in range(4):
                source = landed[8 * g : 8 * g + 8, start + base : start + base + 32, :]
                got = mm(pick, source.reshape(256, 128)).astype(BF16)
                for p in range(spots):
                    row = p * FRAMES + 16 * g
                    ref[row : row + 16, c * 128 : (c + 1) * 128] = got[16 * p : 16 * p + 16]


def unpack_weights(weights, w, gain):
    for j in range(4):
        base, size = ((0, 16), (0, 32), (16, 32), (32, 16))[j]

        def column(r):
            block = twelfth(r)
            return ((block & 3) * 8 + (block >> 2)) * size + (r - block * SHARE) + j * SHARE - base

        pick = picks(column, C, WAYS * size)
        for h in range(2):
            m = 4 * h + j
            source = weights[h, :, :, base : base + size, :].reshape(WAYS * size, C)
            got = mm(pick, source)
            if m < MATS:
                w[:, m * C : (m + 1) * C] = got.astype(BF16)
            else:
                gain[...] = jnp.sum(got, axis=0, keepdims=True)


def pack_out(part, gv, out):
    spots = PARTS[part][1]

    def column(r):
        inner = r & 31
        block = fifth(inner) if spots == 5 else inner >> 2
        spot = inner - block * spots
        return (block >> 1) * (16 * spots) + spot * 16 + (r >> 5) * 2 + (block & 1)

    pick = picks(column, 256, 48 * spots)
    for g in range(4):
        pieces = [
            gv[p * FRAMES + 16 * g : p * FRAMES + 16 * g + 16, c * 128 : (c + 1) * 128]
            for c in range(3) for p in range(spots)
        ]
        got = mm(pick, jnp.concatenate(pieces, 0)).astype(BF16)
        out[8 * g : 8 * g + 8, 32 * part : 32 * part + 32, :] = got.reshape(8, 32, 128)


def unpack_out(landed, grad_video):
    for f in range(2):
        for c in range(3):

            def column(r):
                spot = r - ninth(r) * SPOTS
                inner = jnp.where(spot < 5, c * 10 + f * 5 + spot, 32 + c * 8 + f * 4 + spot - 5)
                return ninth(r) * BACK + inner

            pick = picks(column, 144, 16 * BACK)
            for h in range(2):
                source = landed[16 * h : 16 * h + 16].reshape(16 * BACK, 128)
                got = mm(pick, source).astype(BF16)
                grad_video[0, f, 144 * h : 144 * h + 144, c * 128 : (c + 1) * 128] = got


def gather_weights(me, shard, weights, z_sems, y_sems, x_sems, c_sems):
    half = lax.rem(me.y, 2)
    begun = []

    def go(copy):
        copy.start()
        begun.append(copy)
        return copy

    def block(dz, *rows):
        return weights.at[half, me.rail, wrap(me.z + dz, 8), *rows]

    def over_z():
        for k in (2, 6, 1, 7):
            go(remote(shard.at[half], block(0), z_sems, k, me.at(dz=k)))
        weights[half, me.rail, me.z] = shard[half]

    def onward():
        for copy in begun[:2]:
            copy.wait_recv()
        top, low = pl.ds(0, 32), pl.ds(32, 16)
        go(remote(block(6, top), block(6, top), z_sems, 4, me.at(dz=2)))
        go(remote(block(2, low), block(2, low), z_sems, 0, me.at(dz=6)))
        go(remote(block(6), block(6), z_sems, 3, me.at(dz=1)))
        go(remote(block(2), block(2), z_sems, 5, me.at(dz=7)))

    def rest(between):
        for copy in begun[2:]:
            copy.wait_recv()
        beyond = (1 - me.low) * 2 + me.core
        part = lambda h, rail, i: weights.at[h, rail, pl.ds(4 * i, 4)]
        ys, xs, cs = [], [], []
        for i, step in ((0, 1), (1, 7)):
            mine = part(half, me.rail, i)
            ys.append(go(remote(mine, mine, y_sems, i, me.at(dy=step))))
        for i, step in ((0, 1), (1, 3)):
            mine = part(half, me.rail, i)
            xs.append(go(remote(mine, mine, x_sems, i, me.at(dx=step))))
            cs.append(go(remote(mine, mine, c_sems, i, me.at(other=True))))
        between()
        for i, step in ((0, 1), (1, 3)):
            ys[i].wait_recv()
            mine = part(1 - half, me.rail, i)
            xs.append(go(remote(mine, mine, x_sems, 2 + i, me.at(dx=step))))
            cs.append(go(remote(mine, mine, c_sems, 2 + i, me.at(other=True))))
        for n in range(4):
            xs[n].wait_recv()
            mine = part(half if n < 2 else 1 - half, beyond, n % 2)
            cs.append(go(remote(mine, mine, c_sems, 4 + n, me.at(other=True))))
        for copy in cs:
            copy.wait_recv()

    def drain():
        for copy in begun:
            copy.wait_send()

    return over_z, onward, rest, drain


class Sums:
    def __init__(self, me, sums, core_in, held, mid, x_in, z_in, y_in, y_out, totals, sems):
        self.__dict__.update(locals())
        self.round = lax.rem(me.x + me.core, 2)
        self.mine = lax.div(me.x, 2)

    def to_core(self, r, i):
        slot = (self.me.core if r else 1 - self.me.core) + 2 * i
        return remote(
            self.sums.at[r, slot], self.core_in.at[r, i], self.sems["c"], 2 * r + i,
            self.me.at(other=True),
        )

    def to_mid(self, r, i):
        part = self.held.at[r, 1 - self.mine, pl.ds(i * HALF, HALF)]
        return remote(part, self.mid.at[i], self.sems["m"], 2 * r + i, self.me.at(dx=3 if i else 1))

    def to_owner(self, r, i):
        step = 3 if i else 1
        which = upper(wrap(self.me.x + step, 4))
        copy = remote(
            self.held.at[r, which], self.x_in.at[i], self.sems["x"], 2 * r + i, self.me.at(dx=step)
        )
        return which, copy

    def over_z(self, k):
        first = pl.multiple_of(wrap(self.me.z + k, 8) * QUAD, QUAD)
        part = self.held.at[self.round, self.mine, pl.ds(first, QUAD)]
        return remote(part, self.z_in.at[k], self.sems["z"], 0, self.me.at(dz=k))

    def over_y(self, k):
        mine = self.y_in.at[self.me.y]
        return remote(mine, mine, self.sems["y"], 0, self.me.at(dy=k))

    def over_row(self, k):
        dx, other = ((2, False), (2, True), (1, False), (3, False), (1, True), (3, True), (0, True))[k]
        own = self.round * 4 + self.me.x
        return remote(
            self.y_out, self.totals.at[own], self.sems["f"], 0, self.me.at(dx=dx, other=other)
        )

    def when_owner(self, r, act):
        pl.when(self.round == r)(act)

    def core_send(self, r):
        for i in range(2):
            self.to_core(r, i).start()

    def core_add(self, r):
        for i in range(2):
            self.to_core(r, i).wait_recv()
            slot = (1 - self.me.core if r else self.me.core) + 2 * i
            both = self.sums[r, slot].astype(F32) + self.core_in[r, i].astype(F32)
            self.held[r, i] = both.astype(BF16)

        def act():
            for i in range(2):
                self.to_mid(r, i).start()

        self.when_owner(r, act)

    def relay(self, r):
        def act():
            for i in range(2):
                self.to_mid(r, i).wait_recv()
                which, copy = self.to_owner(r, i)
                rows = pl.ds(i * HALF, HALF)
                both = self.held[r, which, rows, :].astype(F32) + self.mid[i].astype(F32)
                self.held[r, which, rows, :] = both.astype(BF16)
                copy.start()

        self.when_owner(1 - r, act)

    def own_x(self, r):
        def act():
            total = self.held[r, self.mine].astype(F32)
            for i in range(2):
                self.to_owner(r, i)[1].wait_recv()
                total = total + self.x_in[i].astype(F32)
            self.held[r, self.mine] = total.astype(BF16)
            for k in FAR_FIRST:
                self.over_z(k).start()

        self.when_owner(r, act)

    def own_z(self):
        here = pl.ds(pl.multiple_of(self.me.z * QUAD, QUAD), QUAD)
        total = self.held[self.round, self.mine, here, :].astype(F32)
        settle(self.z_in.at[pl.ds(1, 7)], self.sems["z"][1].at[0])
        for k in range(1, 8):
            total = total + self.z_in[k].astype(F32)
        self.y_in[self.me.y] = total.astype(BF16)
        for k in FAR_FIRST:
            self.over_y(k).start()

    def own_y(self):
        settle(self.y_in.at[pl.ds(1, 7)], self.sems["y"][1].at[0])
        total = self.y_in[0].astype(F32)
        for k in range(1, 8):
            total = total + self.y_in[k].astype(F32)
        self.y_out[...] = total.astype(BF16)
        for k in range(7):
            self.over_row(k).start()
        self.totals[self.round * 4 + self.me.x] = self.y_out[...]

    def drain(self):
        for sem in (*self.sems["f"], self.sems["z"][0], self.sems["y"][0]):
            settle(self.z_in.at[pl.ds(1, 7)], sem.at[0])
        for r in range(2):
            for i in range(2):
                self.to_core(r, i).wait_send()

            def owner(r=r):
                for i in range(2):
                    self.to_mid(r, i).wait_send()

            def other(r=r):
                for i in range(2):
                    self.to_owner(r, i)[1].wait_send()

            self.when_owner(r, owner)
            self.when_owner(1 - r, other)


def main_kernel(
    video_in, cot_in, conv_in, qkv_in, out_in, gain_in, grad_video, totals,
    video, cotangent, conv, qkv, out_w, parcels, shard, landed, weights,
    w, gain, parcels_out, landed_out, acc, gain_acc,
    x, cot, s1, s2, hidden, inverse, normed, packed, attended, grad_att, grad_packed,
    grad_hidden, a1, a2, gv,
    sums, core_in, held, mid, x_in, z_in, y_in, y_out,
    l_s, i_s, i_r, o_s, o_r, wz_s, wz_r, wy_s, wy_r, wx_s, wx_r, wc_s, wc_r,
    sc_s, sc_r, sm_s, sm_r, sx_s, sx_r, sz_s, sz_r, sy_s, sy_r, sf_s, sf_r,
):
    me = Place()
    pairs = (
        (conv_in, conv), (qkv_in, qkv), (out_in, out_w), (video_in, video), (cot_in, cotangent)
    )
    reads = [pltpu.make_async_copy(src, dst, l_s.at[n]) for n, (src, dst) in enumerate(pairs)]
    for copy in reads:
        copy.start()
    outer = jnp.where(me.low == 0, 3, 1)
    met = greet(me, [me.at(dx=dx, other=o) for dx in (2, outer) for o in (False, True)])
    for copy in reads[:3]:
        copy.wait()
    pack_weights(me.tm, conv, qkv, out_w, gain_in, shard)
    for copy in reads[3:]:
        copy.wait()
    met()

    over_z, onward, rest, drain = gather_weights(
        me, shard, weights, (wz_s, wz_r), (wy_s, wy_r), (wx_s, wx_r), (wc_s, wc_r)
    )
    over_z()

    def coming(part, k):
        device, rows = me.peer(k), pl.ds(*CUTS[part])
        return remote(
            parcels.at[device[1], rows], landed.at[me.tm, rows], (i_s, i_r), part, device
        )

    def going(part, k):
        device, rows = me.peer(k), pl.ds(32 * part, 32)
        return remote(
            parcels_out.at[device[1], rows], landed_out.at[me.tm, rows], (o_s, o_r), part, device
        )

    def arrive(part, sems):
        settle(landed.at[pl.ds(0, WAYS - 1), pl.ds(*CUTS[part])], sems.at[part])

    def returned(part, sems):
        settle(landed_out.at[pl.ds(0, WAYS - 1), pl.ds(32 * part, 32)], sems.at[part])

    def two(i, carry):
        for k in (16 - i, 16 + i):
            pack_in(me.peer(k)[1], video, cotangent, parcels)
        for k in (16 - i, 16 + i):
            coming(0, k).start()
        return carry

    pack_in(me.peer(16)[1], video, cotangent, parcels)
    coming(0, 16).start()
    lax.fori_loop(1, 6, two, 0)
    onward()
    lax.fori_loop(6, 16, two, 0)
    pack_in(me.tm, video, cotangent, landed)
    rest(lambda: each_peer(lambda k: coming(1, k).start()))
    unpack_weights(weights, w, gain)

    total = Sums(
        me, sums, core_in, held, mid, x_in, z_in, y_in, y_out, totals,
        dict(
            c=(sc_s, sc_r), m=(sm_s, sm_r), x=(sx_s, sx_r), z=(sz_s, sz_r), y=(sy_s, sy_r),
            f=(sf_s, sf_r),
        ),
    )
    tall = (
        x, cot, s1, s2, hidden, inverse, normed, packed, attended, grad_att, grad_packed,
        grad_hidden, a1, a2, gv,
    )
    for part, (first, spots) in enumerate(PARTS):
        rows = pl.ds(first * FRAMES, spots * FRAMES)
        (
            px, pcot, ps1, ps2, phidden, pinverse, pnormed, ppacked, pattended, pgrad_att,
            pgrad_packed, pgrad_hidden, pa1, pa2, pgv,
        ) = (ref.at[rows] for ref in tall)
        blocks = BLOCKS[part]
        arrive(part, i_r)
        unpack_in(part, landed, px, pcot)
        forward(blocks, w, gain, px, ps1, ps2, phidden, pinverse, pnormed, ppacked)
        attention(blocks, w, pcot, ppacked, pattended, pgrad_att, pgrad_packed)

        def add(n, product):
            if part == 0:
                acc[n] = product
            else:
                sums[n // 4, n % 4] = (acc[n] + product).astype(BF16)

        def early_sums():
            add(0, mm_tn(pattended[...], pcot[...]))
            product = mm_tn(pnormed[...], pgrad_packed[...])
            for i in range(3):
                add(1 + i, product[:, i * C : (i + 1) * C])

        def late_sums():
            for tap, ref in enumerate((px, ps1, ps2)):
                add(4 + tap, mm_tn(ref[...], pgrad_hidden[...]))

        def send_back():
            pack_out(part, pgv, parcels_out)
            landed_out[me.tm, 32 * part : 32 * part + 32, :] = (
                parcels_out[me.tm, 32 * part : 32 * part + 32, :]
            )

        def norm_back():
            return normalize_back(w, gain, pcot, phidden, pinverse, pgrad_packed, pgrad_hidden)

        if part == 0:
            gain_acc[...] = norm_back()
            conv_back(blocks, w, pgrad_hidden, pa1, pa2, pgv)
            send_back()
            each_peer(lambda k: going(0, k).start())
            early_sums()
            late_sums()
        else:
            early_sums()
            total.core_send(0)
            gain_sum = gain_acc[...] + norm_back()
            row, col = iotas(C, C)
            sums[1, 3] = jnp.where(row == col, gain_sum, 0.0).astype(BF16)
            late_sums()
            total.core_send(1)
            total.core_add(0)
            conv_back(blocks, w, pgrad_hidden, pa1, pa2, pgv)
            total.relay(0)
            total.core_add(1)
            send_back()
            total.own_x(0)
            each_peer(lambda k: going(1, k).start())
    total.relay(1)
    total.own_x(1)
    total.own_z()
    for part in range(2):
        returned(part, o_r)
    unpack_out(landed_out, grad_video)
    total.own_y()
    total.drain()
    drain()
    for part in range(2):
        arrive(part, i_s)
        returned(part, o_s)


def call(kernel, outs, scratch, places, out_places, mib, collective=None):
    extra = {} if collective is None else dict(collective_id=collective, has_side_effects=True)
    return pl.pallas_call(
        kernel,
        out_shape=[jax.ShapeDtypeStruct(*o) for o in outs],
        in_specs=[pl.BlockSpec(memory_space=place) for place in places],
        out_specs=[pl.BlockSpec(memory_space=place) for place in out_places],
        scratch_shapes=scratch,
        compiler_params=pltpu.CompilerParams(vmem_limit_bytes=mib * 1024 * 1024, **extra),
    )


def main(*args):
    def held(*shape, kind=BF16):
        return pltpu.VMEM(shape, kind)

    tall = held(ROWS, C)
    scratch = [
        held(1, 2, 288, C), held(1, 2, 288, C), held(3, SHARE, C), held(SHARE, 3 * C), held(SHARE, C),
        held(WAYS, PIECE, 128), held(2, QUAD, C), held(WAYS, PIECE, 128), held(2, 4, 8, QUAD, C),
        held(C, WIDE), held(1, C, kind=F32), held(WAYS, BACK, 128), held(WAYS, BACK, 128), held(MATS, C, C, kind=F32),
        held(1, C, kind=F32),
        tall, tall, tall, tall, tall, held(ROWS, 1, kind=F32), tall, held(ROWS, 3 * C), tall, tall,
        held(ROWS, 3 * C), tall, tall, tall, tall,
        held(2, 4, C, C), held(2, 2, C, C), held(2, 2, C, C), held(2, HALF, C), held(2, C, C),
        held(8, QUAD, C), held(8, QUAD, C), held(QUAD, C),
    ]
    counts = [5] + [2] * 4 + [8, 8, 2, 2, 4, 4, 8, 8] + [4] * 6 + [1] * 6
    scratch += [pltpu.SemaphoreType.DMA((n,)) for n in counts]
    outs = [(args[0].shape, BF16), ((8, QUAD, C), BF16)]
    places = [pl.ANY] * 5 + [pltpu.VMEM]
    return call(main_kernel, outs, scratch, places, [pltpu.VMEM] * 2, 56, 1)(*args)


def finish_kernel(
    factor, grad_in, totals_in, grad_video, conv, qkv, out_w, gain, grad, totals, sems
):
    come = pltpu.make_async_copy(grad_in, grad, sems.at[0])
    come.start()
    read = pltpu.make_async_copy(totals_in, totals, sems.at[1])
    read.start()
    come.wait()
    go = pltpu.make_async_copy(grad, grad_video, sems.at[2])
    go.start()
    read.wait()
    tm = lax.axis_index("tm")
    pick = picks(lambda r: r + lax.rem(tm, 4) * SHARE, 16, QUAD)
    got = [mm(pick, totals[m]) for m in range(8)]
    for i in range(3):
        conv[i] = got[4 + i][0:SHARE] * factor
        qkv[:, i * C : (i + 1) * C] = got[1 + i][0:SHARE] * factor
    out_w[...] = got[0][0:SHARE] * factor
    row, col = iotas(C, SHARE)
    line = mm(got[7].astype(BF16), jnp.where(row == tm * SHARE + col, 1.0, 0.0).astype(BF16))
    row, col = iotas(16, SHARE)
    gain[...] = jnp.sum(jnp.where(row == col, line, 0.0), axis=0, keepdims=True) * factor
    go.wait()


def body(video, conv_w, qkv_w, out_w, gain, cotangent):
    grad_video, totals = main(video, cotangent, conv_w, qkv_w, out_w, gain.reshape(1, SHARE))
    factor = 1.0 / math.sqrt(
        lax.axis_size("clip") * lax.axis_size("tm") * video.shape[1] * video.shape[2]
    )
    outs = [
        (video.shape, BF16), (conv_w.shape, F32), (qkv_w.shape, F32), (out_w.shape, F32),
        ((1, SHARE), F32),
    ]
    got = call(
        functools.partial(finish_kernel, factor), outs,
        [
            pltpu.VMEM(video.shape, BF16), pltpu.VMEM((8, QUAD, C), BF16),
            pltpu.SemaphoreType.DMA((3,)),
        ],
        [pl.ANY] * 2, [pl.ANY] + [pltpu.VMEM] * 4, 56,
    )(grad_video, totals)
    return (*got[:4], got[4].reshape(SHARE))


def solution(mesh):
    in_specs = (
        P("clip", "tm", None, None),
        P(None, "tm", None),
        P("tm", None),
        P("tm", None),
        P("tm"),
        P("clip", "tm", None, None),
    )
    out_specs = (
        P("clip", "tm", None, None),
        P(None, "tm", None),
        P("tm", None),
        P("tm", None),
        P("tm"),
    )
    return jax.shard_map(body, mesh=mesh, in_specs=in_specs, out_specs=out_specs, check_vma=False)
```

```python
import functools
import math

import jax
import jax.numpy as jnp
from jax import lax
from jax.experimental import pallas as pl
from jax.experimental.pallas import tpu as pltpu
from jax.sharding import PartitionSpec as P

epsilon = 1e-06
F32 = jnp.float32
BF16 = jnp.bfloat16

C = 384
FRAMES = 64
SPOTS = 9
ROWS = SPOTS * FRAMES
PARTS = ((0, 5), (5, 4))
BLOCKS = (((0, 192), (192, 128)), ((0, 128), (128, 128)))
MATS = 7
WIDE = MATS * C


def mm(a, b):
    return lax.dot_general(a, b, (((1,), (0,)), ((), ())), preferred_element_type=F32)


def mm_nt(a, b):
    return lax.dot_general(a, b, (((1,), (1,)), ((), ())), preferred_element_type=F32)


def mm_tn(a, b):
    return lax.dot_general(a, b, (((0,), (0,)), ((), ())), preferred_element_type=F32)


def iotas(rows, columns):
    shape = (rows, columns)
    return lax.broadcasted_iota(jnp.int32, shape, 0), lax.broadcasted_iota(jnp.int32, shape, 1)


def delay_matrix(size, steps):
    row, col = iotas(size, size)
    return jnp.where((row - col == steps) & ((row & (FRAMES - 1)) >= steps), 1.0, 0.0).astype(BF16)


def forward(blocks, w, gain, x, s1, s2, hidden, inverse, normed, packed):
    for steps, ref in ((1, s1), (2, s2)):
        for first, size in blocks:
            rows = pl.ds(first, size)
            ref[rows, :] = mm(delay_matrix(size, steps), x[rows, :]).astype(BF16)
    mixed = mm(x[...], w[:, 0:C]) + mm(s1[...], w[:, C : 2 * C]) + mm(s2[...], w[:, 2 * C : 3 * C])
    hidden[...] = (x[...].astype(F32) + mixed).astype(BF16)
    wide = hidden[...].astype(F32)
    inverse[...] = lax.rsqrt(jnp.mean(wide * wide, axis=-1, keepdims=True) + epsilon)
    normed[...] = (wide * inverse[...] * gain[...]).astype(BF16)
    packed[...] = mm(normed[...], w[:, 3 * C : 6 * C]).astype(BF16)


def seen(size):
    row, col = iotas(size, size)
    return ((row >> 6) == (col >> 6)) & (col <= row)


def attention(blocks, w, cot, packed, attended, grad_att, grad_packed):
    factor = 1.0 / math.sqrt(C)
    grad_att[...] = mm_nt(cot[...], w[:, 6 * C : 7 * C]).astype(BF16)
    for first, size in blocks:
        part = pl.ds(first, size)
        query, keys, values = (packed[part, i * C : (i + 1) * C] for i in range(3))
        scores = jnp.where(seen(size), mm_nt(query, keys) * factor, -1e30)
        raised = jnp.exp(scores - jnp.max(scores, axis=-1, keepdims=True))
        probs = raised / jnp.sum(raised, axis=-1, keepdims=True)
        rounded = probs.astype(BF16)
        attended[part, :] = mm(rounded, values).astype(BF16)
        incoming = grad_att[part, :]
        dprob = mm_nt(incoming, values)
        dscore = probs * (dprob - jnp.sum(dprob * probs, axis=-1, keepdims=True))
        dscore = (dscore * factor).astype(BF16)
        grad_packed[part, 0:C] = mm(dscore, keys).astype(BF16)
        grad_packed[part, C : 2 * C] = mm_tn(dscore, query).astype(BF16)
        grad_packed[part, 2 * C : 3 * C] = mm_tn(rounded, incoming).astype(BF16)


def normalize_back(w, gain, cot, hidden, inverse, grad_packed, grad_hidden):
    grad_norm = mm_nt(grad_packed[...], w[:, 3 * C : 6 * C]).astype(BF16).astype(F32)
    wide = hidden[...].astype(F32)
    inv = inverse[...]
    scaled = grad_norm * gain[...]
    inner = jnp.mean(scaled * wide, axis=-1, keepdims=True)
    back = cot[...].astype(F32) + inv * scaled - wide * (inv * inv * inv * inner)
    grad_hidden[...] = back.astype(BF16)
    return jnp.sum(grad_norm * wide * inv, axis=0, keepdims=True)


def conv_back(blocks, w, grad_hidden, a1, a2, gv):
    for steps, ref in ((1, a1), (2, a2)):
        for first, size in blocks:
            rows = pl.ds(first, size)
            ref[rows, :] = mm_tn(delay_matrix(size, steps), grad_hidden[rows, :]).astype(BF16)
    grad = grad_hidden[...].astype(F32) + mm_nt(grad_hidden[...], w[:, 0:C])
    grad = grad + mm_nt(a1[...], w[:, C : 2 * C]) + mm_nt(a2[...], w[:, 2 * C : 3 * C])
    gv[...] = grad.astype(BF16)


WAYS = 32
PIECE = 112
CUTS = ((0, 64), (64, 48))
BACK = 64
SHARE = 12
QUAD = 4 * SHARE
HALF = C // 2
MESH = pl.DeviceIdType.MESH
FAR_FIRST = (4, 3, 5, 2, 6, 1, 7)


def ninth(n):
    return (n * 57) >> 9


def fifth(n):
    return (n * 205) >> 10


def twelfth(n):
    return (n * 1366) >> 14


def picks(target, rows, columns):
    width = min(columns, 128)
    row, col = iotas(rows, width)
    lane = target(row) - col
    parts = [
        jnp.where(lane == first, 1.0, 0.0).astype(BF16)
        for first in range(0, columns // width * width, width)
    ]
    rest = columns - columns // width * width
    if rest:
        last = lane[:, 0:rest] == columns - rest
        parts.append(jnp.where(last, 1.0, 0.0).astype(BF16))
    return parts[0] if len(parts) == 1 else jnp.concatenate(parts, 1)


def wrap(n, size):
    return jnp.where(n >= size, n - size, n)


def upper(x):
    return jnp.where(x >= 2, 1, 0)


class Place:
    def __init__(self):
        self.clip, self.tm = lax.axis_index("clip"), lax.axis_index("tm")
        self.y, self.z = lax.rem(self.clip, 8), lax.div(self.tm, 4)
        self.low = lax.rem(lax.div(self.tm, 2), 2)
        self.x = lax.div(self.clip, 8) * 2 + self.low
        self.core = lax.rem(self.tm, 2)
        self.rail = self.low * 2 + self.core

    def at(self, dx=0, dy=0, dz=0, other=False):
        x, y, z = wrap(self.x + dx, 4), wrap(self.y + dy, 8), wrap(self.z + dz, 8)
        core = 1 - self.core if other else self.core
        return (upper(x) * 8 + y, z * 4 + (x - upper(x) * 2) * 2 + core)

    def peer(self, k):
        return (self.clip, wrap(self.tm + k, WAYS))


def greet(me, outer):
    barrier = pltpu.get_barrier_semaphore()

    def tell(device):
        pl.semaphore_signal(barrier, inc=1, device_id=device, device_id_type=MESH)

    def step(k, carry):
        tell(me.peer(k))
        return carry

    lax.fori_loop(1, WAYS, step, 0)
    for k in range(1, 8):
        tell(me.at(dy=k))
    for device in outer:
        tell(device)
    return lambda: pl.semaphore_wait(barrier, WAYS - 1 + 7 + len(outer))


def remote(src, dst, sems, index, device):
    return pltpu.make_async_remote_copy(
        src_ref=src, dst_ref=dst, send_sem=sems[0].at[index], recv_sem=sems[1].at[index],
        device_id=device, device_id_type=MESH,
    )


def settle(ref, sem):
    pltpu.make_async_copy(ref, ref, sem).wait()


def each_peer(act, first=0, last=16):
    def step(i, carry):
        act(16 - i)
        act(16 + i)
        return carry

    if first == 0:
        act(16)
    lax.fori_loop(max(first, 1), last, step, 0)


def pack_in(d, video, cot, out):
    base = lax.min(lax.div(d * SPOTS, 16) * 16, 256)
    base = pl.multiple_of(base, 16)
    pieces = [
        ref[0, f, pl.ds(base, 32), c * 128 : (c + 1) * 128]
        for ref in (video, cot) for c in range(3) for f in range(2)
    ]
    shift = d * SPOTS - base

    def column(r):
        block = jnp.where(r < 64, fifth(r), (r - 64) >> 2)
        spot = jnp.where(r < 64, r - fifth(r) * 5, 5 + (r & 3))
        return block * 32 + spot + shift

    pick = picks(column, PIECE, 384)
    out[d] = mm(pick, jnp.concatenate(pieces, 0)).astype(BF16)


def pack_weights(tm, conv, qkv, out_w, gain, shard):
    row, col = iotas(SHARE, C)
    own = col == tm * SHARE + row
    line = mm(gain[...], jnp.where(own, 1.0, 0.0).astype(BF16))
    diagonal = jnp.where(own, line, 0.0).astype(BF16)
    mats = [conv[0], conv[1], conv[2], qkv[:, 0:C], qkv[:, C : 2 * C], qkv[:, 2 * C : 3 * C], out_w[...], diagonal]
    for h in range(2):
        total = 0.0
        for j in range(4):
            total = total + mm(picks(lambda r: r - j * SHARE, QUAD, SHARE), mats[4 * h + j])
        shard[h] = total.astype(BF16)


def unpack_in(part, landed, x, cot):
    (start, rows), spots = CUTS[part], PARTS[part][1]
    for a, ref in ((0, x), (1, cot)):
        for c in range(3):
            first = (a * 3 + c) * 2 * spots
            base = min(first // 16 * 16, rows - 32)

            def column(r):
                return ((r & 15) >> 1) * 32 + (r & 1) * spots + (r >> 4) + (first - base)

            pick = picks(column, spots * 16, 256)
            for g in range(4):
                source = landed[8 * g : 8 * g + 8, start + base : start + base + 32, :]
                got = mm(pick, source.reshape(256, 128)).astype(BF16)
                for p in range(spots):
                    row = p * FRAMES + 16 * g
                    ref[row : row + 16, c * 128 : (c + 1) * 128] = got[16 * p : 16 * p + 16]


def unpack_weights(weights, w, gain):
    for j in range(4):
        base, size = ((0, 16), (0, 32), (16, 32), (32, 16))[j]

        def column(r):
            block = twelfth(r)
            return ((block & 3) * 8 + (block >> 2)) * size + (r - block * SHARE) + j * SHARE - base

        pick = picks(column, C, WAYS * size)
        for h in range(2):
            m = 4 * h + j
            source = weights[h, :, :, base : base + size, :].reshape(WAYS * size, C)
            got = mm(pick, source)
            if m < MATS:
                w[:, m * C : (m + 1) * C] = got.astype(BF16)
            else:
                gain[...] = jnp.sum(got, axis=0, keepdims=True)


def pack_out(part, gv, out):
    spots = PARTS[part][1]

    def column(r):
        inner = r & 31
        block = fifth(inner) if spots == 5 else inner >> 2
        spot = inner - block * spots
        return (block >> 1) * (16 * spots) + spot * 16 + (r >> 5) * 2 + (block & 1)

    pick = picks(column, 256, 48 * spots)
    for g in range(4):
        pieces = [
            gv[p * FRAMES + 16 * g : p * FRAMES + 16 * g + 16, c * 128 : (c + 1) * 128]
            for c in range(3) for p in range(spots)
        ]
        got = mm(pick, jnp.concatenate(pieces, 0)).astype(BF16)
        out[8 * g : 8 * g + 8, 32 * part : 32 * part + 32, :] = got.reshape(8, 32, 128)


def unpack_out(landed, grad_video):
    for f in range(2):
        for c in range(3):

            def column(r):
                spot = r - ninth(r) * SPOTS
                inner = jnp.where(spot < 5, c * 10 + f * 5 + spot, 32 + c * 8 + f * 4 + spot - 5)
                return ninth(r) * BACK + inner

            pick = picks(column, 144, 16 * BACK)
            for h in range(2):
                source = landed[16 * h : 16 * h + 16].reshape(16 * BACK, 128)
                got = mm(pick, source).astype(BF16)
                grad_video[0, f, 144 * h : 144 * h + 144, c * 128 : (c + 1) * 128] = got


def gather_weights(me, shard, weights, z_sems, y_sems, x_sems, c_sems):
    half = lax.rem(me.y, 2)
    begun = []

    def go(copy):
        copy.start()
        begun.append(copy)
        return copy

    def block(dz, *rows):
        return weights.at[half, me.rail, wrap(me.z + dz, 8), *rows]

    def over_z():
        for k in (2, 6, 1, 7):
            go(remote(shard.at[half], block(0), z_sems, k, me.at(dz=k)))
        weights[half, me.rail, me.z] = shard[half]

    def onward():
        for copy in begun[:2]:
            copy.wait_recv()
        top, low = pl.ds(0, 32), pl.ds(32, 16)
        go(remote(block(6, top), block(6, top), z_sems, 4, me.at(dz=2)))
        go(remote(block(2, low), block(2, low), z_sems, 0, me.at(dz=6)))
        go(remote(block(6), block(6), z_sems, 3, me.at(dz=1)))
        go(remote(block(2), block(2), z_sems, 5, me.at(dz=7)))

    def rest(after):
        for copy in begun[2:]:
            copy.wait_recv()
        beyond = (1 - me.low) * 2 + me.core
        part = lambda h, rail, i: weights.at[h, rail, pl.ds(4 * i, 4)]
        ys, xs, cs = [], [], []
        for i, step in ((0, 1), (1, 7)):
            mine = part(half, me.rail, i)
            ys.append(go(remote(mine, mine, y_sems, i, me.at(dy=step))))
        for i, step in ((0, 1), (1, 3)):
            mine = part(half, me.rail, i)
            xs.append(go(remote(mine, mine, x_sems, i, me.at(dx=step))))
            cs.append(go(remote(mine, mine, c_sems, i, me.at(other=True))))
        for i, step in ((0, 1), (1, 3)):
            ys[i].wait_recv()
            mine = part(1 - half, me.rail, i)
            xs.append(go(remote(mine, mine, x_sems, 2 + i, me.at(dx=step))))
            cs.append(go(remote(mine, mine, c_sems, 2 + i, me.at(other=True))))
        for n in range(4):
            xs[n].wait_recv()
            mine = part(half if n < 2 else 1 - half, beyond, n % 2)
            cs.append(go(remote(mine, mine, c_sems, 4 + n, me.at(other=True))))
        after()
        for copy in cs:
            copy.wait_recv()

    def drain():
        for copy in begun:
            copy.wait_send()

    return over_z, onward, rest, drain


class Sums:
    def __init__(self, me, sums, core_in, held, mid, x_in, z_in, y_in, y_out, totals, sems):
        self.__dict__.update(locals())
        self.round = lax.rem(me.x + me.core, 2)
        self.mine = lax.div(me.x, 2)

    def to_core(self, r, i):
        slot = (self.me.core if r else 1 - self.me.core) + 2 * i
        return remote(
            self.sums.at[r, slot], self.core_in.at[r, i], self.sems["c"], 2 * r + i,
            self.me.at(other=True),
        )

    def to_mid(self, r, i):
        part = self.held.at[r, 1 - self.mine, pl.ds(i * HALF, HALF)]
        return remote(part, self.mid.at[i], self.sems["m"], 2 * r + i, self.me.at(dx=3 if i else 1))

    def to_owner(self, r, i):
        step = 3 if i else 1
        which = upper(wrap(self.me.x + step, 4))
        copy = remote(
            self.held.at[r, which], self.x_in.at[i], self.sems["x"], 2 * r + i, self.me.at(dx=step)
        )
        return which, copy

    def over_z(self, k):
        first = pl.multiple_of(wrap(self.me.z + k, 8) * QUAD, QUAD)
        part = self.held.at[self.round, self.mine, pl.ds(first, QUAD)]
        return remote(part, self.z_in.at[k], self.sems["z"], 0, self.me.at(dz=k))

    def over_y(self, k):
        mine = self.y_in.at[self.me.y]
        return remote(mine, mine, self.sems["y"], 0, self.me.at(dy=k))

    def over_row(self, k):
        dx, other = ((2, False), (2, True), (1, False), (3, False), (1, True), (3, True), (0, True))[k]
        own = self.round * 4 + self.me.x
        return remote(
            self.y_out, self.totals.at[own], self.sems["f"], 0, self.me.at(dx=dx, other=other)
        )

    def when_owner(self, r, act):
        pl.when(self.round == r)(act)

    def core_send(self, r):
        for i in range(2):
            self.to_core(r, i).start()

    def core_add(self, r):
        for i in range(2):
            self.to_core(r, i).wait_recv()
            slot = (1 - self.me.core if r else self.me.core) + 2 * i
            both = self.sums[r, slot].astype(F32) + self.core_in[r, i].astype(F32)
            self.held[r, i] = both.astype(BF16)

        def act():
            for i in range(2):
                self.to_mid(r, i).start()

        self.when_owner(r, act)

    def relay(self, r):
        def act():
            for i in range(2):
                self.to_mid(r, i).wait_recv()
                which, copy = self.to_owner(r, i)
                rows = pl.ds(i * HALF, HALF)
                both = self.held[r, which, rows, :].astype(F32) + self.mid[i].astype(F32)
                self.held[r, which, rows, :] = both.astype(BF16)
                copy.start()

        self.when_owner(1 - r, act)

    def own_x(self, r):
        def act():
            total = self.held[r, self.mine].astype(F32)
            for i in range(2):
                self.to_owner(r, i)[1].wait_recv()
                total = total + self.x_in[i].astype(F32)
            self.held[r, self.mine] = total.astype(BF16)
            for k in FAR_FIRST:
                self.over_z(k).start()

        self.when_owner(r, act)

    def own_z(self):
        here = pl.ds(pl.multiple_of(self.me.z * QUAD, QUAD), QUAD)
        total = self.held[self.round, self.mine, here, :].astype(F32)
        settle(self.z_in.at[pl.ds(1, 7)], self.sems["z"][1].at[0])
        for k in range(1, 8):
            total = total + self.z_in[k].astype(F32)
        self.y_in[self.me.y] = total.astype(BF16)
        for k in FAR_FIRST:
            self.over_y(k).start()

    def own_y(self):
        settle(self.y_in.at[pl.ds(1, 7)], self.sems["y"][1].at[0])
        total = self.y_in[0].astype(F32)
        for k in range(1, 8):
            total = total + self.y_in[k].astype(F32)
        self.y_out[...] = total.astype(BF16)
        for k in range(7):
            self.over_row(k).start()
        self.totals[self.round * 4 + self.me.x] = self.y_out[...]

    def drain(self):
        for sem in (*self.sems["f"], self.sems["z"][0], self.sems["y"][0]):
            settle(self.z_in.at[pl.ds(1, 7)], sem.at[0])
        for r in range(2):
            for i in range(2):
                self.to_core(r, i).wait_send()

            def owner(r=r):
                for i in range(2):
                    self.to_mid(r, i).wait_send()

            def other(r=r):
                for i in range(2):
                    self.to_owner(r, i)[1].wait_send()

            self.when_owner(r, owner)
            self.when_owner(1 - r, other)


def main_kernel(
    video_in, cot_in, conv_in, qkv_in, out_in, gain_in, grad_video, totals,
    video, cotangent, conv, qkv, out_w, parcels, shard, landed, weights,
    w, gain, parcels_out, landed_out, acc, gain_acc,
    x, cot, s1, s2, hidden, inverse, normed, packed, attended, grad_att, grad_packed,
    grad_hidden, a1, a2, gv,
    sums, core_in, held, mid, x_in, z_in, y_in, y_out,
    l_s, i_s, i_r, o_s, o_r, wz_s, wz_r, wy_s, wy_r, wx_s, wx_r, wc_s, wc_r,
    sc_s, sc_r, sm_s, sm_r, sx_s, sx_r, sz_s, sz_r, sy_s, sy_r, sf_s, sf_r,
):
    me = Place()
    pairs = (
        (conv_in, conv), (qkv_in, qkv), (out_in, out_w), (video_in, video), (cot_in, cotangent)
    )
    reads = [pltpu.make_async_copy(src, dst, l_s.at[n]) for n, (src, dst) in enumerate(pairs)]
    for copy in reads:
        copy.start()
    outer = jnp.where(me.low == 0, 3, 1)
    met = greet(me, [me.at(dx=dx, other=o) for dx in (2, outer) for o in (False, True)])
    for copy in reads[:3]:
        copy.wait()
    pack_weights(me.tm, conv, qkv, out_w, gain_in, shard)
    for copy in reads[3:]:
        copy.wait()
    met()

    over_z, onward, rest, drain = gather_weights(
        me, shard, weights, (wz_s, wz_r), (wy_s, wy_r), (wx_s, wx_r), (wc_s, wc_r)
    )
    over_z()

    def coming(part, k):
        device, rows = me.peer(k), pl.ds(*CUTS[part])
        return remote(
            parcels.at[device[1], rows], landed.at[me.tm, rows], (i_s, i_r), part, device
        )

    def going(part, k):
        device, rows = me.peer(k), pl.ds(32 * part, 32)
        return remote(
            parcels_out.at[device[1], rows], landed_out.at[me.tm, rows], (o_s, o_r), part, device
        )

    def arrive(part, sems):
        settle(landed.at[pl.ds(0, WAYS - 1), pl.ds(*CUTS[part])], sems.at[part])

    def returned(part, sems):
        settle(landed_out.at[pl.ds(0, WAYS - 1), pl.ds(32 * part, 32)], sems.at[part])

    def two(i, carry):
        for k in (16 - i, 16 + i):
            pack_in(me.peer(k)[1], video, cotangent, parcels)
        for k in (16 - i, 16 + i):
            coming(0, k).start()
        return carry

    pack_in(me.peer(16)[1], video, cotangent, parcels)
    coming(0, 16).start()
    lax.fori_loop(1, 6, two, 0)
    onward()
    lax.fori_loop(6, 16, two, 0)
    pack_in(me.tm, video, cotangent, landed)
    rest(lambda: each_peer(lambda k: coming(1, k).start()))
    unpack_weights(weights, w, gain)

    total = Sums(
        me, sums, core_in, held, mid, x_in, z_in, y_in, y_out, totals,
        dict(
            c=(sc_s, sc_r), m=(sm_s, sm_r), x=(sx_s, sx_r), z=(sz_s, sz_r), y=(sy_s, sy_r),
            f=(sf_s, sf_r),
        ),
    )
    tall = (
        x, cot, s1, s2, hidden, inverse, normed, packed, attended, grad_att, grad_packed,
        grad_hidden, a1, a2, gv,
    )
    for part, (first, spots) in enumerate(PARTS):
        rows = pl.ds(first * FRAMES, spots * FRAMES)
        (
            px, pcot, ps1, ps2, phidden, pinverse, pnormed, ppacked, pattended, pgrad_att,
            pgrad_packed, pgrad_hidden, pa1, pa2, pgv,
        ) = (ref.at[rows] for ref in tall)
        blocks = BLOCKS[part]
        arrive(part, i_r)
        unpack_in(part, landed, px, pcot)
        forward(blocks, w, gain, px, ps1, ps2, phidden, pinverse, pnormed, ppacked)
        attention(blocks, w, pcot, ppacked, pattended, pgrad_att, pgrad_packed)

        def add(n, product):
            if part == 0:
                acc[n] = product
            else:
                sums[n // 4, n % 4] = (acc[n] + product).astype(BF16)

        def early_sums():
            add(0, mm_tn(pattended[...], pcot[...]))
            product = mm_tn(pnormed[...], pgrad_packed[...])
            for i in range(3):
                add(1 + i, product[:, i * C : (i + 1) * C])

        def late_sums():
            for tap, ref in enumerate((px, ps1, ps2)):
                add(4 + tap, mm_tn(ref[...], pgrad_hidden[...]))

        def send_back():
            pack_out(part, pgv, parcels_out)
            landed_out[me.tm, 32 * part : 32 * part + 32, :] = (
                parcels_out[me.tm, 32 * part : 32 * part + 32, :]
            )

        def norm_back():
            return normalize_back(w, gain, pcot, phidden, pinverse, pgrad_packed, pgrad_hidden)

        if part == 0:
            gain_acc[...] = norm_back()
            conv_back(blocks, w, pgrad_hidden, pa1, pa2, pgv)
            send_back()
            each_peer(lambda k: going(0, k).start())
            early_sums()
            late_sums()
        else:
            early_sums()
            total.core_send(0)
            gain_sum = gain_acc[...] + norm_back()
            row, col = iotas(C, C)
            sums[1, 3] = jnp.where(row == col, gain_sum, 0.0).astype(BF16)
            late_sums()
            total.core_send(1)
            total.core_add(0)
            conv_back(blocks, w, pgrad_hidden, pa1, pa2, pgv)
            total.relay(0)
            total.core_add(1)
            send_back()
            total.own_x(0)
    total.relay(1)
    total.own_x(1)
    each_peer(lambda k: going(1, k).start(), 0, 8)
    total.own_z()
    each_peer(lambda k: going(1, k).start(), 8, 16)
    total.own_y()
    for part in range(2):
        returned(part, o_r)
    unpack_out(landed_out, grad_video)
    total.drain()
    drain()
    for part in range(2):
        arrive(part, i_s)
        returned(part, o_s)


def call(kernel, outs, scratch, places, out_places, mib, collective=None):
    extra = {} if collective is None else dict(collective_id=collective, has_side_effects=True)
    return pl.pallas_call(
        kernel,
        out_shape=[jax.ShapeDtypeStruct(*o) for o in outs],
        in_specs=[pl.BlockSpec(memory_space=place) for place in places],
        out_specs=[pl.BlockSpec(memory_space=place) for place in out_places],
        scratch_shapes=scratch,
        compiler_params=pltpu.CompilerParams(vmem_limit_bytes=mib * 1024 * 1024, **extra),
    )


def main(*args):
    def held(*shape, kind=BF16):
        return pltpu.VMEM(shape, kind)

    tall = held(ROWS, C)
    scratch = [
        held(1, 2, 288, C), held(1, 2, 288, C), held(3, SHARE, C), held(SHARE, 3 * C), held(SHARE, C),
        held(WAYS, PIECE, 128), held(2, QUAD, C), held(WAYS, PIECE, 128), held(2, 4, 8, QUAD, C),
        held(C, WIDE), held(1, C, kind=F32), held(WAYS, BACK, 128), held(WAYS, BACK, 128), held(MATS, C, C, kind=F32),
        held(1, C, kind=F32),
        tall, tall, tall, tall, tall, held(ROWS, 1, kind=F32), tall, held(ROWS, 3 * C), tall, tall,
        held(ROWS, 3 * C), tall, tall, tall, tall,
        held(2, 4, C, C), held(2, 2, C, C), held(2, 2, C, C), held(2, HALF, C), held(2, C, C),
        held(8, QUAD, C), held(8, QUAD, C), held(QUAD, C),
    ]
    counts = [5] + [2] * 4 + [8, 8, 2, 2, 4, 4, 8, 8] + [4] * 6 + [1] * 6
    scratch += [pltpu.SemaphoreType.DMA((n,)) for n in counts]
    outs = [(args[0].shape, BF16), ((8, QUAD, C), BF16)]
    places = [pl.ANY] * 5 + [pltpu.VMEM]
    return call(main_kernel, outs, scratch, places, [pltpu.VMEM] * 2, 56, 1)(*args)


def finish_kernel(
    factor, grad_in, totals_in, grad_video, conv, qkv, out_w, gain, grad, totals, sems
):
    come = pltpu.make_async_copy(grad_in, grad, sems.at[0])
    come.start()
    read = pltpu.make_async_copy(totals_in, totals, sems.at[1])
    read.start()
    come.wait()
    go = pltpu.make_async_copy(grad, grad_video, sems.at[2])
    go.start()
    read.wait()
    tm = lax.axis_index("tm")
    pick = picks(lambda r: r + lax.rem(tm, 4) * SHARE, 16, QUAD)
    got = [mm(pick, totals[m]) for m in range(8)]
    for i in range(3):
        conv[i] = got[4 + i][0:SHARE] * factor
        qkv[:, i * C : (i + 1) * C] = got[1 + i][0:SHARE] * factor
    out_w[...] = got[0][0:SHARE] * factor
    row, col = iotas(C, SHARE)
    line = mm(got[7].astype(BF16), jnp.where(row == tm * SHARE + col, 1.0, 0.0).astype(BF16))
    row, col = iotas(16, SHARE)
    gain[...] = jnp.sum(jnp.where(row == col, line, 0.0), axis=0, keepdims=True) * factor
    go.wait()


def body(video, conv_w, qkv_w, out_w, gain, cotangent):
    grad_video, totals = main(video, cotangent, conv_w, qkv_w, out_w, gain.reshape(1, SHARE))
    factor = 1.0 / math.sqrt(
        lax.axis_size("clip") * lax.axis_size("tm") * video.shape[1] * video.shape[2]
    )
    outs = [
        (video.shape, BF16), (conv_w.shape, F32), (qkv_w.shape, F32), (out_w.shape, F32),
        ((1, SHARE), F32),
    ]
    got = call(
        functools.partial(finish_kernel, factor), outs,
        [
            pltpu.VMEM(video.shape, BF16), pltpu.VMEM((8, QUAD, C), BF16),
            pltpu.SemaphoreType.DMA((3,)),
        ],
        [pl.ANY] * 2, [pl.ANY] + [pltpu.VMEM] * 4, 56,
    )(grad_video, totals)
    return (*got[:4], got[4].reshape(SHARE))


def solution(mesh):
    in_specs = (
        P("clip", "tm", None, None),
        P(None, "tm", None),
        P("tm", None),
        P("tm", None),
        P("tm"),
        P("clip", "tm", None, None),
    )
    out_specs = (
        P("clip", "tm", None, None),
        P(None, "tm", None),
        P("tm", None),
        P("tm", None),
        P("tm"),
    )
    return jax.shard_map(body, mesh=mesh, in_specs=in_specs, out_specs=out_specs, check_vma=False)
```

```python
import functools
import math

import jax
import jax.numpy as jnp
from jax import lax
from jax.experimental import pallas as pl
from jax.experimental.pallas import tpu as pltpu
from jax.sharding import PartitionSpec as P

epsilon = 1e-06
F32 = jnp.float32
BF16 = jnp.bfloat16

C = 384
FRAMES = 64
SPOTS = 9
ROWS = SPOTS * FRAMES
PARTS = ((0, 5), (5, 4))
BLOCKS = (((0, 192), (192, 128)), ((0, 128), (128, 128)))
MATS = 7
WIDE = MATS * C


def mm(a, b):
    return lax.dot_general(a, b, (((1,), (0,)), ((), ())), preferred_element_type=F32)


def mm_nt(a, b):
    return lax.dot_general(a, b, (((1,), (1,)), ((), ())), preferred_element_type=F32)


def mm_tn(a, b):
    return lax.dot_general(a, b, (((0,), (0,)), ((), ())), preferred_element_type=F32)


def iotas(rows, columns):
    shape = (rows, columns)
    return lax.broadcasted_iota(jnp.int32, shape, 0), lax.broadcasted_iota(jnp.int32, shape, 1)


def delay_matrix(size, steps):
    row, col = iotas(size, size)
    return jnp.where((row - col == steps) & ((row & (FRAMES - 1)) >= steps), 1.0, 0.0).astype(BF16)


def forward(blocks, w, gain, x, s1, s2, hidden, inverse, normed, packed):
    for steps, ref in ((1, s1), (2, s2)):
        for first, size in blocks:
            rows = pl.ds(first, size)
            ref[rows, :] = mm(delay_matrix(size, steps), x[rows, :]).astype(BF16)
    mixed = mm(x[...], w[:, 0:C]) + mm(s1[...], w[:, C : 2 * C]) + mm(s2[...], w[:, 2 * C : 3 * C])
    hidden[...] = (x[...].astype(F32) + mixed).astype(BF16)
    wide = hidden[...].astype(F32)
    inverse[...] = lax.rsqrt(jnp.mean(wide * wide, axis=-1, keepdims=True) + epsilon)
    normed[...] = (wide * inverse[...] * gain[...]).astype(BF16)
    packed[...] = mm(normed[...], w[:, 3 * C : 6 * C]).astype(BF16)


def seen(size):
    row, col = iotas(size, size)
    return ((row >> 6) == (col >> 6)) & (col <= row)


def attention(blocks, w, cot, packed, attended, grad_att, grad_packed):
    factor = 1.0 / math.sqrt(C)
    grad_att[...] = mm_nt(cot[...], w[:, 6 * C : 7 * C]).astype(BF16)
    for first, size in blocks:
        part = pl.ds(first, size)
        query, keys, values = (packed[part, i * C : (i + 1) * C] for i in range(3))
        scores = jnp.where(seen(size), mm_nt(query, keys) * factor, -1e30)
        raised = jnp.exp(scores - jnp.max(scores, axis=-1, keepdims=True))
        probs = raised / jnp.sum(raised, axis=-1, keepdims=True)
        rounded = probs.astype(BF16)
        attended[part, :] = mm(rounded, values).astype(BF16)
        incoming = grad_att[part, :]
        dprob = mm_nt(incoming, values)
        dscore = probs * (dprob - jnp.sum(dprob * probs, axis=-1, keepdims=True))
        dscore = (dscore * factor).astype(BF16)
        grad_packed[part, 0:C] = mm(dscore, keys).astype(BF16)
        grad_packed[part, C : 2 * C] = mm_tn(dscore, query).astype(BF16)
        grad_packed[part, 2 * C : 3 * C] = mm_tn(rounded, incoming).astype(BF16)


def normalize_back(w, gain, cot, hidden, inverse, grad_packed, grad_hidden):
    grad_norm = mm_nt(grad_packed[...], w[:, 3 * C : 6 * C]).astype(BF16).astype(F32)
    wide = hidden[...].astype(F32)
    inv = inverse[...]
    scaled = grad_norm * gain[...]
    inner = jnp.mean(scaled * wide, axis=-1, keepdims=True)
    back = cot[...].astype(F32) + inv * scaled - wide * (inv * inv * inv * inner)
    grad_hidden[...] = back.astype(BF16)
    return jnp.sum(grad_norm * wide * inv, axis=0, keepdims=True)


def conv_back(blocks, w, grad_hidden, a1, a2, gv):
    for steps, ref in ((1, a1), (2, a2)):
        for first, size in blocks:
            rows = pl.ds(first, size)
            ref[rows, :] = mm_tn(delay_matrix(size, steps), grad_hidden[rows, :]).astype(BF16)
    grad = grad_hidden[...].astype(F32) + mm_nt(grad_hidden[...], w[:, 0:C])
    grad = grad + mm_nt(a1[...], w[:, C : 2 * C]) + mm_nt(a2[...], w[:, 2 * C : 3 * C])
    gv[...] = grad.astype(BF16)


WAYS = 32
PIECE = 112
CUTS = ((0, 64), (64, 48))
BACK = 64
SHARE = 12
QUAD = 4 * SHARE
HALF = C // 2
MESH = pl.DeviceIdType.MESH
FAR_FIRST = (4, 3, 5, 2, 6, 1, 7)


def ninth(n):
    return (n * 57) >> 9


def fifth(n):
    return (n * 205) >> 10


def twelfth(n):
    return (n * 1366) >> 14


def picks(target, rows, columns):
    width = min(columns, 128)
    row, col = iotas(rows, width)
    lane = target(row) - col
    parts = [
        jnp.where(lane == first, 1.0, 0.0).astype(BF16)
        for first in range(0, columns // width * width, width)
    ]
    rest = columns - columns // width * width
    if rest:
        last = lane[:, 0:rest] == columns - rest
        parts.append(jnp.where(last, 1.0, 0.0).astype(BF16))
    return parts[0] if len(parts) == 1 else jnp.concatenate(parts, 1)


def wrap(n, size):
    return jnp.where(n >= size, n - size, n)


def upper(x):
    return jnp.where(x >= 2, 1, 0)


class Place:
    def __init__(self):
        self.clip, self.tm = lax.axis_index("clip"), lax.axis_index("tm")
        self.y, self.z = lax.rem(self.clip, 8), lax.div(self.tm, 4)
        self.low = lax.rem(lax.div(self.tm, 2), 2)
        self.x = lax.div(self.clip, 8) * 2 + self.low
        self.core = lax.rem(self.tm, 2)
        self.rail = self.low * 2 + self.core

    def at(self, dx=0, dy=0, dz=0, other=False):
        x, y, z = wrap(self.x + dx, 4), wrap(self.y + dy, 8), wrap(self.z + dz, 8)
        core = 1 - self.core if other else self.core
        return (upper(x) * 8 + y, z * 4 + (x - upper(x) * 2) * 2 + core)

    def peer(self, k):
        return (self.clip, wrap(self.tm + k, WAYS))


def greet(me, outer):
    barrier = pltpu.get_barrier_semaphore()

    def tell(device):
        pl.semaphore_signal(barrier, inc=1, device_id=device, device_id_type=MESH)

    def step(k, carry):
        tell(me.peer(k))
        return carry

    lax.fori_loop(1, WAYS, step, 0)
    for k in range(1, 8):
        tell(me.at(dy=k))
    for device in outer:
        tell(device)
    return lambda: pl.semaphore_wait(barrier, WAYS - 1 + 7 + len(outer))


def remote(src, dst, sems, index, device):
    return pltpu.make_async_remote_copy(
        src_ref=src, dst_ref=dst, send_sem=sems[0].at[index], recv_sem=sems[1].at[index],
        device_id=device, device_id_type=MESH,
    )


def settle(ref, sem):
    pltpu.make_async_copy(ref, ref, sem).wait()


def each_peer(act, first=0, last=16):
    def step(i, carry):
        act(16 - i)
        act(16 + i)
        return carry

    if first == 0:
        act(16)
    lax.fori_loop(max(first, 1), last, step, 0)


def pack_in(d, video, cot, out):
    base = lax.min(lax.div(d * SPOTS, 16) * 16, 256)
    base = pl.multiple_of(base, 16)
    pieces = [
        ref[0, f, pl.ds(base, 32), c * 128 : (c + 1) * 128]
        for ref in (video, cot) for c in range(3) for f in range(2)
    ]
    shift = d * SPOTS - base

    def column(r):
        block = jnp.where(r < 64, fifth(r), (r - 64) >> 2)
        spot = jnp.where(r < 64, r - fifth(r) * 5, 5 + (r & 3))
        return block * 32 + spot + shift

    pick = picks(column, PIECE, 384)
    out[d] = mm(pick, jnp.concatenate(pieces, 0)).astype(BF16)


def pack_weights(tm, conv, qkv, out_w, gain, shard):
    row, col = iotas(SHARE, C)
    own = col == tm * SHARE + row
    line = mm(gain[...], jnp.where(own, 1.0, 0.0).astype(BF16))
    diagonal = jnp.where(own, line, 0.0).astype(BF16)
    mats = [conv[0], conv[1], conv[2], qkv[:, 0:C], qkv[:, C : 2 * C], qkv[:, 2 * C : 3 * C], out_w[...], diagonal]
    for h in range(2):
        total = 0.0
        for j in range(4):
            total = total + mm(picks(lambda r: r - j * SHARE, QUAD, SHARE), mats[4 * h + j])
        shard[h] = total.astype(BF16)


def unpack_in(part, landed, x, cot):
    (start, rows), spots = CUTS[part], PARTS[part][1]
    for a, ref in ((0, x), (1, cot)):
        for c in range(3):
            first = (a * 3 + c) * 2 * spots
            base = min(first // 16 * 16, rows - 32)

            def column(r):
                return ((r & 15) >> 1) * 32 + (r & 1) * spots + (r >> 4) + (first - base)

            pick = picks(column, spots * 16, 256)
            for g in range(4):
                source = landed[8 * g : 8 * g + 8, start + base : start + base + 32, :]
                got = mm(pick, source.reshape(256, 128)).astype(BF16)
                for p in range(spots):
                    row = p * FRAMES + 16 * g
                    ref[row : row + 16, c * 128 : (c + 1) * 128] = got[16 * p : 16 * p + 16]


def unpack_weights(weights, w, gain):
    for j in range(4):
        base, size = ((0, 16), (0, 32), (16, 32), (32, 16))[j]

        def column(r):
            block = twelfth(r)
            return ((block & 3) * 8 + (block >> 2)) * size + (r - block * SHARE) + j * SHARE - base

        pick = picks(column, C, WAYS * size)
        for h in range(2):
            m = 4 * h + j
            source = weights[h, :, :, base : base + size, :].reshape(WAYS * size, C)
            got = mm(pick, source)
            if m < MATS:
                w[:, m * C : (m + 1) * C] = got.astype(BF16)
            else:
                gain[...] = jnp.sum(got, axis=0, keepdims=True)


def pack_out(part, gv, out):
    spots = PARTS[part][1]

    def column(r):
        inner = r & 31
        block = fifth(inner) if spots == 5 else inner >> 2
        spot = inner - block * spots
        return (block >> 1) * (16 * spots) + spot * 16 + (r >> 5) * 2 + (block & 1)

    pick = picks(column, 256, 48 * spots)
    for g in range(4):
        pieces = [
            gv[p * FRAMES + 16 * g : p * FRAMES + 16 * g + 16, c * 128 : (c + 1) * 128]
            for c in range(3) for p in range(spots)
        ]
        got = mm(pick, jnp.concatenate(pieces, 0)).astype(BF16)
        out[8 * g : 8 * g + 8, 32 * part : 32 * part + 32, :] = got.reshape(8, 32, 128)


def unpack_out(landed, grad_video):
    for f in range(2):
        for c in range(3):

            def column(r):
                spot = r - ninth(r) * SPOTS
                inner = jnp.where(spot < 5, c * 10 + f * 5 + spot, 32 + c * 8 + f * 4 + spot - 5)
                return ninth(r) * BACK + inner

            pick = picks(column, 144, 16 * BACK)
            for h in range(2):
                source = landed[16 * h : 16 * h + 16].reshape(16 * BACK, 128)
                got = mm(pick, source).astype(BF16)
                grad_video[0, f, 144 * h : 144 * h + 144, c * 128 : (c + 1) * 128] = got


def gather_weights(me, shard, weights, z_sems, y_sems, x_sems, c_sems):
    half = lax.rem(me.y, 2)
    begun = []

    def go(copy):
        copy.start()
        begun.append(copy)
        return copy

    def block(dz, *rows):
        return weights.at[half, me.rail, wrap(me.z + dz, 8), *rows]

    def over_z():
        for k in (2, 6, 1, 7):
            go(remote(shard.at[half], block(0), z_sems, k, me.at(dz=k)))
        weights[half, me.rail, me.z] = shard[half]

    def onward():
        for copy in begun[:2]:
            copy.wait_recv()
        top, low = pl.ds(0, 32), pl.ds(32, 16)
        go(remote(block(6, top), block(6, top), z_sems, 4, me.at(dz=2)))
        go(remote(block(2, low), block(2, low), z_sems, 0, me.at(dz=6)))
        go(remote(block(6), block(6), z_sems, 3, me.at(dz=1)))
        go(remote(block(2), block(2), z_sems, 5, me.at(dz=7)))

    beyond = (1 - me.low) * 2 + me.core
    ways = ((0, 1, 1), (1, 7, 3))
    ys, xs, cs = [], [], []

    def part(h, rail, i):
        return weights.at[h, rail, pl.ds(4 * i, 4)]

    def over_x(h, n, i, step):
        mine = part(h, me.rail, i)
        xs.append(go(remote(mine, mine, x_sems, n, me.at(dx=step))))
        cs.append(go(remote(mine, mine, c_sems, n, me.at(other=True))))

    def own_half():
        for copy in list(begun[2:]):
            copy.wait_recv()
        for i, up, _ in ways:
            mine = part(half, me.rail, i)
            ys.append(go(remote(mine, mine, y_sems, i, me.at(dy=up))))
        for i, _, side in ways:
            over_x(half, i, i, side)

    def other_half():
        for i, _, side in ways:
            ys[i].wait_recv()
            over_x(1 - half, 2 + i, i, side)

    def far_rail():
        for n in range(4):
            xs[n].wait_recv()
            mine = part(half if n < 2 else 1 - half, beyond, n % 2)
            cs.append(go(remote(mine, mine, c_sems, 4 + n, me.at(other=True))))

    def done():
        for copy in cs:
            copy.wait_recv()

    def drain():
        for copy in begun:
            copy.wait_send()

    return (over_z, onward, own_half, other_half, far_rail, done), drain


class Sums:
    def __init__(self, me, sums, core_in, held, mid, x_in, z_in, y_in, y_out, totals, sems):
        self.__dict__.update(locals())
        self.round = lax.rem(me.x + me.core, 2)
        self.mine = lax.div(me.x, 2)

    def to_core(self, r, i):
        slot = (self.me.core if r else 1 - self.me.core) + 2 * i
        return remote(
            self.sums.at[r, slot], self.core_in.at[r, i], self.sems["c"], 2 * r + i,
            self.me.at(other=True),
        )

    def to_mid(self, r, i):
        part = self.held.at[r, 1 - self.mine, pl.ds(i * HALF, HALF)]
        return remote(part, self.mid.at[i], self.sems["m"], 2 * r + i, self.me.at(dx=3 if i else 1))

    def to_owner(self, r, i):
        step = 3 if i else 1
        which = upper(wrap(self.me.x + step, 4))
        copy = remote(
            self.held.at[r, which], self.x_in.at[i], self.sems["x"], 2 * r + i, self.me.at(dx=step)
        )
        return which, copy

    def over_z(self, k):
        first = pl.multiple_of(wrap(self.me.z + k, 8) * QUAD, QUAD)
        part = self.held.at[self.round, self.mine, pl.ds(first, QUAD)]
        return remote(part, self.z_in.at[k], self.sems["z"], 0, self.me.at(dz=k))

    def over_y(self, k):
        mine = self.y_in.at[self.me.y]
        return remote(mine, mine, self.sems["y"], 0, self.me.at(dy=k))

    def over_row(self, k):
        dx, other = ((2, False), (2, True), (1, False), (3, False), (1, True), (3, True), (0, True))[k]
        own = self.round * 4 + self.me.x
        return remote(
            self.y_out, self.totals.at[own], self.sems["f"], 0, self.me.at(dx=dx, other=other)
        )

    def when_owner(self, r, act):
        pl.when(self.round == r)(act)

    def core_send(self, r):
        for i in range(2):
            self.to_core(r, i).start()

    def core_add(self, r):
        for i in range(2):
            self.to_core(r, i).wait_recv()
            slot = (1 - self.me.core if r else self.me.core) + 2 * i
            both = self.sums[r, slot].astype(F32) + self.core_in[r, i].astype(F32)
            self.held[r, i] = both.astype(BF16)

        def act():
            for i in range(2):
                self.to_mid(r, i).start()

        self.when_owner(r, act)

    def relay(self, r):
        def act():
            for i in range(2):
                self.to_mid(r, i).wait_recv()
                which, copy = self.to_owner(r, i)
                rows = pl.ds(i * HALF, HALF)
                both = self.held[r, which, rows, :].astype(F32) + self.mid[i].astype(F32)
                self.held[r, which, rows, :] = both.astype(BF16)
                copy.start()

        self.when_owner(1 - r, act)

    def own_x(self, r):
        def act():
            total = self.held[r, self.mine].astype(F32)
            for i in range(2):
                self.to_owner(r, i)[1].wait_recv()
                total = total + self.x_in[i].astype(F32)
            self.held[r, self.mine] = total.astype(BF16)
            for k in FAR_FIRST:
                self.over_z(k).start()

        self.when_owner(r, act)

    def own_z(self):
        here = pl.ds(pl.multiple_of(self.me.z * QUAD, QUAD), QUAD)
        total = self.held[self.round, self.mine, here, :].astype(F32)
        settle(self.z_in.at[pl.ds(1, 7)], self.sems["z"][1].at[0])
        for k in range(1, 8):
            total = total + self.z_in[k].astype(F32)
        self.y_in[self.me.y] = total.astype(BF16)
        for k in FAR_FIRST:
            self.over_y(k).start()

    def own_y(self):
        settle(self.y_in.at[pl.ds(1, 7)], self.sems["y"][1].at[0])
        total = self.y_in[0].astype(F32)
        for k in range(1, 8):
            total = total + self.y_in[k].astype(F32)
        self.y_out[...] = total.astype(BF16)
        for k in range(7):
            self.over_row(k).start()
        self.totals[self.round * 4 + self.me.x] = self.y_out[...]

    def drain(self):
        for sem in (*self.sems["f"], self.sems["z"][0], self.sems["y"][0]):
            settle(self.z_in.at[pl.ds(1, 7)], sem.at[0])
        for r in range(2):
            for i in range(2):
                self.to_core(r, i).wait_send()

            def owner(r=r):
                for i in range(2):
                    self.to_mid(r, i).wait_send()

            def other(r=r):
                for i in range(2):
                    self.to_owner(r, i)[1].wait_send()

            self.when_owner(r, owner)
            self.when_owner(1 - r, other)


def main_kernel(
    video_in, cot_in, conv_in, qkv_in, out_in, gain_in, grad_video, totals,
    video, cotangent, conv, qkv, out_w, parcels, shard, landed, weights,
    w, gain, parcels_out, landed_out, acc, gain_acc,
    x, cot, s1, s2, hidden, inverse, normed, packed, attended, grad_att, grad_packed,
    grad_hidden, a1, a2, gv,
    sums, core_in, held, mid, x_in, z_in, y_in, y_out,
    l_s, i_s, i_r, o_s, o_r, wz_s, wz_r, wy_s, wy_r, wx_s, wx_r, wc_s, wc_r,
    sc_s, sc_r, sm_s, sm_r, sx_s, sx_r, sz_s, sz_r, sy_s, sy_r, sf_s, sf_r,
):
    me = Place()
    pairs = (
        (conv_in, conv), (qkv_in, qkv), (out_in, out_w), (video_in, video), (cot_in, cotangent)
    )
    reads = [pltpu.make_async_copy(src, dst, l_s.at[n]) for n, (src, dst) in enumerate(pairs)]
    for copy in reads:
        copy.start()
    outer = jnp.where(me.low == 0, 3, 1)
    met = greet(me, [me.at(dx=dx, other=o) for dx in (2, outer) for o in (False, True)])
    for copy in reads[:3]:
        copy.wait()
    pack_weights(me.tm, conv, qkv, out_w, gain_in, shard)
    for copy in reads[3:]:
        copy.wait()
    met()

    steps, drain = gather_weights(
        me, shard, weights, (wz_s, wz_r), (wy_s, wy_r), (wx_s, wx_r), (wc_s, wc_r)
    )
    steps[0]()

    def coming(part, k):
        device, rows = me.peer(k), pl.ds(*CUTS[part])
        return remote(
            parcels.at[device[1], rows], landed.at[me.tm, rows], (i_s, i_r), part, device
        )

    def going(part, k):
        device, rows = me.peer(k), pl.ds(32 * part, 32)
        return remote(
            parcels_out.at[device[1], rows], landed_out.at[me.tm, rows], (o_s, o_r), part, device
        )

    def arrive(part, sems):
        settle(landed.at[pl.ds(0, WAYS - 1), pl.ds(*CUTS[part])], sems.at[part])

    def returned(part, sems):
        settle(landed_out.at[pl.ds(0, WAYS - 1), pl.ds(32 * part, 32)], sems.at[part])

    def two(i, carry):
        for k in (16 - i, 16 + i):
            pack_in(me.peer(k)[1], video, cotangent, parcels)
        for k in (16 - i, 16 + i):
            coming(0, k).start()
        return carry

    pack_in(me.peer(16)[1], video, cotangent, parcels)
    coming(0, 16).start()
    lax.fori_loop(1, 4, two, 0)
    steps[1]()
    lax.fori_loop(4, 7, two, 0)
    steps[2]()
    lax.fori_loop(7, 12, two, 0)
    steps[3]()
    lax.fori_loop(12, 16, two, 0)
    pack_in(me.tm, video, cotangent, landed)
    steps[4]()
    each_peer(lambda k: coming(1, k).start())
    steps[5]()
    unpack_weights(weights, w, gain)

    total = Sums(
        me, sums, core_in, held, mid, x_in, z_in, y_in, y_out, totals,
        dict(
            c=(sc_s, sc_r), m=(sm_s, sm_r), x=(sx_s, sx_r), z=(sz_s, sz_r), y=(sy_s, sy_r),
            f=(sf_s, sf_r),
        ),
    )
    tall = (
        x, cot, s1, s2, hidden, inverse, normed, packed, attended, grad_att, grad_packed,
        grad_hidden, a1, a2, gv,
    )
    for part, (first, spots) in enumerate(PARTS):
        rows = pl.ds(first * FRAMES, spots * FRAMES)
        (
            px, pcot, ps1, ps2, phidden, pinverse, pnormed, ppacked, pattended, pgrad_att,
            pgrad_packed, pgrad_hidden, pa1, pa2, pgv,
        ) = (ref.at[rows] for ref in tall)
        blocks = BLOCKS[part]
        arrive(part, i_r)
        unpack_in(part, landed, px, pcot)
        forward(blocks, w, gain, px, ps1, ps2, phidden, pinverse, pnormed, ppacked)
        attention(blocks, w, pcot, ppacked, pattended, pgrad_att, pgrad_packed)

        def add(n, product):
            if part == 0:
                acc[n] = product
            else:
                sums[n // 4, n % 4] = (acc[n] + product).astype(BF16)

        def early_sums():
            add(0, mm_tn(pattended[...], pcot[...]))
            product = mm_tn(pnormed[...], pgrad_packed[...])
            for i in range(3):
                add(1 + i, product[:, i * C : (i + 1) * C])

        def late_sums():
            for tap, ref in enumerate((px, ps1, ps2)):
                add(4 + tap, mm_tn(ref[...], pgrad_hidden[...]))

        def send_back():
            pack_out(part, pgv, parcels_out)
            landed_out[me.tm, 32 * part : 32 * part + 32, :] = (
                parcels_out[me.tm, 32 * part : 32 * part + 32, :]
            )

        def norm_back():
            return normalize_back(w, gain, pcot, phidden, pinverse, pgrad_packed, pgrad_hidden)

        if part == 0:
            gain_acc[...] = norm_back()
            conv_back(blocks, w, pgrad_hidden, pa1, pa2, pgv)
            send_back()
            each_peer(lambda k: going(0, k).start())
            early_sums()
            late_sums()
        else:
            early_sums()
            total.core_send(0)
            gain_sum = gain_acc[...] + norm_back()
            row, col = iotas(C, C)
            sums[1, 3] = jnp.where(row == col, gain_sum, 0.0).astype(BF16)
            late_sums()
            total.core_send(1)
            total.core_add(0)
            conv_back(blocks, w, pgrad_hidden, pa1, pa2, pgv)
            total.core_add(1)
            total.relay(0)
            send_back()
    total.relay(1)
    total.own_x(0)
    total.own_x(1)
    each_peer(lambda k: going(1, k).start(), 0, 8)
    total.own_z()
    each_peer(lambda k: going(1, k).start(), 8, 16)
    total.own_y()
    for part in range(2):
        returned(part, o_r)
    unpack_out(landed_out, grad_video)
    total.drain()
    drain()
    for part in range(2):
        arrive(part, i_s)
        returned(part, o_s)


def call(kernel, outs, scratch, places, out_places, mib, collective=None):
    extra = {} if collective is None else dict(collective_id=collective, has_side_effects=True)
    return pl.pallas_call(
        kernel,
        out_shape=[jax.ShapeDtypeStruct(*o) for o in outs],
        in_specs=[pl.BlockSpec(memory_space=place) for place in places],
        out_specs=[pl.BlockSpec(memory_space=place) for place in out_places],
        scratch_shapes=scratch,
        compiler_params=pltpu.CompilerParams(vmem_limit_bytes=mib * 1024 * 1024, **extra),
    )


def main(*args):
    def held(*shape, kind=BF16):
        return pltpu.VMEM(shape, kind)

    tall = held(ROWS, C)
    scratch = [
        held(1, 2, 288, C), held(1, 2, 288, C), held(3, SHARE, C), held(SHARE, 3 * C), held(SHARE, C),
        held(WAYS, PIECE, 128), held(2, QUAD, C), held(WAYS, PIECE, 128), held(2, 4, 8, QUAD, C),
        held(C, WIDE), held(1, C, kind=F32), held(WAYS, BACK, 128), held(WAYS, BACK, 128), held(MATS, C, C, kind=F32),
        held(1, C, kind=F32),
        tall, tall, tall, tall, tall, held(ROWS, 1, kind=F32), tall, held(ROWS, 3 * C), tall, tall,
        held(ROWS, 3 * C), tall, tall, tall, tall,
        held(2, 4, C, C), held(2, 2, C, C), held(2, 2, C, C), held(2, HALF, C), held(2, C, C),
        held(8, QUAD, C), held(8, QUAD, C), held(QUAD, C),
    ]
    counts = [5] + [2] * 4 + [8, 8, 2, 2, 4, 4, 8, 8] + [4] * 6 + [1] * 6
    scratch += [pltpu.SemaphoreType.DMA((n,)) for n in counts]
    outs = [(args[0].shape, BF16), ((8, QUAD, C), BF16)]
    places = [pl.ANY] * 5 + [pltpu.VMEM]
    return call(main_kernel, outs, scratch, places, [pltpu.VMEM] * 2, 56, 1)(*args)


def finish_kernel(
    factor, grad_in, totals_in, grad_video, conv, qkv, out_w, gain, grad, totals, sems
):
    come = pltpu.make_async_copy(grad_in, grad, sems.at[0])
    come.start()
    read = pltpu.make_async_copy(totals_in, totals, sems.at[1])
    read.start()
    come.wait()
    go = pltpu.make_async_copy(grad, grad_video, sems.at[2])
    go.start()
    read.wait()
    tm = lax.axis_index("tm")
    pick = picks(lambda r: r + lax.rem(tm, 4) * SHARE, 16, QUAD)
    got = [mm(pick, totals[m]) for m in range(8)]
    for i in range(3):
        conv[i] = got[4 + i][0:SHARE] * factor
        qkv[:, i * C : (i + 1) * C] = got[1 + i][0:SHARE] * factor
    out_w[...] = got[0][0:SHARE] * factor
    row, col = iotas(C, SHARE)
    line = mm(got[7].astype(BF16), jnp.where(row == tm * SHARE + col, 1.0, 0.0).astype(BF16))
    row, col = iotas(16, SHARE)
    gain[...] = jnp.sum(jnp.where(row == col, line, 0.0), axis=0, keepdims=True) * factor
    go.wait()


def body(video, conv_w, qkv_w, out_w, gain, cotangent):
    grad_video, totals = main(video, cotangent, conv_w, qkv_w, out_w, gain.reshape(1, SHARE))
    factor = 1.0 / math.sqrt(
        lax.axis_size("clip") * lax.axis_size("tm") * video.shape[1] * video.shape[2]
    )
    outs = [
        (video.shape, BF16), (conv_w.shape, F32), (qkv_w.shape, F32), (out_w.shape, F32),
        ((1, SHARE), F32),
    ]
    got = call(
        functools.partial(finish_kernel, factor), outs,
        [
            pltpu.VMEM(video.shape, BF16), pltpu.VMEM((8, QUAD, C), BF16),
            pltpu.SemaphoreType.DMA((3,)),
        ],
        [pl.ANY] * 2, [pl.ANY] + [pltpu.VMEM] * 4, 56,
    )(grad_video, totals)
    return (*got[:4], got[4].reshape(SHARE))


def solution(mesh):
    in_specs = (
        P("clip", "tm", None, None),
        P(None, "tm", None),
        P("tm", None),
        P("tm", None),
        P("tm"),
        P("clip", "tm", None, None),
    )
    out_specs = (
        P("clip", "tm", None, None),
        P(None, "tm", None),
        P("tm", None),
        P("tm", None),
        P("tm"),
    )
    return jax.shard_map(body, mesh=mesh, in_specs=in_specs, out_specs=out_specs, check_vma=False)
```

```python
import functools
import math

import jax
import jax.numpy as jnp
from jax import lax
from jax.experimental import pallas as pl
from jax.experimental.pallas import tpu as pltpu
from jax.sharding import PartitionSpec as P

epsilon = 1e-06
F32 = jnp.float32
BF16 = jnp.bfloat16

C = 384
FRAMES = 64
SPOTS = 9
ROWS = SPOTS * FRAMES
PARTS = ((0, 5), (5, 4))
BLOCKS = (((0, 192), (192, 128)), ((0, 128), (128, 128)))
MATS = 7
WIDE = MATS * C


def mm(a, b):
    return lax.dot_general(a, b, (((1,), (0,)), ((), ())), preferred_element_type=F32)


def mm_nt(a, b):
    return lax.dot_general(a, b, (((1,), (1,)), ((), ())), preferred_element_type=F32)


def mm_tn(a, b):
    return lax.dot_general(a, b, (((0,), (0,)), ((), ())), preferred_element_type=F32)


def iotas(rows, columns):
    shape = (rows, columns)
    return lax.broadcasted_iota(jnp.int32, shape, 0), lax.broadcasted_iota(jnp.int32, shape, 1)


def delay_matrix(size, steps):
    row, col = iotas(size, size)
    return jnp.where((row - col == steps) & ((row & (FRAMES - 1)) >= steps), 1.0, 0.0).astype(BF16)


def forward(blocks, w, gain, x, s1, s2, hidden, inverse, normed, packed):
    for steps, ref in ((1, s1), (2, s2)):
        for first, size in blocks:
            rows = pl.ds(first, size)
            ref[rows, :] = mm(delay_matrix(size, steps), x[rows, :]).astype(BF16)
    mixed = mm(x[...], w[:, 0:C]) + mm(s1[...], w[:, C : 2 * C]) + mm(s2[...], w[:, 2 * C : 3 * C])
    hidden[...] = (x[...].astype(F32) + mixed).astype(BF16)
    wide = hidden[...].astype(F32)
    inverse[...] = lax.rsqrt(jnp.mean(wide * wide, axis=-1, keepdims=True) + epsilon)
    normed[...] = (wide * inverse[...] * gain[...]).astype(BF16)
    packed[...] = mm(normed[...], w[:, 3 * C : 6 * C]).astype(BF16)


def seen(size):
    row, col = iotas(size, size)
    return ((row >> 6) == (col >> 6)) & (col <= row)


def attention(blocks, w, cot, packed, attended, grad_att, grad_packed):
    factor = 1.0 / math.sqrt(C)
    grad_att[...] = mm_nt(cot[...], w[:, 6 * C : 7 * C]).astype(BF16)
    for first, size in blocks:
        part = pl.ds(first, size)
        query, keys, values = (packed[part, i * C : (i + 1) * C] for i in range(3))
        scores = jnp.where(seen(size), mm_nt(query, keys) * factor, -1e30)
        raised = jnp.exp(scores - jnp.max(scores, axis=-1, keepdims=True))
        probs = raised / jnp.sum(raised, axis=-1, keepdims=True)
        rounded = probs.astype(BF16)
        attended[part, :] = mm(rounded, values).astype(BF16)
        incoming = grad_att[part, :]
        dprob = mm_nt(incoming, values)
        dscore = probs * (dprob - jnp.sum(dprob * probs, axis=-1, keepdims=True))
        dscore = (dscore * factor).astype(BF16)
        grad_packed[part, 0:C] = mm(dscore, keys).astype(BF16)
        grad_packed[part, C : 2 * C] = mm_tn(dscore, query).astype(BF16)
        grad_packed[part, 2 * C : 3 * C] = mm_tn(rounded, incoming).astype(BF16)


def normalize_back(w, gain, cot, hidden, inverse, grad_packed, grad_hidden):
    grad_norm = mm_nt(grad_packed[...], w[:, 3 * C : 6 * C]).astype(BF16).astype(F32)
    wide = hidden[...].astype(F32)
    inv = inverse[...]
    scaled = grad_norm * gain[...]
    inner = jnp.mean(scaled * wide, axis=-1, keepdims=True)
    back = cot[...].astype(F32) + inv * scaled - wide * (inv * inv * inv * inner)
    grad_hidden[...] = back.astype(BF16)
    return jnp.sum(grad_norm * wide * inv, axis=0, keepdims=True)


def conv_back(blocks, w, grad_hidden, a1, a2, gv):
    for steps, ref in ((1, a1), (2, a2)):
        for first, size in blocks:
            rows = pl.ds(first, size)
            ref[rows, :] = mm_tn(delay_matrix(size, steps), grad_hidden[rows, :]).astype(BF16)
    grad = grad_hidden[...].astype(F32) + mm_nt(grad_hidden[...], w[:, 0:C])
    grad = grad + mm_nt(a1[...], w[:, C : 2 * C]) + mm_nt(a2[...], w[:, 2 * C : 3 * C])
    gv[...] = grad.astype(BF16)


WAYS = 32
PIECE = 112
CUTS = ((0, 64), (64, 48))
BACK = 64
SHARE = 12
QUAD = 4 * SHARE
HALF = C // 2
MESH = pl.DeviceIdType.MESH
FAR_FIRST = (4, 3, 5, 2, 6, 1, 7)


def ninth(n):
    return (n * 57) >> 9


def fifth(n):
    return (n * 205) >> 10


def twelfth(n):
    return (n * 1366) >> 14


def picks(target, rows, columns):
    width = min(columns, 128)
    row, col = iotas(rows, width)
    lane = target(row) - col
    parts = [
        jnp.where(lane == first, 1.0, 0.0).astype(BF16)
        for first in range(0, columns // width * width, width)
    ]
    rest = columns - columns // width * width
    if rest:
        last = lane[:, 0:rest] == columns - rest
        parts.append(jnp.where(last, 1.0, 0.0).astype(BF16))
    return parts[0] if len(parts) == 1 else jnp.concatenate(parts, 1)


def wrap(n, size):
    return jnp.where(n >= size, n - size, n)


def upper(x):
    return jnp.where(x >= 2, 1, 0)


class Place:
    def __init__(self):
        self.clip, self.tm = lax.axis_index("clip"), lax.axis_index("tm")
        self.y, self.z = lax.rem(self.clip, 8), lax.div(self.tm, 4)
        self.low = lax.rem(lax.div(self.tm, 2), 2)
        self.x = lax.div(self.clip, 8) * 2 + self.low
        self.core = lax.rem(self.tm, 2)
        self.rail = self.low * 2 + self.core

    def at(self, dx=0, dy=0, dz=0, other=False):
        x, y, z = wrap(self.x + dx, 4), wrap(self.y + dy, 8), wrap(self.z + dz, 8)
        core = 1 - self.core if other else self.core
        return (upper(x) * 8 + y, z * 4 + (x - upper(x) * 2) * 2 + core)

    def peer(self, k):
        return (self.clip, wrap(self.tm + k, WAYS))


def greet(me, outer):
    barrier = pltpu.get_barrier_semaphore()

    def tell(device):
        pl.semaphore_signal(barrier, inc=1, device_id=device, device_id_type=MESH)

    def step(k, carry):
        tell(me.peer(k))
        return carry

    lax.fori_loop(1, WAYS, step, 0)
    for k in range(1, 8):
        tell(me.at(dy=k))
    for device in outer:
        tell(device)
    return lambda: pl.semaphore_wait(barrier, WAYS - 1 + 7 + len(outer))


def remote(src, dst, sems, index, device):
    return pltpu.make_async_remote_copy(
        src_ref=src, dst_ref=dst, send_sem=sems[0].at[index], recv_sem=sems[1].at[index],
        device_id=device, device_id_type=MESH,
    )


def settle(ref, sem):
    pltpu.make_async_copy(ref, ref, sem).wait()


def each_peer(act, first=0, last=16):
    def step(i, carry):
        act(16 - i)
        act(16 + i)
        return carry

    if first == 0:
        act(16)
    lax.fori_loop(max(first, 1), last, step, 0)


def pack_in(d, video, cot, out):
    base = lax.min(lax.div(d * SPOTS, 16) * 16, 256)
    base = pl.multiple_of(base, 16)
    pieces = [
        ref[0, f, pl.ds(base, 32), c * 128 : (c + 1) * 128]
        for ref in (video, cot) for c in range(3) for f in range(2)
    ]
    shift = d * SPOTS - base

    def column(r):
        block = jnp.where(r < 64, fifth(r), (r - 64) >> 2)
        spot = jnp.where(r < 64, r - fifth(r) * 5, 5 + (r & 3))
        return block * 32 + spot + shift

    pick = picks(column, PIECE, 384)
    out[...] = mm(pick, jnp.concatenate(pieces, 0)).astype(BF16)


def pack_weights(tm, conv, qkv, out_w, gain, shard):
    row, col = iotas(SHARE, C)
    own = col == tm * SHARE + row
    line = mm(gain[...], jnp.where(own, 1.0, 0.0).astype(BF16))
    diagonal = jnp.where(own, line, 0.0).astype(BF16)
    mats = [conv[0], conv[1], conv[2], qkv[:, 0:C], qkv[:, C : 2 * C], qkv[:, 2 * C : 3 * C], out_w[...], diagonal]
    for h in range(2):
        total = 0.0
        for j in range(4):
            total = total + mm(picks(lambda r: r - j * SHARE, QUAD, SHARE), mats[4 * h + j])
        shard[h] = total.astype(BF16)


def unpack_in(part, landed, x, cot):
    (start, rows), spots = CUTS[part], PARTS[part][1]
    for a, ref in ((0, x), (1, cot)):
        for c in range(3):
            first = (a * 3 + c) * 2 * spots
            base = min(first // 16 * 16, rows - 32)

            def column(r):
                return ((r & 15) >> 1) * 32 + (r & 1) * spots + (r >> 4) + (first - base)

            pick = picks(column, spots * 16, 256)
            for g in range(4):
                source = landed[8 * g : 8 * g + 8, start + base : start + base + 32, :]
                got = mm(pick, source.reshape(256, 128)).astype(BF16)
                for p in range(spots):
                    row = p * FRAMES + 16 * g
                    ref[row : row + 16, c * 128 : (c + 1) * 128] = got[16 * p : 16 * p + 16]


def unpack_weights(weights, w, gain):
    for j in range(4):
        base, size = ((0, 16), (0, 32), (16, 32), (32, 16))[j]

        def column(r):
            block = twelfth(r)
            return ((block & 3) * 8 + (block >> 2)) * size + (r - block * SHARE) + j * SHARE - base

        pick = picks(column, C, WAYS * size)
        for h in range(2):
            m = 4 * h + j
            source = weights[h, :, :, base : base + size, :].reshape(WAYS * size, C)
            got = mm(pick, source)
            if m < MATS:
                w[:, m * C : (m + 1) * C] = got.astype(BF16)
            else:
                gain[...] = jnp.sum(got, axis=0, keepdims=True)


def pack_out(part, gv, out):
    spots = PARTS[part][1]

    def column(r):
        inner = r & 31
        block = fifth(inner) if spots == 5 else inner >> 2
        spot = inner - block * spots
        return (block >> 1) * (16 * spots) + spot * 16 + (r >> 5) * 2 + (block & 1)

    pick = picks(column, 256, 48 * spots)
    for g in range(4):
        pieces = [
            gv[p * FRAMES + 16 * g : p * FRAMES + 16 * g + 16, c * 128 : (c + 1) * 128]
            for c in range(3) for p in range(spots)
        ]
        got = mm(pick, jnp.concatenate(pieces, 0)).astype(BF16)
        out[8 * g : 8 * g + 8, 32 * part : 32 * part + 32, :] = got.reshape(8, 32, 128)


def unpack_out(landed, grad_video):
    for f in range(2):
        for c in range(3):

            def column(r):
                spot = r - ninth(r) * SPOTS
                inner = jnp.where(spot < 5, c * 10 + f * 5 + spot, 32 + c * 8 + f * 4 + spot - 5)
                return ninth(r) * BACK + inner

            pick = picks(column, 144, 16 * BACK)
            for h in range(2):
                source = landed[16 * h : 16 * h + 16].reshape(16 * BACK, 128)
                got = mm(pick, source).astype(BF16)
                grad_video[0, f, 144 * h : 144 * h + 144, c * 128 : (c + 1) * 128] = got


def gather_weights(me, shard, weights, z_sems, y_sems, x_sems, c_sems):
    half = lax.rem(me.y, 2)
    begun = []

    def go(copy):
        copy.start()
        begun.append(copy)
        return copy

    def block(dz, *rows):
        return weights.at[half, me.rail, wrap(me.z + dz, 8), *rows]

    def over_z():
        for k in (2, 6, 1, 7):
            go(remote(shard.at[half], block(0), z_sems, k, me.at(dz=k)))
        weights[half, me.rail, me.z] = shard[half]

    def onward():
        for copy in begun[:2]:
            copy.wait_recv()
        top, low = pl.ds(0, 32), pl.ds(32, 16)
        go(remote(block(6, top), block(6, top), z_sems, 4, me.at(dz=2)))
        go(remote(block(2, low), block(2, low), z_sems, 0, me.at(dz=6)))
        go(remote(block(6), block(6), z_sems, 3, me.at(dz=1)))
        go(remote(block(2), block(2), z_sems, 5, me.at(dz=7)))

    beyond = (1 - me.low) * 2 + me.core
    ways = ((0, 1, 1), (1, 7, 3))
    ys, xs, cs = [], [], []

    def part(h, rail, i):
        return weights.at[h, rail, pl.ds(4 * i, 4)]

    def over_x(h, n, i, step):
        mine = part(h, me.rail, i)
        xs.append(go(remote(mine, mine, x_sems, n, me.at(dx=step))))
        cs.append(go(remote(mine, mine, c_sems, n, me.at(other=True))))

    def own_half():
        for copy in list(begun[2:]):
            copy.wait_recv()
        for i, up, _ in ways:
            mine = part(half, me.rail, i)
            ys.append(go(remote(mine, mine, y_sems, i, me.at(dy=up))))
        for i, _, side in ways:
            over_x(half, i, i, side)

    def other_half():
        for i, _, side in ways:
            ys[i].wait_recv()
            over_x(1 - half, 2 + i, i, side)

    def far_rail():
        for n in range(4):
            xs[n].wait_recv()
            mine = part(half if n < 2 else 1 - half, beyond, n % 2)
            cs.append(go(remote(mine, mine, c_sems, 4 + n, me.at(other=True))))

    def done():
        for copy in cs:
            copy.wait_recv()

    def drain():
        for copy in begun:
            copy.wait_send()

    return (over_z, onward, own_half, other_half, far_rail, done), drain


class Sums:
    def __init__(self, me, sums, core_in, held, mid, x_in, z_in, y_in, y_out, totals, sems):
        self.__dict__.update(locals())
        self.round = lax.rem(me.x + me.core, 2)
        self.mine = lax.div(me.x, 2)

    def to_core(self, r, i):
        slot = (self.me.core if r else 1 - self.me.core) + 2 * i
        return remote(
            self.sums.at[r, slot], self.core_in.at[r, i], self.sems["c"], 2 * r + i,
            self.me.at(other=True),
        )

    def to_mid(self, r, i):
        part = self.held.at[r, 1 - self.mine, pl.ds(i * HALF, HALF)]
        return remote(part, self.mid.at[i], self.sems["m"], 2 * r + i, self.me.at(dx=3 if i else 1))

    def to_owner(self, r, i):
        step = 3 if i else 1
        which = upper(wrap(self.me.x + step, 4))
        copy = remote(
            self.held.at[r, which], self.x_in.at[i], self.sems["x"], 2 * r + i, self.me.at(dx=step)
        )
        return which, copy

    def over_z(self, k):
        first = pl.multiple_of(wrap(self.me.z + k, 8) * QUAD, QUAD)
        part = self.held.at[self.round, self.mine, pl.ds(first, QUAD)]
        return remote(part, self.z_in.at[k], self.sems["z"], 0, self.me.at(dz=k))

    def over_y(self, k):
        mine = self.y_in.at[self.me.y]
        return remote(mine, mine, self.sems["y"], 0, self.me.at(dy=k))

    def over_row(self, k):
        dx, other = ((2, False), (2, True), (1, False), (3, False), (1, True), (3, True), (0, True))[k]
        own = self.round * 4 + self.me.x
        return remote(
            self.y_out, self.totals.at[own], self.sems["f"], 0, self.me.at(dx=dx, other=other)
        )

    def when_owner(self, r, act):
        pl.when(self.round == r)(act)

    def core_send(self, r):
        for i in range(2):
            self.to_core(r, i).start()

    def core_add(self, r):
        for i in range(2):
            self.to_core(r, i).wait_recv()
            slot = (1 - self.me.core if r else self.me.core) + 2 * i
            both = self.sums[r, slot].astype(F32) + self.core_in[r, i].astype(F32)
            self.held[r, i] = both.astype(BF16)

        def act():
            for i in range(2):
                self.to_mid(r, i).start()

        self.when_owner(r, act)

    def relay(self, r):
        def act():
            for i in range(2):
                self.to_mid(r, i).wait_recv()
                which, copy = self.to_owner(r, i)
                rows = pl.ds(i * HALF, HALF)
                both = self.held[r, which, rows, :].astype(F32) + self.mid[i].astype(F32)
                self.held[r, which, rows, :] = both.astype(BF16)
                copy.start()

        self.when_owner(1 - r, act)

    def own_x(self, r):
        def act():
            total = self.held[r, self.mine].astype(F32)
            for i in range(2):
                self.to_owner(r, i)[1].wait_recv()
                total = total + self.x_in[i].astype(F32)
            self.held[r, self.mine] = total.astype(BF16)
            for k in FAR_FIRST:
                self.over_z(k).start()

        self.when_owner(r, act)

    def own_z(self):
        here = pl.ds(pl.multiple_of(self.me.z * QUAD, QUAD), QUAD)
        total = self.held[self.round, self.mine, here, :].astype(F32)
        settle(self.z_in.at[pl.ds(1, 7)], self.sems["z"][1].at[0])
        for k in range(1, 8):
            total = total + self.z_in[k].astype(F32)
        self.y_in[self.me.y] = total.astype(BF16)
        for k in FAR_FIRST:
            self.over_y(k).start()

    def own_y(self):
        settle(self.y_in.at[pl.ds(1, 7)], self.sems["y"][1].at[0])
        total = self.y_in[0].astype(F32)
        for k in range(1, 8):
            total = total + self.y_in[k].astype(F32)
        self.y_out[...] = total.astype(BF16)
        for k in range(7):
            self.over_row(k).start()
        self.totals[self.round * 4 + self.me.x] = self.y_out[...]

    def drain(self):
        for sem in (*self.sems["f"], self.sems["z"][0], self.sems["y"][0]):
            settle(self.z_in.at[pl.ds(1, 7)], sem.at[0])
        for r in range(2):
            for i in range(2):
                self.to_core(r, i).wait_send()

            def owner(r=r):
                for i in range(2):
                    self.to_mid(r, i).wait_send()

            def other(r=r):
                for i in range(2):
                    self.to_owner(r, i)[1].wait_send()

            self.when_owner(r, owner)
            self.when_owner(1 - r, other)


def main_kernel(
    video_in, cot_in, conv_in, qkv_in, out_in, gain_in, grad_video, totals,
    video, cotangent, conv, qkv, out_w, parcels, shard, landed, weights,
    w, gain, parcels_out, landed_out, acc, gain_acc,
    x, cot, s1, s2, hidden, inverse, normed, packed, attended, grad_att, grad_packed,
    grad_hidden, a1, a2, gv,
    sums, core_in, held, mid, x_in, z_in, y_in, y_out,
    l_s, v_s, v_r, i_s, i_r, o_s, o_r, wz_s, wz_r, wy_s, wy_r, wx_s, wx_r, wc_s, wc_r,
    sc_s, sc_r, sm_s, sm_r, sx_s, sx_r, sz_s, sz_r, sy_s, sy_r, sf_s, sf_r,
):
    me = Place()
    pairs = (
        (conv_in, conv), (qkv_in, qkv), (out_in, out_w), (video_in, video.at[me.core]),
        (cot_in, cotangent.at[me.core]),
    )
    reads = [pltpu.make_async_copy(src, dst, l_s.at[n]) for n, (src, dst) in enumerate(pairs)]
    for copy in reads:
        copy.start()
    outer = jnp.where(me.low == 0, 3, 1)
    met = greet(me, [me.at(dx=dx, other=o) for dx in (2, outer) for o in (False, True)])
    for copy in reads[:3]:
        copy.wait()
    pack_weights(me.tm, conv, qkv, out_w, gain_in, shard)
    for copy in reads[3:]:
        copy.wait()
    met()
    swaps = [
        remote(ref.at[me.core], ref.at[me.core], (v_s, v_r), n, me.at(other=True))
        for n, ref in enumerate((video, cotangent))
    ]
    for copy in swaps:
        copy.start()

    steps, drain = gather_weights(
        me, shard, weights, (wz_s, wz_r), (wy_s, wy_r), (wx_s, wx_r), (wc_s, wc_r)
    )
    steps[0]()

    chip = lax.div(me.tm, 2)

    def toward(k):
        there = wrap(chip + k, WAYS // 2)
        return there, 2 * there + me.core

    def coming(part, k):
        (there, target), rows = toward(k), pl.ds(*CUTS[part])
        return remote(
            parcels.at[there, pl.ds(0, 2), rows], landed.at[pl.ds(2 * chip, 2), rows],
            (i_s, i_r), part, (me.clip, target),
        )

    def going(part, k):
        device, rows = me.peer(k), pl.ds(32 * part, 32)
        return remote(
            parcels_out.at[device[1], rows], landed_out.at[me.tm, rows], (o_s, o_r), part, device
        )

    def arrive(part, sems):
        settle(landed.at[pl.ds(0, WAYS - 2), pl.ds(*CUTS[part])], sems.at[part])

    def returned(part, sems):
        settle(landed_out.at[pl.ds(0, WAYS - 1), pl.ds(32 * part, 32)], sems.at[part])

    def pack(target, place):
        for source in range(2):
            pack_in(target, video.at[source], cotangent.at[source], place(source))

    def one(k):
        there, target = toward(k)
        pack(target, lambda source: parcels.at[there, source])
        coming(0, k).start()

    def two(i, carry):
        one(8 - i)
        one(8 + i)
        return carry

    for copy in swaps:
        copy.wait_recv()
    one(8)
    lax.fori_loop(1, 2, two, 0)
    steps[1]()
    lax.fori_loop(2, 4, two, 0)
    steps[2]()
    lax.fori_loop(4, 6, two, 0)
    steps[3]()
    lax.fori_loop(6, 8, two, 0)
    pack(me.tm, lambda source: landed.at[2 * chip + source])
    steps[4]()

    def late(i, carry):
        coming(1, 8 - i).start()
        coming(1, 8 + i).start()
        return carry

    coming(1, 8).start()
    lax.fori_loop(1, 8, late, 0)
    steps[5]()
    unpack_weights(weights, w, gain)

    total = Sums(
        me, sums, core_in, held, mid, x_in, z_in, y_in, y_out, totals,
        dict(
            c=(sc_s, sc_r), m=(sm_s, sm_r), x=(sx_s, sx_r), z=(sz_s, sz_r), y=(sy_s, sy_r),
            f=(sf_s, sf_r),
        ),
    )
    tall = (
        x, cot, s1, s2, hidden, inverse, normed, packed, attended, grad_att, grad_packed,
        grad_hidden, a1, a2, gv,
    )
    for part, (first, spots) in enumerate(PARTS):
        rows = pl.ds(first * FRAMES, spots * FRAMES)
        (
            px, pcot, ps1, ps2, phidden, pinverse, pnormed, ppacked, pattended, pgrad_att,
            pgrad_packed, pgrad_hidden, pa1, pa2, pgv,
        ) = (ref.at[rows] for ref in tall)
        blocks = BLOCKS[part]
        arrive(part, i_r)
        unpack_in(part, landed, px, pcot)
        forward(blocks, w, gain, px, ps1, ps2, phidden, pinverse, pnormed, ppacked)
        attention(blocks, w, pcot, ppacked, pattended, pgrad_att, pgrad_packed)

        def add(n, product):
            if part == 0:
                acc[n] = product
            else:
                sums[n // 4, n % 4] = (acc[n] + product).astype(BF16)

        def early_sums():
            add(0, mm_tn(pattended[...], pcot[...]))
            product = mm_tn(pnormed[...], pgrad_packed[...])
            for i in range(3):
                add(1 + i, product[:, i * C : (i + 1) * C])

        def late_sums():
            for tap, ref in enumerate((px, ps1, ps2)):
                add(4 + tap, mm_tn(ref[...], pgrad_hidden[...]))

        def send_back():
            pack_out(part, pgv, parcels_out)
            landed_out[me.tm, 32 * part : 32 * part + 32, :] = (
                parcels_out[me.tm, 32 * part : 32 * part + 32, :]
            )

        def norm_back():
            return normalize_back(w, gain, pcot, phidden, pinverse, pgrad_packed, pgrad_hidden)

        if part == 0:
            gain_acc[...] = norm_back()
            conv_back(blocks, w, pgrad_hidden, pa1, pa2, pgv)
            send_back()
            each_peer(lambda k: going(0, k).start())
            early_sums()
            late_sums()
        else:
            early_sums()
            total.core_send(0)
            gain_sum = gain_acc[...] + norm_back()
            row, col = iotas(C, C)
            sums[1, 3] = jnp.where(row == col, gain_sum, 0.0).astype(BF16)
            late_sums()
            total.core_send(1)
            total.core_add(0)
            conv_back(blocks, w, pgrad_hidden, pa1, pa2, pgv)
            total.core_add(1)
            total.relay(0)
            send_back()
    total.relay(1)
    total.own_x(0)
    total.own_x(1)
    each_peer(lambda k: going(1, k).start(), 0, 8)
    total.own_z()
    each_peer(lambda k: going(1, k).start(), 8, 16)
    total.own_y()
    for part in range(2):
        returned(part, o_r)
    unpack_out(landed_out, grad_video)
    total.drain()
    drain()
    for copy in swaps:
        copy.wait_send()
    for part in range(2):
        arrive(part, i_s)
        returned(part, o_s)


def call(kernel, outs, scratch, places, out_places, mib, collective=None):
    extra = {} if collective is None else dict(collective_id=collective, has_side_effects=True)
    return pl.pallas_call(
        kernel,
        out_shape=[jax.ShapeDtypeStruct(*o) for o in outs],
        in_specs=[pl.BlockSpec(memory_space=place) for place in places],
        out_specs=[pl.BlockSpec(memory_space=place) for place in out_places],
        scratch_shapes=scratch,
        compiler_params=pltpu.CompilerParams(vmem_limit_bytes=mib * 1024 * 1024, **extra),
    )


def main(*args):
    def held(*shape, kind=BF16):
        return pltpu.VMEM(shape, kind)

    tall = held(ROWS, C)
    scratch = [
        held(2, 1, 2, 288, C), held(2, 1, 2, 288, C), held(3, SHARE, C), held(SHARE, 3 * C), held(SHARE, C),
        held(WAYS // 2, 2, PIECE, 128), held(2, QUAD, C), held(WAYS, PIECE, 128), held(2, 4, 8, QUAD, C),
        held(C, WIDE), held(1, C, kind=F32), held(WAYS, BACK, 128), held(WAYS, BACK, 128), held(MATS, C, C, kind=F32),
        held(1, C, kind=F32),
        tall, tall, tall, tall, tall, held(ROWS, 1, kind=F32), tall, held(ROWS, 3 * C), tall, tall,
        held(ROWS, 3 * C), tall, tall, tall, tall,
        held(2, 4, C, C), held(2, 2, C, C), held(2, 2, C, C), held(2, HALF, C), held(2, C, C),
        held(8, QUAD, C), held(8, QUAD, C), held(QUAD, C),
    ]
    counts = [5] + [2] * 6 + [8, 8, 2, 2, 4, 4, 8, 8] + [4] * 6 + [1] * 6
    scratch += [pltpu.SemaphoreType.DMA((n,)) for n in counts]
    outs = [(args[0].shape, BF16), ((8, QUAD, C), BF16)]
    places = [pl.ANY] * 5 + [pltpu.VMEM]
    return call(main_kernel, outs, scratch, places, [pltpu.VMEM] * 2, 56, 1)(*args)


def finish_kernel(
    factor, grad_in, totals_in, grad_video, conv, qkv, out_w, gain, grad, totals, sems
):
    come = pltpu.make_async_copy(grad_in, grad, sems.at[0])
    come.start()
    read = pltpu.make_async_copy(totals_in, totals, sems.at[1])
    read.start()
    come.wait()
    go = pltpu.make_async_copy(grad, grad_video, sems.at[2])
    go.start()
    read.wait()
    tm = lax.axis_index("tm")
    pick = picks(lambda r: r + lax.rem(tm, 4) * SHARE, 16, QUAD)
    got = [mm(pick, totals[m]) for m in range(8)]
    for i in range(3):
        conv[i] = got[4 + i][0:SHARE] * factor
        qkv[:, i * C : (i + 1) * C] = got[1 + i][0:SHARE] * factor
    out_w[...] = got[0][0:SHARE] * factor
    row, col = iotas(C, SHARE)
    line = mm(got[7].astype(BF16), jnp.where(row == tm * SHARE + col, 1.0, 0.0).astype(BF16))
    row, col = iotas(16, SHARE)
    gain[...] = jnp.sum(jnp.where(row == col, line, 0.0), axis=0, keepdims=True) * factor
    go.wait()


def body(video, conv_w, qkv_w, out_w, gain, cotangent):
    grad_video, totals = main(video, cotangent, conv_w, qkv_w, out_w, gain.reshape(1, SHARE))
    factor = 1.0 / math.sqrt(
        lax.axis_size("clip") * lax.axis_size("tm") * video.shape[1] * video.shape[2]
    )
    outs = [
        (video.shape, BF16), (conv_w.shape, F32), (qkv_w.shape, F32), (out_w.shape, F32),
        ((1, SHARE), F32),
    ]
    got = call(
        functools.partial(finish_kernel, factor), outs,
        [
            pltpu.VMEM(video.shape, BF16), pltpu.VMEM((8, QUAD, C), BF16),
            pltpu.SemaphoreType.DMA((3,)),
        ],
        [pl.ANY] * 2, [pl.ANY] + [pltpu.VMEM] * 4, 56,
    )(grad_video, totals)
    return (*got[:4], got[4].reshape(SHARE))


def solution(mesh):
    in_specs = (
        P("clip", "tm", None, None),
        P(None, "tm", None),
        P("tm", None),
        P("tm", None),
        P("tm"),
        P("clip", "tm", None, None),
    )
    out_specs = (
        P("clip", "tm", None, None),
        P(None, "tm", None),
        P("tm", None),
        P("tm", None),
        P("tm"),
    )
    return jax.shard_map(body, mesh=mesh, in_specs=in_specs, out_specs=out_specs, check_vma=False)
```

```python
import functools
import math

import jax
import jax.numpy as jnp
from jax import lax
from jax.experimental import pallas as pl
from jax.experimental.pallas import tpu as pltpu
from jax.sharding import PartitionSpec as P

epsilon = 1e-06
F32 = jnp.float32
BF16 = jnp.bfloat16

C = 384
FRAMES = 64
SPOTS = 9
ROWS = SPOTS * FRAMES
PARTS = ((0, 5), (5, 4))
BLOCKS = (((0, 192), (192, 128)), ((0, 128), (128, 128)))
MATS = 7
WIDE = MATS * C


def mm(a, b):
    return lax.dot_general(a, b, (((1,), (0,)), ((), ())), preferred_element_type=F32)


def mm_nt(a, b):
    return lax.dot_general(a, b, (((1,), (1,)), ((), ())), preferred_element_type=F32)


def mm_tn(a, b):
    return lax.dot_general(a, b, (((0,), (0,)), ((), ())), preferred_element_type=F32)


def iotas(rows, columns):
    shape = (rows, columns)
    return lax.broadcasted_iota(jnp.int32, shape, 0), lax.broadcasted_iota(jnp.int32, shape, 1)


def delay_matrix(size, steps):
    row, col = iotas(size, size)
    return jnp.where((row - col == steps) & ((row & (FRAMES - 1)) >= steps), 1.0, 0.0).astype(BF16)


def forward(blocks, w, gain, x, s1, s2, hidden, inverse, normed, packed):
    for steps, ref in ((1, s1), (2, s2)):
        for first, size in blocks:
            rows = pl.ds(first, size)
            ref[rows, :] = mm(delay_matrix(size, steps), x[rows, :]).astype(BF16)
    mixed = mm(x[...], w[:, 0:C]) + mm(s1[...], w[:, C : 2 * C]) + mm(s2[...], w[:, 2 * C : 3 * C])
    hidden[...] = (x[...].astype(F32) + mixed).astype(BF16)
    wide = hidden[...].astype(F32)
    inverse[...] = lax.rsqrt(jnp.mean(wide * wide, axis=-1, keepdims=True) + epsilon)
    normed[...] = (wide * inverse[...] * gain[...]).astype(BF16)
    packed[...] = mm(normed[...], w[:, 3 * C : 6 * C]).astype(BF16)


def seen(size):
    row, col = iotas(size, size)
    return ((row >> 6) == (col >> 6)) & (col <= row)


def attention(blocks, w, cot, packed, attended, grad_att, grad_packed):
    factor = 1.0 / math.sqrt(C)
    grad_att[...] = mm_nt(cot[...], w[:, 6 * C : 7 * C]).astype(BF16)
    for first, size in blocks:
        part = pl.ds(first, size)
        query, keys, values = (packed[part, i * C : (i + 1) * C] for i in range(3))
        scores = jnp.where(seen(size), mm_nt(query, keys) * factor, -1e30)
        raised = jnp.exp(scores - jnp.max(scores, axis=-1, keepdims=True))
        probs = raised / jnp.sum(raised, axis=-1, keepdims=True)
        rounded = probs.astype(BF16)
        attended[part, :] = mm(rounded, values).astype(BF16)
        incoming = grad_att[part, :]
        dprob = mm_nt(incoming, values)
        dscore = probs * (dprob - jnp.sum(dprob * probs, axis=-1, keepdims=True))
        dscore = (dscore * factor).astype(BF16)
        grad_packed[part, 0:C] = mm(dscore, keys).astype(BF16)
        grad_packed[part, C : 2 * C] = mm_tn(dscore, query).astype(BF16)
        grad_packed[part, 2 * C : 3 * C] = mm_tn(rounded, incoming).astype(BF16)


def normalize_back(w, gain, cot, hidden, inverse, grad_packed, grad_hidden):
    grad_norm = mm_nt(grad_packed[...], w[:, 3 * C : 6 * C]).astype(BF16).astype(F32)
    wide = hidden[...].astype(F32)
    inv = inverse[...]
    scaled = grad_norm * gain[...]
    inner = jnp.mean(scaled * wide, axis=-1, keepdims=True)
    back = cot[...].astype(F32) + inv * scaled - wide * (inv * inv * inv * inner)
    grad_hidden[...] = back.astype(BF16)
    return jnp.sum(grad_norm * wide * inv, axis=0, keepdims=True)


def conv_back(blocks, w, grad_hidden, a1, a2, gv):
    for steps, ref in ((1, a1), (2, a2)):
        for first, size in blocks:
            rows = pl.ds(first, size)
            ref[rows, :] = mm_tn(delay_matrix(size, steps), grad_hidden[rows, :]).astype(BF16)
    grad = grad_hidden[...].astype(F32) + mm_nt(grad_hidden[...], w[:, 0:C])
    grad = grad + mm_nt(a1[...], w[:, C : 2 * C]) + mm_nt(a2[...], w[:, 2 * C : 3 * C])
    gv[...] = grad.astype(BF16)


WAYS = 32
PIECE = 112
CUTS = ((0, 64), (64, 48))
BACK = 64
SHARE = 12
QUAD = 4 * SHARE
HALF = C // 2
MESH = pl.DeviceIdType.MESH
FAR_FIRST = (4, 3, 5, 2, 6, 1, 7)


def ninth(n):
    return (n * 57) >> 9


def fifth(n):
    return (n * 205) >> 10


def twelfth(n):
    return (n * 1366) >> 14


def picks(target, rows, columns):
    width = min(columns, 128)
    row, col = iotas(rows, width)
    lane = target(row) - col
    parts = [
        jnp.where(lane == first, 1.0, 0.0).astype(BF16)
        for first in range(0, columns // width * width, width)
    ]
    rest = columns - columns // width * width
    if rest:
        last = lane[:, 0:rest] == columns - rest
        parts.append(jnp.where(last, 1.0, 0.0).astype(BF16))
    return parts[0] if len(parts) == 1 else jnp.concatenate(parts, 1)


def wrap(n, size):
    return jnp.where(n >= size, n - size, n)


def upper(x):
    return jnp.where(x >= 2, 1, 0)


class Place:
    def __init__(self):
        self.clip, self.tm = lax.axis_index("clip"), lax.axis_index("tm")
        self.y, self.z = lax.rem(self.clip, 8), lax.div(self.tm, 4)
        self.low = lax.rem(lax.div(self.tm, 2), 2)
        self.x = lax.div(self.clip, 8) * 2 + self.low
        self.core = lax.rem(self.tm, 2)
        self.rail = self.low * 2 + self.core

    def at(self, dx=0, dy=0, dz=0, other=False):
        x, y, z = wrap(self.x + dx, 4), wrap(self.y + dy, 8), wrap(self.z + dz, 8)
        core = 1 - self.core if other else self.core
        return (upper(x) * 8 + y, z * 4 + (x - upper(x) * 2) * 2 + core)

    def peer(self, k):
        return (self.clip, wrap(self.tm + k, WAYS))


def greet(me, outer):
    barrier = pltpu.get_barrier_semaphore()

    def tell(device):
        pl.semaphore_signal(barrier, inc=1, device_id=device, device_id_type=MESH)

    def step(k, carry):
        tell(me.peer(k))
        return carry

    lax.fori_loop(1, WAYS, step, 0)
    for k in range(1, 8):
        tell(me.at(dy=k))
    for device in outer:
        tell(device)
    return lambda: pl.semaphore_wait(barrier, WAYS - 1 + 7 + len(outer))


def remote(src, dst, sems, index, device):
    return pltpu.make_async_remote_copy(
        src_ref=src, dst_ref=dst, send_sem=sems[0].at[index], recv_sem=sems[1].at[index],
        device_id=device, device_id_type=MESH,
    )


def settle(ref, sem):
    pltpu.make_async_copy(ref, ref, sem).wait()


def each_peer(act):
    def step(i, carry):
        act(16 - i)
        act(16 + i)
        return carry

    act(16)
    lax.fori_loop(1, 16, step, 0)


def pack_in(d, video, cot, out):
    base = lax.min(lax.div(d * SPOTS, 16) * 16, 256)
    base = pl.multiple_of(base, 16)
    pieces = [
        ref[0, f, pl.ds(base, 32), c * 128 : (c + 1) * 128]
        for ref in (video, cot) for c in range(3) for f in range(2)
    ]
    shift = d * SPOTS - base

    def column(r):
        block = jnp.where(r < 64, fifth(r), (r - 64) >> 2)
        spot = jnp.where(r < 64, r - fifth(r) * 5, 5 + (r & 3))
        return block * 32 + spot + shift

    pick = picks(column, PIECE, 384)
    out[...] = mm(pick, jnp.concatenate(pieces, 0)).astype(BF16)


def pack_weights(tm, conv, qkv, out_w, gain, shard):
    row, col = iotas(SHARE, C)
    own = col == tm * SHARE + row
    line = mm(gain[...], jnp.where(own, 1.0, 0.0).astype(BF16))
    diagonal = jnp.where(own, line, 0.0).astype(BF16)
    mats = [conv[0], conv[1], conv[2], qkv[:, 0:C], qkv[:, C : 2 * C], qkv[:, 2 * C : 3 * C], out_w[...], diagonal]
    for h in range(2):
        total = 0.0
        for j in range(4):
            total = total + mm(picks(lambda r: r - j * SHARE, QUAD, SHARE), mats[4 * h + j])
        shard[h] = total.astype(BF16)


def unpack_in(part, landed, x, cot):
    (start, rows), spots = CUTS[part], PARTS[part][1]
    for a, ref in ((0, x), (1, cot)):
        for c in range(3):
            first = (a * 3 + c) * 2 * spots
            base = min(first // 16 * 16, rows - 32)

            def column(r):
                return ((r & 15) >> 1) * 32 + (r & 1) * spots + (r >> 4) + (first - base)

            pick = picks(column, spots * 16, 256)
            for g in range(4):
                source = landed[8 * g : 8 * g + 8, start + base : start + base + 32, :]
                got = mm(pick, source.reshape(256, 128)).astype(BF16)
                for p in range(spots):
                    row = p * FRAMES + 16 * g
                    ref[row : row + 16, c * 128 : (c + 1) * 128] = got[16 * p : 16 * p + 16]


def unpack_weights(weights, w, gain):
    for j in range(4):
        base, size = ((0, 16), (0, 32), (16, 32), (32, 16))[j]

        def column(r):
            block = twelfth(r)
            return ((block & 3) * 8 + (block >> 2)) * size + (r - block * SHARE) + j * SHARE - base

        pick = picks(column, C, WAYS * size)
        for h in range(2):
            m = 4 * h + j
            source = weights[h, :, :, base : base + size, :].reshape(WAYS * size, C)
            got = mm(pick, source)
            if m < MATS:
                w[:, m * C : (m + 1) * C] = got.astype(BF16)
            else:
                gain[...] = jnp.sum(got, axis=0, keepdims=True)


def pack_out(part, gv, out):
    spots = PARTS[part][1]

    def column(r):
        inner = r & 31
        block = fifth(inner) if spots == 5 else inner >> 2
        spot = inner - block * spots
        return (block >> 1) * (16 * spots) + spot * 16 + (r >> 5) * 2 + (block & 1)

    pick = picks(column, 256, 48 * spots)
    for g in range(4):
        pieces = [
            gv[p * FRAMES + 16 * g : p * FRAMES + 16 * g + 16, c * 128 : (c + 1) * 128]
            for c in range(3) for p in range(spots)
        ]
        got = mm(pick, jnp.concatenate(pieces, 0)).astype(BF16)
        out[8 * g : 8 * g + 8, 32 * part : 32 * part + 32, :] = got.reshape(8, 32, 128)


def unpack_out(landed, grad_video):
    for f in range(2):
        for c in range(3):

            def column(r):
                spot = r - ninth(r) * SPOTS
                inner = jnp.where(spot < 5, c * 10 + f * 5 + spot, 32 + c * 8 + f * 4 + spot - 5)
                return ninth(r) * BACK + inner

            pick = picks(column, 144, 16 * BACK)
            for h in range(2):
                source = landed[16 * h : 16 * h + 16].reshape(16 * BACK, 128)
                got = mm(pick, source).astype(BF16)
                grad_video[0, f, 144 * h : 144 * h + 144, c * 128 : (c + 1) * 128] = got


def gather_weights(me, shard, weights, z_sems, y_sems, x_sems, c_sems):
    half = lax.rem(me.y, 2)
    begun = []

    def go(copy):
        copy.start()
        begun.append(copy)
        return copy

    def block(dz, *rows):
        return weights.at[half, me.rail, wrap(me.z + dz, 8), *rows]

    def over_z():
        for k in (2, 6, 1, 7):
            go(remote(shard.at[half], block(0), z_sems, k, me.at(dz=k)))
        weights[half, me.rail, me.z] = shard[half]

    def onward():
        for copy in begun[:2]:
            copy.wait_recv()
        top, low = pl.ds(0, 32), pl.ds(32, 16)
        go(remote(block(6, top), block(6, top), z_sems, 4, me.at(dz=2)))
        go(remote(block(2, low), block(2, low), z_sems, 0, me.at(dz=6)))
        go(remote(block(6), block(6), z_sems, 3, me.at(dz=1)))
        go(remote(block(2), block(2), z_sems, 5, me.at(dz=7)))

    beyond = (1 - me.low) * 2 + me.core
    ways = ((0, 1, 1), (1, 7, 3))
    ys, xs, cs = [], [], []

    def part(h, rail, i):
        return weights.at[h, rail, pl.ds(4 * i, 4)]

    def over_x(h, n, i, step):
        mine = part(h, me.rail, i)
        xs.append(go(remote(mine, mine, x_sems, n, me.at(dx=step))))
        cs.append(go(remote(mine, mine, c_sems, n, me.at(other=True))))

    def own_half():
        for copy in list(begun[2:]):
            copy.wait_recv()
        for i, up, _ in ways:
            mine = part(half, me.rail, i)
            ys.append(go(remote(mine, mine, y_sems, i, me.at(dy=up))))
        for i, _, side in ways:
            over_x(half, i, i, side)

    def other_half():
        for i, _, side in ways:
            ys[i].wait_recv()
            over_x(1 - half, 2 + i, i, side)

    def far_rail():
        for n in range(4):
            xs[n].wait_recv()
            mine = part(half if n < 2 else 1 - half, beyond, n % 2)
            cs.append(go(remote(mine, mine, c_sems, 4 + n, me.at(other=True))))

    def done():
        for copy in cs:
            copy.wait_recv()

    def drain():
        for copy in begun:
            copy.wait_send()

    return (over_z, onward, own_half, other_half, far_rail, done), drain


class Sums:
    def __init__(self, me, sums, core_in, held, mid, x_in, z_in, y_in, y_out, totals, sems):
        self.__dict__.update(locals())
        self.round = lax.rem(me.x + me.core, 2)
        self.mine = lax.div(me.x, 2)

    def to_core(self, r, i):
        slot = (self.me.core if r else 1 - self.me.core) + 2 * i
        return remote(
            self.sums.at[r, slot], self.core_in.at[r, i], self.sems["c"], 2 * r + i,
            self.me.at(other=True),
        )

    def to_mid(self, r, i):
        part = self.held.at[r, 1 - self.mine, pl.ds(i * HALF, HALF)]
        return remote(part, self.mid.at[i], self.sems["m"], 2 * r + i, self.me.at(dx=3 if i else 1))

    def to_owner(self, r, i, half):
        step, rows = (3 if i else 1), pl.ds(half * HALF, HALF)
        which = upper(wrap(self.me.x + step, 4))
        copy = remote(
            self.held.at[r, which, rows], self.x_in.at[i, rows], self.sems["x"],
            4 * r + 2 * i + half, self.me.at(dx=step),
        )
        return which, copy

    def over_z(self, k):
        first = pl.multiple_of(wrap(self.me.z + k, 8) * QUAD, QUAD)
        part = self.held.at[self.round, self.mine, pl.ds(first, QUAD)]
        return remote(part, self.z_in.at[k], self.sems["z"], 0, self.me.at(dz=k))

    def over_y(self, k):
        mine = self.y_in.at[self.me.y]
        return remote(mine, mine, self.sems["y"], 0, self.me.at(dy=k))

    def over_row(self, k):
        dx, other = ((2, False), (2, True), (1, False), (3, False), (1, True), (3, True), (0, True))[k]
        own = self.round * 4 + self.me.x
        return remote(
            self.y_out, self.totals.at[own], self.sems["f"], 0, self.me.at(dx=dx, other=other)
        )

    def when_owner(self, r, act):
        pl.when(self.round == r)(act)

    def core_send(self, r):
        for i in range(2):
            self.to_core(r, i).start()

    def core_add(self, r):
        def add(i):
            slot = (1 - self.me.core if r else self.me.core) + 2 * i
            both = self.sums[r, slot].astype(F32) + self.core_in[r, i].astype(F32)
            self.held[r, i] = both.astype(BF16)

        for i in range(2):
            self.to_core(r, i).wait_recv()

        def owner():
            add(1 - self.mine)
            for i in range(2):
                self.to_mid(r, i).start()
            add(self.mine)

        def other():
            for i in range(2):
                add(i)
            for i in range(2):
                self.to_owner(r, i, 1 - i)[1].start()

        self.when_owner(r, owner)
        self.when_owner(1 - r, other)

    def relay(self, r):
        def act():
            for i in range(2):
                self.to_mid(r, i).wait_recv()
                which, copy = self.to_owner(r, i, i)
                rows = pl.ds(i * HALF, HALF)
                both = self.held[r, which, rows, :].astype(F32) + self.mid[i].astype(F32)
                self.held[r, which, rows, :] = both.astype(BF16)
                copy.start()

        self.when_owner(1 - r, act)

    def own_x(self, r):
        def act():
            total = self.held[r, self.mine].astype(F32)
            for i in range(2):
                for half in range(2):
                    self.to_owner(r, i, half)[1].wait_recv()
                total = total + self.x_in[i].astype(F32)
            self.held[r, self.mine] = total.astype(BF16)
            for k in FAR_FIRST:
                self.over_z(k).start()

        self.when_owner(r, act)

    def own_z(self):
        here = pl.ds(pl.multiple_of(self.me.z * QUAD, QUAD), QUAD)
        total = self.held[self.round, self.mine, here, :].astype(F32)
        settle(self.z_in.at[pl.ds(1, 7)], self.sems["z"][1].at[0])
        for k in range(1, 8):
            total = total + self.z_in[k].astype(F32)
        self.y_in[self.me.y] = total.astype(BF16)
        for k in FAR_FIRST:
            self.over_y(k).start()

    def own_y(self):
        settle(self.y_in.at[pl.ds(1, 7)], self.sems["y"][1].at[0])
        total = self.y_in[0].astype(F32)
        for k in range(1, 8):
            total = total + self.y_in[k].astype(F32)
        self.y_out[...] = total.astype(BF16)
        for k in range(7):
            self.over_row(k).start()
        self.totals[self.round * 4 + self.me.x] = self.y_out[...]

    def drain(self):
        for sem in (*self.sems["f"], self.sems["z"][0], self.sems["y"][0]):
            settle(self.z_in.at[pl.ds(1, 7)], sem.at[0])
        for r in range(2):
            for i in range(2):
                self.to_core(r, i).wait_send()

            def owner(r=r):
                for i in range(2):
                    self.to_mid(r, i).wait_send()

            def other(r=r):
                for i in range(2):
                    for half in range(2):
                        self.to_owner(r, i, half)[1].wait_send()

            self.when_owner(r, owner)
            self.when_owner(1 - r, other)


def main_kernel(
    video_in, cot_in, conv_in, qkv_in, out_in, gain_in, grad_video, totals,
    video, cotangent, conv, qkv, out_w, parcels, shard, landed, weights,
    w, gain, parcels_out, landed_out, acc, gain_acc,
    x, cot, s1, s2, hidden, inverse, normed, packed, attended, grad_att, grad_packed,
    grad_hidden, a1, a2, gv,
    sums, core_in, held, mid, x_in, z_in, y_in, y_out,
    l_s, v_s, v_r, i_s, i_r, o_s, o_r, wz_s, wz_r, wy_s, wy_r, wx_s, wx_r, wc_s, wc_r,
    sc_s, sc_r, sm_s, sm_r, sx_s, sx_r, sz_s, sz_r, sy_s, sy_r, sf_s, sf_r,
):
    me = Place()
    pairs = (
        (conv_in, conv), (qkv_in, qkv), (out_in, out_w), (video_in, video.at[me.core]),
        (cot_in, cotangent.at[me.core]),
    )
    reads = [pltpu.make_async_copy(src, dst, l_s.at[n]) for n, (src, dst) in enumerate(pairs)]
    for copy in reads:
        copy.start()
    outer = jnp.where(me.low == 0, 3, 1)
    met = greet(me, [me.at(dx=dx, other=o) for dx in (2, outer) for o in (False, True)])
    for copy in reads[:3]:
        copy.wait()
    pack_weights(me.tm, conv, qkv, out_w, gain_in, shard)
    for copy in reads[3:]:
        copy.wait()
    met()
    swaps = [
        remote(ref.at[me.core], ref.at[me.core], (v_s, v_r), n, me.at(other=True))
        for n, ref in enumerate((video, cotangent))
    ]
    for copy in swaps:
        copy.start()

    steps, drain = gather_weights(
        me, shard, weights, (wz_s, wz_r), (wy_s, wy_r), (wx_s, wx_r), (wc_s, wc_r)
    )
    steps[0]()

    chip = lax.div(me.tm, 2)

    def toward(k):
        there = wrap(chip + k, WAYS // 2)
        return there, 2 * there + me.core

    def coming(part, k):
        (there, target), rows = toward(k), pl.ds(*CUTS[part])
        return remote(
            parcels.at[there, pl.ds(0, 2), rows], landed.at[pl.ds(2 * chip, 2), rows],
            (i_s, i_r), part, (me.clip, target),
        )

    def going(part, k):
        device, rows = me.peer(k), pl.ds(32 * part, 32)
        return remote(
            parcels_out.at[device[1], rows], landed_out.at[me.tm, rows], (o_s, o_r), part, device
        )

    def arrive(part, sems):
        settle(landed.at[pl.ds(0, WAYS - 2), pl.ds(*CUTS[part])], sems.at[part])

    def returned(part, sems):
        settle(landed_out.at[pl.ds(0, WAYS - 1), pl.ds(32 * part, 32)], sems.at[part])

    def pack(target, place):
        for source in range(2):
            pack_in(target, video.at[source], cotangent.at[source], place(source))

    def one(k):
        there, target = toward(k)
        pack(target, lambda source: parcels.at[there, source])
        coming(0, k).start()

    def two(i, carry):
        one(8 - i)
        one(8 + i)
        return carry

    for copy in swaps:
        copy.wait_recv()
    one(8)
    lax.fori_loop(1, 2, two, 0)
    steps[1]()
    lax.fori_loop(2, 4, two, 0)
    steps[2]()
    lax.fori_loop(4, 6, two, 0)
    steps[3]()
    lax.fori_loop(6, 8, two, 0)
    pack(me.tm, lambda source: landed.at[2 * chip + source])
    steps[4]()

    def late(i, carry):
        coming(1, 8 - i).start()
        coming(1, 8 + i).start()
        return carry

    coming(1, 8).start()
    lax.fori_loop(1, 8, late, 0)
    steps[5]()
    unpack_weights(weights, w, gain)

    total = Sums(
        me, sums, core_in, held, mid, x_in, z_in, y_in, y_out, totals,
        dict(
            c=(sc_s, sc_r), m=(sm_s, sm_r), x=(sx_s, sx_r), z=(sz_s, sz_r), y=(sy_s, sy_r),
            f=(sf_s, sf_r),
        ),
    )
    tall = (
        x, cot, s1, s2, hidden, inverse, normed, packed, attended, grad_att, grad_packed,
        grad_hidden, a1, a2, gv,
    )
    for part, (first, spots) in enumerate(PARTS):
        rows = pl.ds(first * FRAMES, spots * FRAMES)
        (
            px, pcot, ps1, ps2, phidden, pinverse, pnormed, ppacked, pattended, pgrad_att,
            pgrad_packed, pgrad_hidden, pa1, pa2, pgv,
        ) = (ref.at[rows] for ref in tall)
        blocks = BLOCKS[part]
        arrive(part, i_r)
        unpack_in(part, landed, px, pcot)
        forward(blocks, w, gain, px, ps1, ps2, phidden, pinverse, pnormed, ppacked)
        attention(blocks, w, pcot, ppacked, pattended, pgrad_att, pgrad_packed)

        def add(n, product):
            if part == 0:
                acc[n] = product
            else:
                sums[n // 4, n % 4] = (acc[n] + product).astype(BF16)

        def early_sums():
            add(0, mm_tn(pattended[...], pcot[...]))
            product = mm_tn(pnormed[...], pgrad_packed[...])
            for i in range(3):
                add(1 + i, product[:, i * C : (i + 1) * C])

        def late_sums():
            for tap, ref in enumerate((px, ps1, ps2)):
                add(4 + tap, mm_tn(ref[...], pgrad_hidden[...]))

        def send_back():
            pack_out(part, pgv, parcels_out)
            landed_out[me.tm, 32 * part : 32 * part + 32, :] = (
                parcels_out[me.tm, 32 * part : 32 * part + 32, :]
            )

        def norm_back():
            return normalize_back(w, gain, pcot, phidden, pinverse, pgrad_packed, pgrad_hidden)

        if part == 0:
            gain_acc[...] = norm_back()
            conv_back(blocks, w, pgrad_hidden, pa1, pa2, pgv)
            send_back()
            each_peer(lambda k: going(0, k).start())
            early_sums()
            late_sums()
        else:
            early_sums()
            total.core_send(0)
            gain_sum = gain_acc[...] + norm_back()
            row, col = iotas(C, C)
            sums[1, 3] = jnp.where(row == col, gain_sum, 0.0).astype(BF16)
            late_sums()
            total.core_send(1)
            total.core_add(0)
            conv_back(blocks, w, pgrad_hidden, pa1, pa2, pgv)
            total.core_add(1)
            total.relay(0)
            send_back()
    total.relay(1)
    total.own_x(0)
    total.own_x(1)
    total.own_z()
    each_peer(lambda k: going(1, k).start())
    total.own_y()
    for part in range(2):
        returned(part, o_r)
    unpack_out(landed_out, grad_video)
    total.drain()
    drain()
    for copy in swaps:
        copy.wait_send()
    for part in range(2):
        arrive(part, i_s)
        returned(part, o_s)


def call(kernel, outs, scratch, places, out_places, mib, collective=None):
    extra = {} if collective is None else dict(collective_id=collective, has_side_effects=True)
    return pl.pallas_call(
        kernel,
        out_shape=[jax.ShapeDtypeStruct(*o) for o in outs],
        in_specs=[pl.BlockSpec(memory_space=place) for place in places],
        out_specs=[pl.BlockSpec(memory_space=place) for place in out_places],
        scratch_shapes=scratch,
        compiler_params=pltpu.CompilerParams(vmem_limit_bytes=mib * 1024 * 1024, **extra),
    )


def main(*args):
    def held(*shape, kind=BF16):
        return pltpu.VMEM(shape, kind)

    tall = held(ROWS, C)
    scratch = [
        held(2, 1, 2, 288, C), held(2, 1, 2, 288, C), held(3, SHARE, C), held(SHARE, 3 * C), held(SHARE, C),
        held(WAYS // 2, 2, PIECE, 128), held(2, QUAD, C), held(WAYS, PIECE, 128), held(2, 4, 8, QUAD, C),
        held(C, WIDE), held(1, C, kind=F32), held(WAYS, BACK, 128), held(WAYS, BACK, 128), held(MATS, C, C, kind=F32),
        held(1, C, kind=F32),
        tall, tall, tall, tall, tall, held(ROWS, 1, kind=F32), tall, held(ROWS, 3 * C), tall, tall,
        held(ROWS, 3 * C), tall, tall, tall, tall,
        held(2, 4, C, C), held(2, 2, C, C), held(2, 2, C, C), held(2, HALF, C), held(2, C, C),
        held(8, QUAD, C), held(8, QUAD, C), held(QUAD, C),
    ]
    counts = [5] + [2] * 6 + [8, 8, 2, 2, 4, 4, 8, 8] + [4] * 4 + [8] * 2 + [1] * 6
    scratch += [pltpu.SemaphoreType.DMA((n,)) for n in counts]
    outs = [(args[0].shape, BF16), ((8, QUAD, C), BF16)]
    places = [pl.ANY] * 5 + [pltpu.VMEM]
    return call(main_kernel, outs, scratch, places, [pltpu.VMEM] * 2, 56, 1)(*args)


def finish_kernel(
    factor, grad_in, totals_in, grad_video, conv, qkv, out_w, gain, grad, totals, sems
):
    come = pltpu.make_async_copy(grad_in, grad, sems.at[0])
    come.start()
    read = pltpu.make_async_copy(totals_in, totals, sems.at[1])
    read.start()
    come.wait()
    go = pltpu.make_async_copy(grad, grad_video, sems.at[2])
    go.start()
    read.wait()
    tm = lax.axis_index("tm")
    pick = picks(lambda r: r + lax.rem(tm, 4) * SHARE, 16, QUAD)
    got = [mm(pick, totals[m]) for m in range(8)]
    for i in range(3):
        conv[i] = got[4 + i][0:SHARE] * factor
        qkv[:, i * C : (i + 1) * C] = got[1 + i][0:SHARE] * factor
    out_w[...] = got[0][0:SHARE] * factor
    row, col = iotas(C, SHARE)
    line = mm(got[7].astype(BF16), jnp.where(row == tm * SHARE + col, 1.0, 0.0).astype(BF16))
    row, col = iotas(16, SHARE)
    gain[...] = jnp.sum(jnp.where(row == col, line, 0.0), axis=0, keepdims=True) * factor
    go.wait()


def body(video, conv_w, qkv_w, out_w, gain, cotangent):
    grad_video, totals = main(video, cotangent, conv_w, qkv_w, out_w, gain.reshape(1, SHARE))
    factor = 1.0 / math.sqrt(
        lax.axis_size("clip") * lax.axis_size("tm") * video.shape[1] * video.shape[2]
    )
    outs = [
        (video.shape, BF16), (conv_w.shape, F32), (qkv_w.shape, F32), (out_w.shape, F32),
        ((1, SHARE), F32),
    ]
    got = call(
        functools.partial(finish_kernel, factor), outs,
        [
            pltpu.VMEM(video.shape, BF16), pltpu.VMEM((8, QUAD, C), BF16),
            pltpu.SemaphoreType.DMA((3,)),
        ],
        [pl.ANY] * 2, [pl.ANY] + [pltpu.VMEM] * 4, 56,
    )(grad_video, totals)
    return (*got[:4], got[4].reshape(SHARE))


def solution(mesh):
    in_specs = (
        P("clip", "tm", None, None),
        P(None, "tm", None),
        P("tm", None),
        P("tm", None),
        P("tm"),
        P("clip", "tm", None, None),
    )
    out_specs = (
        P("clip", "tm", None, None),
        P(None, "tm", None),
        P("tm", None),
        P("tm", None),
        P("tm"),
    )
    return jax.shard_map(body, mesh=mesh, in_specs=in_specs, out_specs=out_specs, check_vma=False)
```

```python
import functools
import math

import jax
import jax.numpy as jnp
from jax import lax
from jax.experimental import pallas as pl
from jax.experimental.pallas import tpu as pltpu
from jax.sharding import PartitionSpec as P

epsilon = 1e-06
F32 = jnp.float32
BF16 = jnp.bfloat16

C = 384
FRAMES = 64
SPOTS = 9
ROWS = SPOTS * FRAMES
PARTS = ((0, 5), (5, 4))
BLOCKS = (((0, 192), (192, 128)), ((0, 128), (128, 128)))
MATS = 7
WIDE = MATS * C


def mm(a, b):
    return lax.dot_general(a, b, (((1,), (0,)), ((), ())), preferred_element_type=F32)


def mm_nt(a, b):
    return lax.dot_general(a, b, (((1,), (1,)), ((), ())), preferred_element_type=F32)


def mm_tn(a, b):
    return lax.dot_general(a, b, (((0,), (0,)), ((), ())), preferred_element_type=F32)


def iotas(rows, columns):
    shape = (rows, columns)
    return lax.broadcasted_iota(jnp.int32, shape, 0), lax.broadcasted_iota(jnp.int32, shape, 1)


def delay_matrix(size, steps):
    row, col = iotas(size, size)
    return jnp.where((row - col == steps) & ((row & (FRAMES - 1)) >= steps), 1.0, 0.0).astype(BF16)


def forward(blocks, w, gain, x, s1, s2, hidden, inverse, normed, packed):
    for steps, ref in ((1, s1), (2, s2)):
        for first, size in blocks:
            rows = pl.ds(first, size)
            ref[rows, :] = mm(delay_matrix(size, steps), x[rows, :]).astype(BF16)
    mixed = mm(x[...], w[:, 0:C]) + mm(s1[...], w[:, C : 2 * C]) + mm(s2[...], w[:, 2 * C : 3 * C])
    hidden[...] = (x[...].astype(F32) + mixed).astype(BF16)
    wide = hidden[...].astype(F32)
    inverse[...] = lax.rsqrt(jnp.mean(wide * wide, axis=-1, keepdims=True) + epsilon)
    normed[...] = (wide * inverse[...] * gain[...]).astype(BF16)
    packed[...] = mm(normed[...], w[:, 3 * C : 6 * C]).astype(BF16)


def seen(size):
    row, col = iotas(size, size)
    return ((row >> 6) == (col >> 6)) & (col <= row)


def attention(blocks, w, cot, packed, attended, grad_att, grad_packed):
    factor = 1.0 / math.sqrt(C)
    grad_att[...] = mm_nt(cot[...], w[:, 6 * C : 7 * C]).astype(BF16)
    for first, size in blocks:
        part = pl.ds(first, size)
        query, keys, values = (packed[part, i * C : (i + 1) * C] for i in range(3))
        scores = jnp.where(seen(size), mm_nt(query, keys) * factor, -1e30)
        raised = jnp.exp(scores - jnp.max(scores, axis=-1, keepdims=True))
        probs = raised / jnp.sum(raised, axis=-1, keepdims=True)
        rounded = probs.astype(BF16)
        attended[part, :] = mm(rounded, values).astype(BF16)
        incoming = grad_att[part, :]
        dprob = mm_nt(incoming, values)
        dscore = probs * (dprob - jnp.sum(dprob * probs, axis=-1, keepdims=True))
        dscore = (dscore * factor).astype(BF16)
        grad_packed[part, 0:C] = mm(dscore, keys).astype(BF16)
        grad_packed[part, C : 2 * C] = mm_tn(dscore, query).astype(BF16)
        grad_packed[part, 2 * C : 3 * C] = mm_tn(rounded, incoming).astype(BF16)


def normalize_back(w, gain, cot, hidden, inverse, grad_packed, grad_hidden):
    grad_norm = mm_nt(grad_packed[...], w[:, 3 * C : 6 * C]).astype(BF16).astype(F32)
    wide = hidden[...].astype(F32)
    inv = inverse[...]
    scaled = grad_norm * gain[...]
    inner = jnp.mean(scaled * wide, axis=-1, keepdims=True)
    back = cot[...].astype(F32) + inv * scaled - wide * (inv * inv * inv * inner)
    grad_hidden[...] = back.astype(BF16)
    return jnp.sum(grad_norm * wide * inv, axis=0, keepdims=True)


def conv_back(blocks, w, grad_hidden, a1, a2, gv):
    for steps, ref in ((1, a1), (2, a2)):
        for first, size in blocks:
            rows = pl.ds(first, size)
            ref[rows, :] = mm_tn(delay_matrix(size, steps), grad_hidden[rows, :]).astype(BF16)
    grad = grad_hidden[...].astype(F32) + mm_nt(grad_hidden[...], w[:, 0:C])
    grad = grad + mm_nt(a1[...], w[:, C : 2 * C]) + mm_nt(a2[...], w[:, 2 * C : 3 * C])
    gv[...] = grad.astype(BF16)


WAYS = 32
PIECE = 112
CUTS = ((0, 64), (64, 48))
BACK = 64
SHARE = 12
QUAD = 4 * SHARE
HALF = C // 2
MESH = pl.DeviceIdType.MESH
FAR_FIRST = (4, 3, 5, 2, 6, 1, 7)


def ninth(n):
    return (n * 57) >> 9


def fifth(n):
    return (n * 205) >> 10


def twelfth(n):
    return (n * 1366) >> 14


def picks(target, rows, columns):
    width = min(columns, 128)
    row, col = iotas(rows, width)
    lane = target(row) - col
    parts = [
        jnp.where(lane == first, 1.0, 0.0).astype(BF16)
        for first in range(0, columns // width * width, width)
    ]
    rest = columns - columns // width * width
    if rest:
        last = lane[:, 0:rest] == columns - rest
        parts.append(jnp.where(last, 1.0, 0.0).astype(BF16))
    return parts[0] if len(parts) == 1 else jnp.concatenate(parts, 1)


def wrap(n, size):
    return jnp.where(n >= size, n - size, n)


def upper(x):
    return jnp.where(x >= 2, 1, 0)


class Place:
    def __init__(self):
        self.clip, self.tm = lax.axis_index("clip"), lax.axis_index("tm")
        self.y, self.z = lax.rem(self.clip, 8), lax.div(self.tm, 4)
        self.low = lax.rem(lax.div(self.tm, 2), 2)
        self.x = lax.div(self.clip, 8) * 2 + self.low
        self.core = lax.rem(self.tm, 2)
        self.rail = self.low * 2 + self.core

    def at(self, dx=0, dy=0, dz=0, other=False):
        x, y, z = wrap(self.x + dx, 4), wrap(self.y + dy, 8), wrap(self.z + dz, 8)
        core = 1 - self.core if other else self.core
        return (upper(x) * 8 + y, z * 4 + (x - upper(x) * 2) * 2 + core)

    def peer(self, k):
        return (self.clip, wrap(self.tm + k, WAYS))


def greet(me, outer):
    barrier = pltpu.get_barrier_semaphore()

    def tell(device):
        pl.semaphore_signal(barrier, inc=1, device_id=device, device_id_type=MESH)

    def step(k, carry):
        tell(me.peer(k))
        return carry

    lax.fori_loop(1, WAYS, step, 0)
    for k in range(1, 8):
        tell(me.at(dy=k))
    for device in outer:
        tell(device)
    return lambda: pl.semaphore_wait(barrier, WAYS - 1 + 7 + len(outer))


def remote(src, dst, sems, index, device):
    return pltpu.make_async_remote_copy(
        src_ref=src, dst_ref=dst, send_sem=sems[0].at[index], recv_sem=sems[1].at[index],
        device_id=device, device_id_type=MESH,
    )


def settle(ref, sem):
    pltpu.make_async_copy(ref, ref, sem).wait()


def each_peer(act):
    def step(i, carry):
        act(16 - i)
        act(16 + i)
        return carry

    act(16)
    lax.fori_loop(1, 16, step, 0)


def pack_in(d, video, cot, out):
    base = lax.min(lax.div(d * SPOTS, 16) * 16, 256)
    base = pl.multiple_of(base, 16)
    pieces = [
        ref[0, f, pl.ds(base, 32), c * 128 : (c + 1) * 128]
        for ref in (video, cot) for c in range(3) for f in range(2)
    ]
    shift = d * SPOTS - base

    def column(r):
        block = jnp.where(r < 64, fifth(r), (r - 64) >> 2)
        spot = jnp.where(r < 64, r - fifth(r) * 5, 5 + (r & 3))
        return block * 32 + spot + shift

    pick = picks(column, PIECE, 384)
    out[...] = mm(pick, jnp.concatenate(pieces, 0)).astype(BF16)


def pack_weights(tm, conv, qkv, out_w, gain, shard):
    row, col = iotas(SHARE, C)
    own = col == tm * SHARE + row
    line = mm(gain[...], jnp.where(own, 1.0, 0.0).astype(BF16))
    diagonal = jnp.where(own, line, 0.0).astype(BF16)
    mats = [conv[0], conv[1], conv[2], qkv[:, 0:C], qkv[:, C : 2 * C], qkv[:, 2 * C : 3 * C], out_w[...], diagonal]
    for h in range(2):
        total = 0.0
        for j in range(4):
            total = total + mm(picks(lambda r: r - j * SHARE, QUAD, SHARE), mats[4 * h + j])
        shard[h] = total.astype(BF16)


def unpack_in(part, landed, x, cot):
    (start, rows), spots = CUTS[part], PARTS[part][1]
    for a, ref in ((0, x), (1, cot)):
        for c in range(3):
            first = (a * 3 + c) * 2 * spots
            base = min(first // 16 * 16, rows - 32)

            def column(r):
                return ((r & 15) >> 1) * 32 + (r & 1) * spots + (r >> 4) + (first - base)

            pick = picks(column, spots * 16, 256)
            for g in range(4):
                source = landed[8 * g : 8 * g + 8, start + base : start + base + 32, :]
                got = mm(pick, source.reshape(256, 128)).astype(BF16)
                for p in range(spots):
                    row = p * FRAMES + 16 * g
                    ref[row : row + 16, c * 128 : (c + 1) * 128] = got[16 * p : 16 * p + 16]


def unpack_weights(weights, w, gain):
    for j in range(4):
        base, size = ((0, 16), (0, 32), (16, 32), (32, 16))[j]

        def column(r):
            block = twelfth(r)
            return ((block & 3) * 8 + (block >> 2)) * size + (r - block * SHARE) + j * SHARE - base

        pick = picks(column, C, WAYS * size)
        for h in range(2):
            m = 4 * h + j
            source = weights[h, :, :, base : base + size, :].reshape(WAYS * size, C)
            got = mm(pick, source)
            if m < MATS:
                w[:, m * C : (m + 1) * C] = got.astype(BF16)
            else:
                gain[...] = jnp.sum(got, axis=0, keepdims=True)


def pack_out(part, gv, out):
    spots = PARTS[part][1]

    def column(r):
        inner = r & 31
        block = fifth(inner) if spots == 5 else inner >> 2
        spot = inner - block * spots
        return (block >> 1) * (16 * spots) + spot * 16 + (r >> 5) * 2 + (block & 1)

    pick = picks(column, 256, 48 * spots)
    for g in range(4):
        pieces = [
            gv[p * FRAMES + 16 * g : p * FRAMES + 16 * g + 16, c * 128 : (c + 1) * 128]
            for c in range(3) for p in range(spots)
        ]
        got = mm(pick, jnp.concatenate(pieces, 0)).astype(BF16)
        out[8 * g : 8 * g + 8, 32 * part : 32 * part + 32, :] = got.reshape(8, 32, 128)


def unpack_out(landed, grad_video):
    for f in range(2):
        for c in range(3):

            def column(r):
                spot = r - ninth(r) * SPOTS
                inner = jnp.where(spot < 5, c * 10 + f * 5 + spot, 32 + c * 8 + f * 4 + spot - 5)
                return ninth(r) * BACK + inner

            pick = picks(column, 144, 16 * BACK)
            for h in range(2):
                source = landed[16 * h : 16 * h + 16].reshape(16 * BACK, 128)
                got = mm(pick, source).astype(BF16)
                grad_video[0, f, 144 * h : 144 * h + 144, c * 128 : (c + 1) * 128] = got


def gather_weights(me, shard, weights, z_sems, y_sems, x_sems, c_sems):
    half = lax.rem(me.y, 2)
    begun = []

    def go(copy):
        copy.start()
        begun.append(copy)
        return copy

    def block(dz, *rows):
        return weights.at[half, me.rail, wrap(me.z + dz, 8), *rows]

    def over_z():
        for k in (2, 6, 1, 7):
            go(remote(shard.at[half], block(0), z_sems, k, me.at(dz=k)))
        weights[half, me.rail, me.z] = shard[half]

    def onward():
        for copy in begun[:2]:
            copy.wait_recv()
        top, low = pl.ds(0, 32), pl.ds(32, 16)
        go(remote(block(6, top), block(6, top), z_sems, 4, me.at(dz=2)))
        go(remote(block(2, low), block(2, low), z_sems, 0, me.at(dz=6)))
        go(remote(block(6), block(6), z_sems, 3, me.at(dz=1)))
        go(remote(block(2), block(2), z_sems, 5, me.at(dz=7)))

    beyond = (1 - me.low) * 2 + me.core
    ways = ((0, 1, 1), (1, 7, 3))
    ys, xs, cs = [], [], []

    def part(h, rail, i):
        return weights.at[h, rail, pl.ds(4 * i, 4)]

    def over_x(h, n, i, step):
        mine = part(h, me.rail, i)
        xs.append(go(remote(mine, mine, x_sems, n, me.at(dx=step))))
        cs.append(go(remote(mine, mine, c_sems, n, me.at(other=True))))

    def own_half():
        for copy in list(begun[2:]):
            copy.wait_recv()
        for i, up, _ in ways:
            mine = part(half, me.rail, i)
            ys.append(go(remote(mine, mine, y_sems, i, me.at(dy=up))))
        for i, _, side in ways:
            over_x(half, i, i, side)

    def other_half():
        for i, _, side in ways:
            ys[i].wait_recv()
            over_x(1 - half, 2 + i, i, side)

    def far_rail():
        for n in range(4):
            xs[n].wait_recv()
            mine = part(half if n < 2 else 1 - half, beyond, n % 2)
            cs.append(go(remote(mine, mine, c_sems, 4 + n, me.at(other=True))))

    def done():
        for copy in cs:
            copy.wait_recv()

    def drain():
        for copy in begun:
            copy.wait_send()

    return (over_z, onward, own_half, other_half, far_rail, done), drain


class Sums:
    def __init__(self, me, sums, core_in, held, mid, x_in, z_in, y_in, y_out, totals, sems):
        self.__dict__.update(locals())
        self.round = lax.rem(me.x + me.core, 2)
        self.mine = lax.div(me.x, 2)

    def to_core(self, r, i):
        slot = (self.me.core if r else 1 - self.me.core) + 2 * i
        return remote(
            self.sums.at[r, slot], self.core_in.at[r, i], self.sems["c"], 2 * r + i,
            self.me.at(other=True),
        )

    def to_mid(self, r, i):
        part = self.held.at[r, 1 - self.mine, pl.ds(i * HALF, HALF)]
        return remote(part, self.mid.at[i], self.sems["m"], 2 * r + i, self.me.at(dx=3 if i else 1))

    def to_owner(self, r, i, half):
        step, rows = (3 if i else 1), pl.ds(half * HALF, HALF)
        which = upper(wrap(self.me.x + step, 4))
        copy = remote(
            self.held.at[r, which, rows], self.x_in.at[i, rows], self.sems["x"],
            4 * r + 2 * i + half, self.me.at(dx=step),
        )
        return which, copy

    def over_z(self, k):
        first = pl.multiple_of(wrap(self.me.z + k, 8) * QUAD, QUAD)
        part = self.held.at[self.round, self.mine, pl.ds(first, QUAD)]
        return remote(part, self.z_in.at[k], self.sems["z"], 0, self.me.at(dz=k))

    def over_y(self, k):
        mine = self.y_in.at[self.me.y]
        return remote(mine, mine, self.sems["y"], 0, self.me.at(dy=k))

    def over_row(self, k):
        dx, other = ((2, False), (2, True), (1, False), (3, False), (1, True), (3, True), (0, True))[k]
        own = self.round * 4 + self.me.x
        return remote(
            self.y_out, self.totals.at[own], self.sems["f"], 0, self.me.at(dx=dx, other=other)
        )

    def when_owner(self, r, act):
        pl.when(self.round == r)(act)

    def core_send(self, r):
        for i in range(2):
            self.to_core(r, i).start()

    def core_add(self, r):
        def add(i):
            slot = (1 - self.me.core if r else self.me.core) + 2 * i
            both = self.sums[r, slot].astype(F32) + self.core_in[r, i].astype(F32)
            self.held[r, i] = both.astype(BF16)

        for i in range(2):
            self.to_core(r, i).wait_recv()

        def owner():
            add(1 - self.mine)
            for i in range(2):
                self.to_mid(r, i).start()
            add(self.mine)

        def other():
            for i in range(2):
                add(i)
            for i in range(2):
                self.to_owner(r, i, 1 - i)[1].start()

        self.when_owner(r, owner)
        self.when_owner(1 - r, other)

    def relay(self, r):
        def act():
            for i in range(2):
                self.to_mid(r, i).wait_recv()
                which, copy = self.to_owner(r, i, i)
                rows = pl.ds(i * HALF, HALF)
                both = self.held[r, which, rows, :].astype(F32) + self.mid[i].astype(F32)
                self.held[r, which, rows, :] = both.astype(BF16)
                copy.start()

        self.when_owner(1 - r, act)

    def own_x(self, r):
        def act():
            total = self.held[r, self.mine].astype(F32)
            for i in range(2):
                for half in range(2):
                    self.to_owner(r, i, half)[1].wait_recv()
                total = total + self.x_in[i].astype(F32)
            self.held[r, self.mine] = total.astype(BF16)
            for k in FAR_FIRST:
                self.over_z(k).start()

        self.when_owner(r, act)

    def own_z(self):
        here = pl.ds(pl.multiple_of(self.me.z * QUAD, QUAD), QUAD)
        total = self.held[self.round, self.mine, here, :].astype(F32)
        settle(self.z_in.at[pl.ds(1, 7)], self.sems["z"][1].at[0])
        for k in range(1, 8):
            total = total + self.z_in[k].astype(F32)
        self.y_in[self.me.y] = total.astype(BF16)
        for k in FAR_FIRST:
            self.over_y(k).start()

    def own_y(self):
        settle(self.y_in.at[pl.ds(1, 7)], self.sems["y"][1].at[0])
        total = self.y_in[0].astype(F32)
        for k in range(1, 8):
            total = total + self.y_in[k].astype(F32)
        self.y_out[...] = total.astype(BF16)
        for k in range(7):
            self.over_row(k).start()
        self.totals[self.round * 4 + self.me.x] = self.y_out[...]

    def drain(self):
        for sem in (*self.sems["f"], self.sems["z"][0], self.sems["y"][0]):
            settle(self.z_in.at[pl.ds(1, 7)], sem.at[0])
        for r in range(2):
            for i in range(2):
                self.to_core(r, i).wait_send()

            def owner(r=r):
                for i in range(2):
                    self.to_mid(r, i).wait_send()

            def other(r=r):
                for i in range(2):
                    for half in range(2):
                        self.to_owner(r, i, half)[1].wait_send()

            self.when_owner(r, owner)
            self.when_owner(1 - r, other)


def main_kernel(
    video_in, cot_in, conv_in, qkv_in, out_in, gain_in, grad_video, totals,
    video, cotangent, conv, qkv, out_w, parcels, shard, landed, weights,
    w, gain, parcels_out, landed_out, acc, gain_acc,
    x, cot, s1, s2, hidden, inverse, normed, packed, attended, grad_att, grad_packed,
    grad_hidden, a1, a2, gv,
    sums, core_in, held, mid, x_in, z_in, y_in, y_out,
    l_s, v_s, v_r, i_s, i_r, o_s, o_r, wz_s, wz_r, wy_s, wy_r, wx_s, wx_r, wc_s, wc_r,
    sc_s, sc_r, sm_s, sm_r, sx_s, sx_r, sz_s, sz_r, sy_s, sy_r, sf_s, sf_r,
):
    me = Place()
    pairs = (
        (conv_in, conv), (qkv_in, qkv), (out_in, out_w), (video_in, video.at[me.core]),
        (cot_in, cotangent.at[me.core]),
    )
    reads = [pltpu.make_async_copy(src, dst, l_s.at[n]) for n, (src, dst) in enumerate(pairs)]
    for copy in reads:
        copy.start()
    outer = jnp.where(me.low == 0, 3, 1)
    met = greet(me, [me.at(dx=dx, other=o) for dx in (2, outer) for o in (False, True)])
    for copy in reads[:3]:
        copy.wait()
    pack_weights(me.tm, conv, qkv, out_w, gain_in, shard)
    for copy in reads[3:]:
        copy.wait()
    met()
    swaps = [
        remote(ref.at[me.core], ref.at[me.core], (v_s, v_r), n, me.at(other=True))
        for n, ref in enumerate((video, cotangent))
    ]
    for copy in swaps:
        copy.start()

    steps, drain = gather_weights(
        me, shard, weights, (wz_s, wz_r), (wy_s, wy_r), (wx_s, wx_r), (wc_s, wc_r)
    )
    steps[0]()

    chip = lax.div(me.tm, 2)

    def toward(k):
        there = wrap(chip + k, WAYS // 2)
        return there, 2 * there + me.core

    def coming(part, k):
        (there, target), rows = toward(k), pl.ds(*CUTS[part])
        return remote(
            parcels.at[there, pl.ds(0, 2), rows], landed.at[pl.ds(2 * chip, 2), rows],
            (i_s, i_r), part, (me.clip, target),
        )

    def going(part, k):
        device, rows = me.peer(k), pl.ds(32 * part, 32)
        return remote(
            parcels_out.at[device[1], rows], landed_out.at[me.tm, rows], (o_s, o_r), part, device
        )

    def arrive(part, sems):
        settle(landed.at[pl.ds(0, WAYS - 2), pl.ds(*CUTS[part])], sems.at[part])

    def returned(part, sems):
        settle(landed_out.at[pl.ds(0, WAYS - 1), pl.ds(32 * part, 32)], sems.at[part])

    def pack(target, place):
        for source in range(2):
            pack_in(target, video.at[source], cotangent.at[source], place(source))

    def one(k):
        there, target = toward(k)
        pack(target, lambda source: parcels.at[there, source])
        coming(0, k).start()

    def two(i, carry):
        one(8 - i)
        one(8 + i)
        return carry

    for copy in swaps:
        copy.wait_recv()
    one(8)
    lax.fori_loop(1, 2, two, 0)
    steps[1]()
    lax.fori_loop(2, 4, two, 0)
    steps[2]()
    lax.fori_loop(4, 6, two, 0)
    steps[3]()
    lax.fori_loop(6, 8, two, 0)
    pack(me.tm, lambda source: landed.at[2 * chip + source])
    steps[4]()

    def late(i, carry):
        coming(1, 8 - i).start()
        coming(1, 8 + i).start()
        return carry

    coming(1, 8).start()
    lax.fori_loop(1, 8, late, 0)
    steps[5]()
    unpack_weights(weights, w, gain)

    total = Sums(
        me, sums, core_in, held, mid, x_in, z_in, y_in, y_out, totals,
        dict(
            c=(sc_s, sc_r), m=(sm_s, sm_r), x=(sx_s, sx_r), z=(sz_s, sz_r), y=(sy_s, sy_r),
            f=(sf_s, sf_r),
        ),
    )
    tall = (
        x, cot, s1, s2, hidden, inverse, normed, packed, attended, grad_att, grad_packed,
        grad_hidden, a1, a2, gv,
    )
    for part, (first, spots) in enumerate(PARTS):
        rows = pl.ds(first * FRAMES, spots * FRAMES)
        (
            px, pcot, ps1, ps2, phidden, pinverse, pnormed, ppacked, pattended, pgrad_att,
            pgrad_packed, pgrad_hidden, pa1, pa2, pgv,
        ) = (ref.at[rows] for ref in tall)
        blocks = BLOCKS[part]
        arrive(part, i_r)
        unpack_in(part, landed, px, pcot)
        forward(blocks, w, gain, px, ps1, ps2, phidden, pinverse, pnormed, ppacked)
        attention(blocks, w, pcot, ppacked, pattended, pgrad_att, pgrad_packed)

        def add(n, product):
            if part == 0:
                acc[n] = product
            else:
                sums[n // 4, n % 4] = (acc[n] + product).astype(BF16)

        def early_sums():
            add(0, mm_tn(pattended[...], pcot[...]))
            product = mm_tn(pnormed[...], pgrad_packed[...])
            for i in range(3):
                add(1 + i, product[:, i * C : (i + 1) * C])

        def late_sums():
            for tap, ref in enumerate((px, ps1, ps2)):
                add(4 + tap, mm_tn(ref[...], pgrad_hidden[...]))

        def send_back():
            pack_out(part, pgv, parcels_out)
            landed_out[me.tm, 32 * part : 32 * part + 32, :] = (
                parcels_out[me.tm, 32 * part : 32 * part + 32, :]
            )

        def norm_back():
            return normalize_back(w, gain, pcot, phidden, pinverse, pgrad_packed, pgrad_hidden)

        if part == 0:
            gain_acc[...] = norm_back()
            conv_back(blocks, w, pgrad_hidden, pa1, pa2, pgv)
            send_back()
            each_peer(lambda k: going(0, k).start())
            early_sums()
            late_sums()
        else:
            early_sums()
            total.core_send(0)
            gain_sum = gain_acc[...] + norm_back()
            row, col = iotas(C, C)
            sums[1, 3] = jnp.where(row == col, gain_sum, 0.0).astype(BF16)
            late_sums()
            total.core_send(1)
            total.core_add(0)
            conv_back(blocks, w, pgrad_hidden, pa1, pa2, pgv)
            total.core_add(1)
            total.relay(0)
    total.relay(1)
    total.own_x(0)
    total.own_x(1)
    send_back()
    total.own_z()
    each_peer(lambda k: going(1, k).start())
    total.own_y()
    for part in range(2):
        returned(part, o_r)
    unpack_out(landed_out, grad_video)
    total.drain()
    drain()
    for copy in swaps:
        copy.wait_send()
    for part in range(2):
        arrive(part, i_s)
        returned(part, o_s)


def call(kernel, outs, scratch, places, out_places, mib, collective=None):
    extra = {} if collective is None else dict(collective_id=collective, has_side_effects=True)
    return pl.pallas_call(
        kernel,
        out_shape=[jax.ShapeDtypeStruct(*o) for o in outs],
        in_specs=[pl.BlockSpec(memory_space=place) for place in places],
        out_specs=[pl.BlockSpec(memory_space=place) for place in out_places],
        scratch_shapes=scratch,
        compiler_params=pltpu.CompilerParams(vmem_limit_bytes=mib * 1024 * 1024, **extra),
    )


def main(*args):
    def held(*shape, kind=BF16):
        return pltpu.VMEM(shape, kind)

    tall = held(ROWS, C)
    scratch = [
        held(2, 1, 2, 288, C), held(2, 1, 2, 288, C), held(3, SHARE, C), held(SHARE, 3 * C), held(SHARE, C),
        held(WAYS // 2, 2, PIECE, 128), held(2, QUAD, C), held(WAYS, PIECE, 128), held(2, 4, 8, QUAD, C),
        held(C, WIDE), held(1, C, kind=F32), held(WAYS, BACK, 128), held(WAYS, BACK, 128), held(MATS, C, C, kind=F32),
        held(1, C, kind=F32),
        tall, tall, tall, tall, tall, held(ROWS, 1, kind=F32), tall, held(ROWS, 3 * C), tall, tall,
        held(ROWS, 3 * C), tall, tall, tall, tall,
        held(2, 4, C, C), held(2, 2, C, C), held(2, 2, C, C), held(2, HALF, C), held(2, C, C),
        held(8, QUAD, C), held(8, QUAD, C), held(QUAD, C),
    ]
    counts = [5] + [2] * 6 + [8, 8, 2, 2, 4, 4, 8, 8] + [4] * 4 + [8] * 2 + [1] * 6
    scratch += [pltpu.SemaphoreType.DMA((n,)) for n in counts]
    outs = [(args[0].shape, BF16), ((8, QUAD, C), BF16)]
    places = [pl.ANY] * 5 + [pltpu.VMEM]
    return call(main_kernel, outs, scratch, places, [pltpu.VMEM] * 2, 56, 1)(*args)


def finish_kernel(
    factor, grad_in, totals_in, grad_video, conv, qkv, out_w, gain, grad, totals, sems
):
    come = pltpu.make_async_copy(grad_in, grad, sems.at[0])
    come.start()
    read = pltpu.make_async_copy(totals_in, totals, sems.at[1])
    read.start()
    come.wait()
    go = pltpu.make_async_copy(grad, grad_video, sems.at[2])
    go.start()
    read.wait()
    tm = lax.axis_index("tm")
    pick = picks(lambda r: r + lax.rem(tm, 4) * SHARE, 16, QUAD)
    got = [mm(pick, totals[m]) for m in range(8)]
    for i in range(3):
        conv[i] = got[4 + i][0:SHARE] * factor
        qkv[:, i * C : (i + 1) * C] = got[1 + i][0:SHARE] * factor
    out_w[...] = got[0][0:SHARE] * factor
    row, col = iotas(C, SHARE)
    line = mm(got[7].astype(BF16), jnp.where(row == tm * SHARE + col, 1.0, 0.0).astype(BF16))
    row, col = iotas(16, SHARE)
    gain[...] = jnp.sum(jnp.where(row == col, line, 0.0), axis=0, keepdims=True) * factor
    go.wait()


def body(video, conv_w, qkv_w, out_w, gain, cotangent):
    grad_video, totals = main(video, cotangent, conv_w, qkv_w, out_w, gain.reshape(1, SHARE))
    factor = 1.0 / math.sqrt(
        lax.axis_size("clip") * lax.axis_size("tm") * video.shape[1] * video.shape[2]
    )
    outs = [
        (video.shape, BF16), (conv_w.shape, F32), (qkv_w.shape, F32), (out_w.shape, F32),
        ((1, SHARE), F32),
    ]
    got = call(
        functools.partial(finish_kernel, factor), outs,
        [
            pltpu.VMEM(video.shape, BF16), pltpu.VMEM((8, QUAD, C), BF16),
            pltpu.SemaphoreType.DMA((3,)),
        ],
        [pl.ANY] * 2, [pl.ANY] + [pltpu.VMEM] * 4, 56,
    )(grad_video, totals)
    return (*got[:4], got[4].reshape(SHARE))


def solution(mesh):
    in_specs = (
        P("clip", "tm", None, None),
        P(None, "tm", None),
        P("tm", None),
        P("tm", None),
        P("tm"),
        P("clip", "tm", None, None),
    )
    out_specs = (
        P("clip", "tm", None, None),
        P(None, "tm", None),
        P("tm", None),
        P("tm", None),
        P("tm"),
    )
    return jax.shard_map(body, mesh=mesh, in_specs=in_specs, out_specs=out_specs, check_vma=False)
```
